32 devices in a mesh: dp: 8 (over z, core), shard: 4 (over y, x).
Axes of the slice: x: 2, y: 2, z: 4, core: 2. Of those that a mesh axis runs over, the one named last changes fastest.
Arguments:
- grads: bfloat16 [8, 256, 7168], P('dp', 'shard'), may hold values from -6 to 6
- errors: float32 [8, 256, 7168], P('dp', 'shard'), may hold values from -4 to 4
- q_prev: float32 [7168, 32], P('shard'), may hold values from -6 to 6
Outputs:
- new_errors: float32 [8, 256, 7168], P('dp', 'shard')
- q_new: float32 [7168, 32], P('shard')
The draws below stay inside these ranges and needn't reach their ends.
All inputs are finite; a program needn't handle non-finite values.
Results may differ from the reference program's by a relative error of at most 0.0003.
Values sent between devices are 32-bit elements; how exact they have to be, the bound alone decides.
A program may use at most 64 MiB of HBM per device.

```python
import jax
import jax.numpy as jnp
from jax import lax

D = 7168
RANK = 32
ROWS = 256
N_DP = 8


def block_levels(rng, extent, pieces, smallest, largest):
    loudness, own = 1.0, jax.random.fold_in(rng, 6)
    for axis_at, parts in pieces:
        heights = jnp.exp(jax.random.uniform(jax.random.fold_in(own, axis_at), (parts,), jnp.float32, smallest / len(pieces), largest / len(pieces)))
        loudness = loudness * jnp.repeat(heights, extent[axis_at] // parts).reshape([-1 if axis == axis_at else 1 for axis in range(len(extent))])
    return loudness


def gaussian(rng, shape, width, reach, split=(), dtype=jnp.bfloat16):
    values = jax.random.normal(rng, shape, jnp.float32) * width
    if len(split) > 0:
        values = block_levels(rng, shape, split, -0.22, 0.18) * values
    return jnp.clip(values, min=-reach, max=reach).astype(dtype)


def setup_inputs(seed: int = 0) -> dict:
    streams_of = jax.random.split(jax.random.key(seed), 4)
    grads = gaussian(streams_of[0], (N_DP, ROWS, D), 1.0, 6.0, ((0, 8), (1, 4)))
    errors = gaussian(streams_of[1], (N_DP, ROWS, D), 0.5, 4.0, ((0, 8), (1, 4)), jnp.float32)
    q_prev = gaussian(streams_of[2], (D, RANK), 1.0, 6.0, ((0, 4),), jnp.float32)
    return {"grads": grads, "errors": errors, "q_prev": q_prev}


def reference(grads, errors, q_prev):
    high = lax.Precision.HIGHEST
    merged = grads.astype(jnp.float32) + errors
    left = jnp.einsum('krd,dc->rc', merged, q_prev, precision=high) / N_DP
    gram = jnp.dot(left.T, left, precision=high)
    lower = jnp.linalg.cholesky(gram)
    p_hat = jax.scipy.linalg.solve_triangular(lower, left.T, lower=True).T
    right = jnp.einsum('krd,rc->dc', merged, p_hat, precision=high) / N_DP
    approx = jnp.dot(p_hat, right.T, precision=high)
    return (merged - approx[None], right)
```

```python
import functools

import jax
import jax.numpy as jnp
from jax import lax
from jax.experimental import pallas as pl
from jax.experimental.pallas import tpu as pltpu
from jax.sharding import PartitionSpec as P

MESH = pl.DeviceIdType.MESH
HIGH = lax.Precision.HIGHEST
F32 = jnp.float32
BF16 = jnp.bfloat16
NT = (((1,), (1,)), ((), ()))
NN = (((1,), (0,)), ((), ()))


def dot(a, b, dims=NN, precision=None):
    return lax.dot_general(a, b, dims, precision=precision, preferred_element_type=F32)


def halves(x):
    hi = x.astype(BF16)
    return hi, (x - hi.astype(F32)).astype(BF16)


def inverse_factor(gram):
    n = gram.shape[0]
    rows = lax.broadcasted_iota(jnp.int32, (n, 128), 0)
    lanes = lax.broadcasted_iota(jnp.int32, (n, 128), 1)
    work = jnp.where(lanes == rows + n, 1.0, gram)
    for j in range(n):
        pivot = work[j : j + 1, :]
        column = work[:, j : j + 1]
        scale = column / pivot[:, j : j + 1]
        work = jnp.where(rows > j, work - scale * pivot, work)
    diag = jnp.sum(jnp.where(lanes == rows, work, 0.0), axis=1, keepdims=True)
    work = work * lax.rsqrt(diag)
    return work[:, n : 2 * n]


def kernel(
    dims, g_hbm, e_hbm, q_ref, out_hbm, qnew_ref,
    g_v, e_v, m2, mf, q_all, pbuf, gbuf, w_a, w_b, w_c, w_r, r_buf, z_r, z_full, y_all, out_v,
    in_sem, q_s, q_r, qf_s, qf_r, p_s, p_r, g_s, g_r, c_s, c_r, w_s, w_rs, zr_s, zr_r, za_s, za_r,
    y_s, y_r, yc_s, yc_r, out_sem,
):
    n_dp, n_sh, nz, zrows, split_z, aligned, width = dims
    rank = q_ref.shape[0]
    pieces = 2 * n_sh
    d = lax.axis_index("dp")
    s = lax.axis_index("shard")
    z = d // 2
    c = d % 2
    oc = 1 - c
    sib = d + 1 - 2 * c

    load_g = pltpu.make_async_copy(g_hbm.at[0], g_v, in_sem.at[0])
    load_e = pltpu.make_async_copy(e_hbm.at[0], e_v, in_sem.at[1])
    load_g.start()
    load_e.start()

    def at_dp(i):
        return lax.rem(d + i, n_dp)

    def at_sh(i):
        return lax.rem(s + i, n_sh)

    def at_z(i):
        return lax.rem(z + i, nz)

    barrier = pltpu.get_barrier_semaphore()
    for i in range(1, n_dp):
        pl.semaphore_signal(barrier, inc=1, device_id=(at_dp(i), s), device_id_type=MESH)
    for i in range(1, n_sh):
        pl.semaphore_signal(barrier, inc=1, device_id=(d, at_sh(i)), device_id_type=MESH)
    for h in range(2):
        q_all[2 * s + h] = q_ref[:, h * width : (h + 1) * width]
    pl.semaphore_wait(barrier, n_dp - 1 + n_sh - 1)

    def remote(src, dst, send, recv, target):
        return pltpu.make_async_remote_copy(
            src_ref=src, dst_ref=dst, send_sem=send, recv_sem=recv, device_id=target, device_id_type=MESH
        )

    sends = []

    def send(src, dst, send_sem, recv_sem, target):
        copy = remote(src, dst, send_sem, recv_sem, target)
        copy.start()
        sends.append(copy)

    def arrived(dst, send_sem, recv_sem):
        remote(dst, dst, send_sem, recv_sem, (sib, s)).wait_recv()

    mine = 2 * s + c
    for i in range(1, n_sh):
        send(q_all.at[mine], q_all.at[mine], q_s.at[i], q_r.at[s], (d, at_sh(i)))

    load_g.wait()
    load_e.wait()
    for k in range(pieces):
        span = slice(k * width, (k + 1) * width)
        m = g_v[:, span].astype(F32) + e_v[:, span]
        hi, lo = halves(m)
        mf[k] = m
        m2[k, : m.shape[0]] = hi
        m2[k, m.shape[0] :] = lo

    def left_term(k):
        hi, lo = halves(q_all[k])
        return dot(jnp.concatenate([hi, lo], axis=0), m2[k], NT)

    acc = left_term(2 * s) + left_term(2 * s + 1)
    for i in range(1, n_sh):
        o = at_sh(i)
        k = 2 * o + c
        arrived(q_all.at[k], q_s.at[i], q_r.at[o])
        send(q_all.at[k], q_all.at[k], qf_s.at[i], qf_r.at[o], (sib, s))
        acc = acc + left_term(k)
    for i in range(1, n_sh):
        o = at_sh(i)
        k = 2 * o + oc
        arrived(q_all.at[k], qf_s.at[i], qf_r.at[o])
        acc = acc + left_term(k)
    acc = acc[:rank] + acc[rank:]
    n_rows = mf.shape[1]
    part = acc[:, :n_rows] + acc[:, n_rows:]
    half = rank // 2

    pbuf[d] = jnp.concatenate([part[:half], part[half:]], axis=1)
    for i in range(1, n_dp):
        send(pbuf.at[d], pbuf.at[d], p_s.at[i], p_r.at[d], (at_dp(i), s))
    for i in range(1, n_dp):
        o = at_dp(i)
        arrived(pbuf.at[o], p_s.at[i], p_r.at[o])
    total = pbuf[0]
    for k in range(1, n_dp):
        total = total + pbuf[k]
    total = total * (1.0 / n_dp)
    pt = jnp.concatenate([total[:, :n_rows], total[:, n_rows:]], axis=0)

    padded = jnp.concatenate([pt, jnp.zeros((128 - rank, n_rows), F32)], axis=0)
    gbuf[s] = dot(pt, padded, NT, HIGH)
    for i in range(1, n_sh):
        send(gbuf.at[s], gbuf.at[s], g_s.at[i], g_r.at[s], (d, at_sh(i)))

    twice = jnp.concatenate([pt, pt], axis=1) * (1.0 / n_dp)
    p_hi, p_lo = halves(twice)
    p2 = jnp.concatenate([p_hi, p_lo], axis=0)

    def w_term(k):
        t = dot(p2, m2[k])
        return t[:rank] + t[rank:]

    order = list(range(1, n_sh)) + [0]
    for i in order:
        o = at_sh(i)
        w_a[o] = w_term(2 * o + oc)
        send(w_a.at[o], w_b.at[o], c_s.at[i], c_r.at[o], (sib, s))
    for i in order:
        o = at_sh(i)
        own = w_term(2 * o + c)
        arrived(w_b.at[o], c_s.at[i], c_r.at[o])
        if i == 0:
            w_r[s] = own + w_b[s]
        else:
            w_c[o] = own + w_b[o]
            send(w_c.at[o], w_r.at[s], w_s.at[i], w_rs.at[s], (d, at_sh(i)))

    for i in range(1, n_sh):
        o = at_sh(i)
        arrived(gbuf.at[o], g_s.at[i], g_r.at[o])
    gram = gbuf[0]
    for k in range(1, n_sh):
        gram = gram + gbuf[k]
    linv = inverse_factor(gram)
    p_hat_t = dot(linv, pt, NN, HIGH)
    three = jnp.concatenate([p_hat_t, p_hat_t, p_hat_t], axis=0)
    rounded = three.astype(BF16).astype(F32)
    row = lax.broadcasted_iota(jnp.int32, three.shape, 0)
    ph3 = jnp.where(row < 2 * rank, rounded, three - rounded).T.astype(BF16)

    for i in range(1, n_sh):
        o = at_sh(i)
        arrived(w_r.at[o], w_s.at[i], w_rs.at[o])
    r = w_r[0]
    for k in range(1, n_sh):
        r = r + w_r[k]

    if split_z:
        for k in range(nz):
            r_buf[k] = r[k * zrows : (k + 1) * zrows]
        z_r[z] = r_buf[z]
        for i in range(1, nz):
            o = at_z(i)
            send(r_buf.at[o], z_r.at[z], zr_s.at[i], zr_r.at[z], (2 * o + c, s))
    else:
        z_r[z] = r
        for i in range(1, nz):
            o = at_z(i)
            send(z_r.at[z], z_r.at[z], zr_s.at[i], zr_r.at[z], (2 * o + c, s))
    for i in range(1, nz):
        o = at_z(i)
        arrived(z_r.at[o], zr_s.at[i], zr_r.at[o])
    r = z_r[0]
    for k in range(1, nz):
        r = r + z_r[k]
    if split_z:
        z_full[z] = r
        for i in range(1, nz):
            o = at_z(i)
            send(z_full.at[z], z_full.at[z], za_s.at[i], za_r.at[z], (2 * o + c, s))
        for i in range(1, nz):
            o = at_z(i)
            arrived(z_full.at[o], za_s.at[i], za_r.at[o])
        r = jnp.concatenate([z_full[k] for k in range(nz)], axis=0)

    y_all[mine] = dot(linv, r, NN, HIGH)
    send(y_all.at[mine], y_all.at[mine], yc_s.at[0], yc_r.at[s], (sib, s))
    for i in range(1, n_sh):
        send(y_all.at[mine], y_all.at[mine], y_s.at[i], y_r.at[s], (d, at_sh(i)))

    stores = []

    def finish(k, slot):
        hi, lo = halves(y_all[k])
        mf[k] = mf[k] - dot(ph3, jnp.concatenate([hi, lo, hi], axis=0))
        if aligned:
            start = pl.multiple_of(k * width, 128)
            copy = pltpu.make_async_copy(mf.at[k], out_hbm.at[0, :, pl.ds(start, width)], out_sem.at[slot])
            copy.start()
            stores.append(copy)

    finish(mine, 0)
    arrived(y_all.at[2 * s + oc], yc_s.at[0], yc_r.at[s])
    finish(2 * s + oc, 1)
    for h in range(2):
        qnew_ref[:, h * width : (h + 1) * width] = y_all[2 * s + h]
    for i in range(1, n_sh):
        o = at_sh(i)
        k = 2 * o + c
        arrived(y_all.at[k], y_s.at[i], y_r.at[o])
        send(y_all.at[k], y_all.at[k], yc_s.at[i], yc_r.at[o], (sib, s))
        finish(k, 2 * i)
    for i in range(1, n_sh):
        o = at_sh(i)
        k = 2 * o + oc
        arrived(y_all.at[k], yc_s.at[i], yc_r.at[o])
        finish(k, 2 * i + 1)
    if not aligned:
        for k in range(pieces):
            out_v[:, k * width : (k + 1) * width] = mf[k]
        copy = pltpu.make_async_copy(out_v, out_hbm.at[0], out_sem.at[0])
        copy.start()
        stores.append(copy)
    for copy in sends:
        copy.wait_send()
    for copy in stores:
        copy.wait()


def per_device(n_dp, n_sh, grads, errors, q_prev):
    _, n_rows, full = grads.shape
    share, rank = q_prev.shape
    width = share // 2
    nz = n_dp // 2
    split_z = rank % (8 * nz) == 0
    zrows = rank // nz if split_z else rank
    aligned = width % 128 == 0
    pieces = 2 * n_sh
    dims = (n_dp, n_sh, nz, zrows, split_z, aligned, width)
    vm = pltpu.VMEM
    dma = pltpu.SemaphoreType.DMA
    small = (8, 128)
    scratch = [
        vm((n_rows, full), BF16),
        vm((n_rows, full), F32),
        vm((pieces, 2 * n_rows, width), BF16),
        vm((pieces, n_rows, width), F32),
        vm((pieces, rank, width), F32),
        vm((n_dp, rank // 2, 2 * n_rows), F32),
        vm((n_sh, rank, 128), F32),
        vm((n_sh, rank, width), F32),
        vm((n_sh, rank, width), F32),
        vm((n_sh, rank, width), F32),
        vm((n_sh, rank, width), F32),
        vm((nz, zrows, width) if split_z else small, F32),
        vm((nz, zrows, width), F32),
        vm((nz, zrows, width) if split_z else small, F32),
        vm((pieces, rank, width), F32),
        vm(small if aligned else (n_rows, full), F32),
        dma((2,)),
    ]
    for count in (n_sh, n_sh, n_dp, n_sh, n_sh, n_sh, nz, nz, n_sh, n_sh):
        scratch += [dma((count,)), dma((count,))]
    scratch.append(dma((pieces,)))
    out, q_new = pl.pallas_call(
        functools.partial(kernel, dims),
        out_shape=(
            jax.ShapeDtypeStruct((1, n_rows, full), F32),
            jax.ShapeDtypeStruct((rank, share), F32),
        ),
        in_specs=[
            pl.BlockSpec(memory_space=pl.ANY),
            pl.BlockSpec(memory_space=pl.ANY),
            pl.BlockSpec(memory_space=pltpu.VMEM),
        ],
        out_specs=(pl.BlockSpec(memory_space=pl.ANY), pl.BlockSpec(memory_space=pltpu.VMEM)),
        scratch_shapes=scratch,
        compiler_params=pltpu.CompilerParams(
            collective_id=0, has_side_effects=True, vmem_limit_bytes=48 * 1024 * 1024
        ),
        cost_estimate=pl.CostEstimate(
            flops=18 * n_rows * full * rank, bytes_accessed=10 * n_rows * full, transcendentals=0
        ),
    )(grads, errors, q_prev.T)
    return out, q_new.T


def solution(mesh):
    in_specs = (P("dp", "shard", None), P("dp", "shard", None), P("shard", None))
    out_specs = (P("dp", "shard", None), P("shard", None))
    return jax.shard_map(
        functools.partial(per_device, mesh.shape["dp"], mesh.shape["shard"]),
        mesh=mesh, in_specs=in_specs, out_specs=out_specs, check_vma=False,
    )
```

```python
import functools

import jax
import jax.numpy as jnp
from jax import lax
from jax.experimental import pallas as pl
from jax.experimental.pallas import tpu as pltpu
from jax.sharding import PartitionSpec as P

MESH = pl.DeviceIdType.MESH
HIGH = lax.Precision.HIGHEST
F32 = jnp.float32
BF16 = jnp.bfloat16
NT = (((1,), (1,)), ((), ()))
NN = (((1,), (0,)), ((), ()))


def dot(a, b, dims=NN, precision=None):
    return lax.dot_general(a, b, dims, precision=precision, preferred_element_type=F32)


def halves(x):
    hi = x.astype(BF16)
    return hi, (x - hi.astype(F32)).astype(BF16)


def inverse_factor(gram):
    n = gram.shape[0]
    rows = lax.broadcasted_iota(jnp.int32, (n, 128), 0)
    lanes = lax.broadcasted_iota(jnp.int32, (n, 128), 1)
    work = jnp.where(lanes == rows + n, 1.0, gram)
    block = 8
    for first in range(0, n, block):
        columns = [jnp.broadcast_to(work[:, first + t : first + t + 1], (n, 128)) for t in range(block)]
        for t in range(block):
            j = first + t
            scale = jnp.where(rows > j, columns[t] * (1.0 / columns[t][j : j + 1]), 0.0)
            for u in range(t + 1, block):
                columns[u] = columns[u] - scale * columns[u][j : j + 1]
            work = work - scale * work[j : j + 1]
    diag = jnp.sum(jnp.where(lanes == rows, work, 0.0), axis=1, keepdims=True)
    work = work * lax.rsqrt(diag)
    return work[:, n : 2 * n]


def kernel(
    dims, g_hbm, e_hbm, q_hbm, out_hbm, qnew_ref,
    g_v, e_v, q_v, m2, mf, q_all, pbuf, gbuf, w_a, w_b, w_c, w_r, r_buf, z_r, z_full, y_all, out_v,
    in_sem, q_s, q_r, qf_s, qf_r, p_s, p_r, g_s, g_r, c_s, c_r, w_s, w_rs, zr_s, zr_r, za_s, za_r,
    y_s, y_r, yc_s, yc_r, out_sem,
):
    n_dp, n_sh, nz, zrows, split_z, aligned, width = dims
    rank = q_hbm.shape[0]
    pieces = 2 * n_sh
    d = lax.axis_index("dp")
    s = lax.axis_index("shard")
    z = d // 2
    c = d % 2
    oc = 1 - c
    sib = d + 1 - 2 * c

    load_g = pltpu.make_async_copy(g_hbm.at[0], g_v, in_sem.at[0])
    load_e = pltpu.make_async_copy(e_hbm.at[0], e_v, in_sem.at[1])
    q_loads = []
    if aligned:
        for h in range(2):
            half_copy = pltpu.make_async_copy(
                q_hbm.at[:, h * width : (h + 1) * width], q_all.at[2 * s + h], in_sem.at[2 + h]
            )
            half_copy.start()
            q_loads.append(half_copy)
    else:
        whole_copy = pltpu.make_async_copy(q_hbm, q_v, in_sem.at[2])
        whole_copy.start()
        q_loads.append(whole_copy)
    load_g.start()
    load_e.start()

    def at_dp(i):
        return lax.rem(d + i, n_dp)

    def at_sh(i):
        return lax.rem(s + i, n_sh)

    def at_z(i):
        return lax.rem(z + i, nz)

    barrier = pltpu.get_barrier_semaphore()
    for i in range(1, n_dp):
        pl.semaphore_signal(barrier, inc=1, device_id=(at_dp(i), s), device_id_type=MESH)
    for i in range(1, n_sh):
        pl.semaphore_signal(barrier, inc=1, device_id=(d, at_sh(i)), device_id_type=MESH)
    for q_load in q_loads:
        q_load.wait()
    if not aligned:
        for h in range(2):
            q_all[2 * s + h] = q_v[:, h * width : (h + 1) * width]
    pl.semaphore_wait(barrier, n_dp - 1 + n_sh - 1)

    def remote(src, dst, send, recv, target):
        return pltpu.make_async_remote_copy(
            src_ref=src, dst_ref=dst, send_sem=send, recv_sem=recv, device_id=target, device_id_type=MESH
        )

    sends = []

    def send(src, dst, send_sem, recv_sem, target):
        copy = remote(src, dst, send_sem, recv_sem, target)
        copy.start()
        sends.append(copy)

    def arrived(dst, send_sem, recv_sem):
        remote(dst, dst, send_sem, recv_sem, (sib, s)).wait_recv()

    mine = 2 * s + c
    for i in range(1, n_sh):
        send(q_all.at[mine], q_all.at[mine], q_s.at[i], q_r.at[s], (d, at_sh(i)))

    load_g.wait()
    load_e.wait()
    for k in range(pieces):
        span = slice(k * width, (k + 1) * width)
        m = g_v[:, span].astype(F32) + e_v[:, span]
        hi, lo = halves(m)
        mf[k] = m
        m2[k, : m.shape[0]] = hi
        m2[k, m.shape[0] :] = lo

    def left_term(k):
        hi, lo = halves(q_all[k])
        return dot(jnp.concatenate([hi, lo], axis=0), m2[k], NT)

    acc = left_term(2 * s) + left_term(2 * s + 1)
    for i in range(1, n_sh):
        o = at_sh(i)
        k = 2 * o + c
        arrived(q_all.at[k], q_s.at[i], q_r.at[o])
        send(q_all.at[k], q_all.at[k], qf_s.at[i], qf_r.at[o], (sib, s))
        acc = acc + left_term(k)
    for i in range(1, n_sh):
        o = at_sh(i)
        k = 2 * o + oc
        arrived(q_all.at[k], qf_s.at[i], qf_r.at[o])
        acc = acc + left_term(k)
    acc = acc[:rank] + acc[rank:]
    n_rows = mf.shape[1]
    part = acc[:, :n_rows] + acc[:, n_rows:]
    half = rank // 2

    pbuf[d] = jnp.concatenate([part[:half], part[half:]], axis=1)
    for i in range(1, n_dp):
        send(pbuf.at[d], pbuf.at[d], p_s.at[i], p_r.at[d], (at_dp(i), s))
    for i in range(1, n_dp):
        o = at_dp(i)
        arrived(pbuf.at[o], p_s.at[i], p_r.at[o])
    total = pbuf[0]
    for k in range(1, n_dp):
        total = total + pbuf[k]
    total = total * (1.0 / n_dp)
    pt = jnp.concatenate([total[:, :n_rows], total[:, n_rows:]], axis=0)

    padded = jnp.concatenate([pt, jnp.zeros((128 - rank, n_rows), F32)], axis=0)
    gbuf[s] = dot(pt, padded, NT, HIGH)
    for i in range(1, n_sh):
        send(gbuf.at[s], gbuf.at[s], g_s.at[i], g_r.at[s], (d, at_sh(i)))

    twice = jnp.concatenate([pt, pt], axis=1) * (1.0 / n_dp)
    p_hi, p_lo = halves(twice)
    p2 = jnp.concatenate([p_hi, p_lo], axis=0)

    def w_term(k):
        t = dot(p2, m2[k])
        return t[:rank] + t[rank:]

    order = list(range(1, n_sh)) + [0]
    for i in order:
        o = at_sh(i)
        w_a[o] = w_term(2 * o + oc)
        send(w_a.at[o], w_b.at[o], c_s.at[i], c_r.at[o], (sib, s))
    for i in order:
        o = at_sh(i)
        own = w_term(2 * o + c)
        arrived(w_b.at[o], c_s.at[i], c_r.at[o])
        if i == 0:
            w_r[s] = own + w_b[s]
        else:
            w_c[o] = own + w_b[o]
            send(w_c.at[o], w_r.at[s], w_s.at[i], w_rs.at[s], (d, at_sh(i)))

    for i in range(1, n_sh):
        o = at_sh(i)
        arrived(gbuf.at[o], g_s.at[i], g_r.at[o])
    gram = gbuf[0]
    for k in range(1, n_sh):
        gram = gram + gbuf[k]
    linv = inverse_factor(gram)
    p_hat_t = dot(linv, pt, NN, HIGH)
    three = jnp.concatenate([p_hat_t, p_hat_t, p_hat_t], axis=0)
    rounded = three.astype(BF16).astype(F32)
    row = lax.broadcasted_iota(jnp.int32, three.shape, 0)
    ph3 = jnp.where(row < 2 * rank, rounded, three - rounded).T.astype(BF16)

    for i in range(1, n_sh):
        o = at_sh(i)
        arrived(w_r.at[o], w_s.at[i], w_rs.at[o])
    r = w_r[0]
    for k in range(1, n_sh):
        r = r + w_r[k]

    if split_z:
        for k in range(nz):
            r_buf[k] = r[k * zrows : (k + 1) * zrows]
        z_r[z] = r_buf[z]
        for i in range(1, nz):
            o = at_z(i)
            send(r_buf.at[o], z_r.at[z], zr_s.at[i], zr_r.at[z], (2 * o + c, s))
    else:
        z_r[z] = r
        for i in range(1, nz):
            o = at_z(i)
            send(z_r.at[z], z_r.at[z], zr_s.at[i], zr_r.at[z], (2 * o + c, s))
    for i in range(1, nz):
        o = at_z(i)
        arrived(z_r.at[o], zr_s.at[i], zr_r.at[o])
    r = z_r[0]
    for k in range(1, nz):
        r = r + z_r[k]
    if split_z:
        z_full[z] = r
        for i in range(1, nz):
            o = at_z(i)
            send(z_full.at[z], z_full.at[z], za_s.at[i], za_r.at[z], (2 * o + c, s))
        for i in range(1, nz):
            o = at_z(i)
            arrived(z_full.at[o], za_s.at[i], za_r.at[o])
        r = jnp.concatenate([z_full[k] for k in range(nz)], axis=0)

    y_all[mine] = dot(linv, r, NN, HIGH)
    send(y_all.at[mine], y_all.at[mine], yc_s.at[0], yc_r.at[s], (sib, s))
    for i in range(1, n_sh):
        send(y_all.at[mine], y_all.at[mine], y_s.at[i], y_r.at[s], (d, at_sh(i)))

    stores = []

    def finish(k, slot):
        hi, lo = halves(y_all[k])
        mf[k] = mf[k] - dot(ph3, jnp.concatenate([hi, lo, hi], axis=0))
        if aligned:
            start = pl.multiple_of(k * width, 128)
            copy = pltpu.make_async_copy(mf.at[k], out_hbm.at[0, :, pl.ds(start, width)], out_sem.at[slot])
            copy.start()
            stores.append(copy)

    finish(mine, 0)
    arrived(y_all.at[2 * s + oc], yc_s.at[0], yc_r.at[s])
    finish(2 * s + oc, 1)
    for h in range(2):
        qnew_ref[:, h * width : (h + 1) * width] = y_all[2 * s + h]
    for i in range(1, n_sh):
        o = at_sh(i)
        k = 2 * o + c
        arrived(y_all.at[k], y_s.at[i], y_r.at[o])
        send(y_all.at[k], y_all.at[k], yc_s.at[i], yc_r.at[o], (sib, s))
        finish(k, 2 * i)
    for i in range(1, n_sh):
        o = at_sh(i)
        k = 2 * o + oc
        arrived(y_all.at[k], yc_s.at[i], yc_r.at[o])
        finish(k, 2 * i + 1)
    if not aligned:
        for k in range(pieces):
            out_v[:, k * width : (k + 1) * width] = mf[k]
        copy = pltpu.make_async_copy(out_v, out_hbm.at[0], out_sem.at[0])
        copy.start()
        stores.append(copy)
    for copy in sends:
        copy.wait_send()
    for copy in stores:
        copy.wait()


def per_device(n_dp, n_sh, grads, errors, q_prev):
    _, n_rows, full = grads.shape
    share, rank = q_prev.shape
    width = share // 2
    nz = n_dp // 2
    split_z = rank % (8 * nz) == 0
    zrows = rank // nz if split_z else rank
    aligned = width % 128 == 0
    pieces = 2 * n_sh
    dims = (n_dp, n_sh, nz, zrows, split_z, aligned, width)
    vm = pltpu.VMEM
    dma = pltpu.SemaphoreType.DMA
    small = (8, 128)
    scratch = [
        vm((n_rows, full), BF16),
        vm((n_rows, full), F32),
        vm(small if aligned else (rank, share), F32),
        vm((pieces, 2 * n_rows, width), BF16),
        vm((pieces, n_rows, width), F32),
        vm((pieces, rank, width), F32),
        vm((n_dp, rank // 2, 2 * n_rows), F32),
        vm((n_sh, rank, 128), F32),
        vm((n_sh, rank, width), F32),
        vm((n_sh, rank, width), F32),
        vm((n_sh, rank, width), F32),
        vm((n_sh, rank, width), F32),
        vm((nz, zrows, width) if split_z else small, F32),
        vm((nz, zrows, width), F32),
        vm((nz, zrows, width) if split_z else small, F32),
        vm((pieces, rank, width), F32),
        vm(small if aligned else (n_rows, full), F32),
        dma((4,)),
    ]
    for count in (n_sh, n_sh, n_dp, n_sh, n_sh, n_sh, nz, nz, n_sh, n_sh):
        scratch += [dma((count,)), dma((count,))]
    scratch.append(dma((pieces,)))
    out, q_new = pl.pallas_call(
        functools.partial(kernel, dims),
        out_shape=(
            jax.ShapeDtypeStruct((1, n_rows, full), F32),
            jax.ShapeDtypeStruct((rank, share), F32),
        ),
        in_specs=[
            pl.BlockSpec(memory_space=pltpu.HBM),
            pl.BlockSpec(memory_space=pltpu.HBM),
            pl.BlockSpec(memory_space=pltpu.HBM),
        ],
        out_specs=(pl.BlockSpec(memory_space=pl.ANY), pl.BlockSpec(memory_space=pltpu.VMEM)),
        scratch_shapes=scratch,
        compiler_params=pltpu.CompilerParams(
            collective_id=0, has_side_effects=True, vmem_limit_bytes=63 * 1024 * 1024
        ),
        cost_estimate=pl.CostEstimate(
            flops=18 * n_rows * full * rank, bytes_accessed=10 * n_rows * full, transcendentals=0
        ),
    )(grads, errors, q_prev.T)
    return out, q_new.T


def solution(mesh):
    in_specs = (P("dp", "shard", None), P("dp", "shard", None), P("shard", None))
    out_specs = (P("dp", "shard", None), P("shard", None))
    return jax.shard_map(
        functools.partial(per_device, mesh.shape["dp"], mesh.shape["shard"]),
        mesh=mesh, in_specs=in_specs, out_specs=out_specs, check_vma=False,
    )
```

```python
import functools

import jax
import jax.numpy as jnp
from jax import lax
from jax.experimental import pallas as pl
from jax.experimental.pallas import tpu as pltpu
from jax.sharding import PartitionSpec as P

MESH = pl.DeviceIdType.MESH
HIGH = lax.Precision.HIGHEST
F32 = jnp.float32
BF16 = jnp.bfloat16
NT = (((1,), (1,)), ((), ()))
NN = (((1,), (0,)), ((), ()))
N_CHUNKS = 2
PLACE_PARTS = 4


def dot(a, b, dims=NN, precision=None):
    return lax.dot_general(a, b, dims, precision=precision, preferred_element_type=F32)


def halves(x):
    hi = x.astype(BF16)
    return hi, (x - hi.astype(F32)).astype(BF16)


def inverse_factor(gram):
    n = gram.shape[0]
    rows = lax.broadcasted_iota(jnp.int32, (n, 128), 0)
    lanes = lax.broadcasted_iota(jnp.int32, (n, 128), 1)
    work = jnp.where(lanes == rows + n, 1.0, gram)
    block = 8
    for first in range(0, n, block):
        columns = [jnp.broadcast_to(work[:, first + t : first + t + 1], (n, 128)) for t in range(block)]
        for t in range(block):
            j = first + t
            scale = jnp.where(rows > j, columns[t] * (1.0 / columns[t][j : j + 1]), 0.0)
            for u in range(t + 1, block):
                columns[u] = columns[u] - scale * columns[u][j : j + 1]
            work = work - scale * work[j : j + 1]
    diag = jnp.sum(jnp.where(lanes == rows, work, 0.0), axis=1, keepdims=True)
    work = work * lax.rsqrt(diag)
    return work[:, n : 2 * n]


def kernel(
    dims, chunks, g_hbm, e_hbm, q_hbm, out_hbm, qnew_hbm,
    g_v, e_v, q_v, m2, mf, q_all, pbuf, gbuf, w_a, w_b, w_c, w_r, r_buf, z_r, z_full, y_all, out_v, qn_v,
    in_sem, q_s, q_r, qf_s, qf_r, p_s, p_r, g_s, g_r, c_s, c_r, w_s, w_rs, zr_s, zr_r, za_s, za_r,
    y_s, y_r, yc_s, yc_r, out_sem, qn_sem,
):
    n_dp, n_sh, nz, zrows, split_z, aligned, width = dims
    spans = [pl.ds(lo, hi - lo) for lo, hi in chunks]
    n_ch = len(chunks)
    rank = q_hbm.shape[0]
    pieces = 2 * n_sh
    d = lax.axis_index("dp")
    s = lax.axis_index("shard")
    z = d // 2
    c = d % 2
    oc = 1 - c
    sib = d + 1 - 2 * c

    load_g = pltpu.make_async_copy(g_hbm.at[0], g_v, in_sem.at[0])
    load_e = pltpu.make_async_copy(e_hbm.at[0], e_v, in_sem.at[1])
    q_loads = []
    if aligned:
        for h in range(2):
            half_copy = pltpu.make_async_copy(
                q_hbm.at[:, h * width : (h + 1) * width], q_all.at[2 * s + h], in_sem.at[2 + h]
            )
            half_copy.start()
            q_loads.append(half_copy)
    else:
        whole_copy = pltpu.make_async_copy(q_hbm, q_v, in_sem.at[2])
        whole_copy.start()
        q_loads.append(whole_copy)
    load_g.start()
    load_e.start()

    def at_dp(i):
        return lax.rem(d + i, n_dp)

    def at_sh(i):
        return lax.rem(s + i, n_sh)

    def at_z(i):
        return lax.rem(z + i, nz)

    barrier = pltpu.get_barrier_semaphore()
    for i in range(1, n_dp):
        pl.semaphore_signal(barrier, inc=1, device_id=(at_dp(i), s), device_id_type=MESH)
    for i in range(1, n_sh):
        pl.semaphore_signal(barrier, inc=1, device_id=(d, at_sh(i)), device_id_type=MESH)
    for q_load in q_loads:
        q_load.wait()
    if not aligned:
        for h in range(2):
            q_all[2 * s + h] = q_v[:, h * width : (h + 1) * width]
    pl.semaphore_wait(barrier, n_dp - 1 + n_sh - 1)

    def remote(src, dst, send, recv, target):
        return pltpu.make_async_remote_copy(
            src_ref=src, dst_ref=dst, send_sem=send, recv_sem=recv, device_id=target, device_id_type=MESH
        )

    sends = []

    def send(src, dst, send_sem, recv_sem, target):
        copy = remote(src, dst, send_sem, recv_sem, target)
        copy.start()
        sends.append(copy)

    def arrived(dst, send_sem, recv_sem):
        remote(dst, dst, send_sem, recv_sem, (sib, s)).wait_recv()

    mine = 2 * s + c
    other = 2 * s + oc
    for ch, span in enumerate(spans):
        part = q_all.at[mine, :, span]
        for i in range(1, n_sh):
            send(part, part, q_s.at[ch, i], q_r.at[ch, s], (d, at_sh(i)))

    load_g.wait()
    load_e.wait()
    for k in range(pieces):
        cols = slice(k * width, (k + 1) * width)
        m = g_v[:, cols].astype(F32) + e_v[:, cols]
        hi, lo = halves(m)
        mf[k] = m
        m2[k, : m.shape[0]] = hi
        m2[k, m.shape[0] :] = lo

    def left_term(k, span):
        hi, lo = halves(q_all[k, :, span])
        return dot(jnp.concatenate([hi, lo], axis=0), m2[k, :, span], NT)

    acc = left_term(2 * s, pl.ds(0, width)) + left_term(2 * s + 1, pl.ds(0, width))
    for ch, span in enumerate(spans):
        for i in range(1, n_sh):
            o = at_sh(i)
            part = q_all.at[2 * o + c, :, span]
            arrived(part, q_s.at[ch, i], q_r.at[ch, o])
            send(part, part, qf_s.at[ch, i], qf_r.at[ch, o], (sib, s))
        for i in range(1, n_sh):
            acc = acc + left_term(2 * at_sh(i) + c, span)
        for i in range(1, n_sh):
            o = at_sh(i)
            arrived(q_all.at[2 * o + oc, :, span], qf_s.at[ch, i], qf_r.at[ch, o])
            acc = acc + left_term(2 * o + oc, span)
    acc = acc[:rank] + acc[rank:]
    n_rows = mf.shape[1]
    part = acc[:, :n_rows] + acc[:, n_rows:]
    half = rank // 2

    pbuf[d] = jnp.concatenate([part[:half], part[half:]], axis=1)
    for i in range(1, n_dp):
        send(pbuf.at[d], pbuf.at[d], p_s.at[i], p_r.at[d], (at_dp(i), s))
    for i in range(1, n_dp):
        o = at_dp(i)
        arrived(pbuf.at[o], p_s.at[i], p_r.at[o])
    total = pbuf[0]
    for k in range(1, n_dp):
        total = total + pbuf[k]
    total = total * (1.0 / n_dp)
    pt = jnp.concatenate([total[:, :n_rows], total[:, n_rows:]], axis=0)

    twice = jnp.concatenate([pt, pt], axis=1) * (1.0 / n_dp)
    p_hi, p_lo = halves(twice)
    p2 = jnp.concatenate([p_hi, p_lo], axis=0)

    def w_term(k, span):
        t = dot(p2, m2[k, :, span])
        return t[:rank] + t[rank:]

    order = list(range(1, n_sh)) + [0]
    for ch, span in enumerate(spans):
        for i in order:
            o = at_sh(i)
            w_a[o, :, span] = w_term(2 * o + oc, span)
            send(w_a.at[o, :, span], w_b.at[o, :, span], c_s.at[ch, i], c_r.at[ch, o], (sib, s))
        if ch == 0:
            padded = jnp.concatenate([pt, jnp.zeros((128 - rank, n_rows), F32)], axis=0)
            gbuf[s] = dot(pt, padded, NT, HIGH)
            for i in range(1, n_sh):
                send(gbuf.at[s], gbuf.at[s], g_s.at[i], g_r.at[s], (d, at_sh(i)))
        for i in order:
            o = at_sh(i)
            own = w_term(2 * o + c, span)
            arrived(w_b.at[o, :, span], c_s.at[ch, i], c_r.at[ch, o])
            if i == 0:
                w_r[s, :, span] = own + w_b[s, :, span]
            else:
                w_c[o, :, span] = own + w_b[o, :, span]
                send(
                    w_c.at[o, :, span], w_r.at[s, :, span], w_s.at[ch, i], w_rs.at[ch, s], (d, at_sh(i))
                )

    for i in range(1, n_sh):
        o = at_sh(i)
        arrived(gbuf.at[o], g_s.at[i], g_r.at[o])
    gram = gbuf[0]
    for k in range(1, n_sh):
        gram = gram + gbuf[k]
    linv = inverse_factor(gram)
    p_hat_t = dot(linv, pt, NN, HIGH)
    three = jnp.concatenate([p_hat_t, p_hat_t, p_hat_t], axis=0)
    rounded = three.astype(BF16).astype(F32)
    row = lax.broadcasted_iota(jnp.int32, three.shape, 0)
    ph3 = jnp.where(row < 2 * rank, rounded, three - rounded).T.astype(BF16)

    def over_shards(ch, span):
        for i in range(1, n_sh):
            o = at_sh(i)
            arrived(w_r.at[o, :, span], w_s.at[ch, i], w_rs.at[ch, o])
        r = w_r[0, :, span]
        for k in range(1, n_sh):
            r = r + w_r[k, :, span]
        if split_z:
            for k in range(nz):
                r_buf[k, :, span] = r[k * zrows : (k + 1) * zrows]
            z_r[z, :, span] = r_buf[z, :, span]
        else:
            z_r[z, :, span] = r
        for i in range(1, nz):
            o = at_z(i)
            src = r_buf.at[o, :, span] if split_z else z_r.at[z, :, span]
            send(src, z_r.at[z, :, span], zr_s.at[ch, i], zr_r.at[ch, z], (2 * o + c, s))

    def over_z(ch, span):
        for i in range(1, nz):
            o = at_z(i)
            arrived(z_r.at[o, :, span], zr_s.at[ch, i], zr_r.at[ch, o])
        r = z_r[0, :, span]
        for k in range(1, nz):
            r = r + z_r[k, :, span]
        if split_z:
            z_full[z, :, span] = r
            part = z_full.at[z, :, span]
            for i in range(1, nz):
                send(part, part, za_s.at[ch, i], za_r.at[ch, z], (2 * at_z(i) + c, s))
        else:
            z_full[0, :, span] = r

    def share_out(ch, span):
        r = z_full[0, :, span]
        if split_z:
            for i in range(1, nz):
                o = at_z(i)
                arrived(z_full.at[o, :, span], za_s.at[ch, i], za_r.at[ch, o])
            r = jnp.concatenate([z_full[k, :, span] for k in range(nz)], axis=0)
        y_all[mine, :, span] = dot(linv, r, NN, HIGH)
        part = y_all.at[mine, :, span]
        for i in range(1, n_sh):
            send(part, part, y_s.at[ch, i], y_r.at[ch, s], (d, at_sh(i)))
        send(part, part, yc_s.at[ch, 0], yc_r.at[ch, s], (sib, s))

    for step in range(n_ch + 2):
        if step < n_ch:
            over_shards(step, spans[step])
        if 0 <= step - 1 < n_ch:
            over_z(step - 1, spans[step - 1])
        if 0 <= step - 2 < n_ch:
            share_out(step - 2, spans[step - 2])

    stores = []

    def finish(k, ch):
        lo_lane, hi_lane = chunks[ch]
        hi, lo = halves(y_all[k, :, spans[ch]])
        mf[k, :, spans[ch]] = mf[k, :, spans[ch]] - dot(ph3, jnp.concatenate([hi, lo, hi], axis=0))
        if aligned:
            columns = pl.ds(pl.multiple_of(k * width + lo_lane, 128), hi_lane - lo_lane)
            copy = pltpu.make_async_copy(
                mf.at[k, :, spans[ch]], out_hbm.at[0, :, columns], out_sem.at[len(stores)]
            )
            copy.start()
            stores.append(copy)

    for ch, span in enumerate(spans):
        finish(mine, ch)
        arrived(y_all.at[other, :, span], yc_s.at[ch, 0], yc_r.at[ch, s])
        finish(other, ch)
    late = []
    for h in range(2):
        if aligned:
            target = qnew_hbm.at[:, h * width : (h + 1) * width]
            copy = pltpu.make_async_copy(y_all.at[2 * s + h], target, qn_sem.at[h])
            copy.start()
            late.append(copy)
        else:
            qn_v[:, h * width : (h + 1) * width] = y_all[2 * s + h]
    for ch, span in enumerate(spans):
        for i in range(1, n_sh):
            o = at_sh(i)
            part = y_all.at[2 * o + c, :, span]
            arrived(part, y_s.at[ch, i], y_r.at[ch, o])
            send(part, part, yc_s.at[ch, i], yc_r.at[ch, o], (sib, s))
        for i in range(1, n_sh):
            finish(2 * at_sh(i) + c, ch)
        for i in range(1, n_sh):
            o = at_sh(i)
            arrived(y_all.at[2 * o + oc, :, span], yc_s.at[ch, i], yc_r.at[ch, o])
            finish(2 * o + oc, ch)
    if not aligned:
        for k in range(pieces):
            out_v[:, k * width : (k + 1) * width] = mf[k]
        for src, dst, sem in ((out_v, out_hbm.at[0], out_sem.at[0]), (qn_v, qnew_hbm, qn_sem.at[0])):
            copy = pltpu.make_async_copy(src, dst, sem)
            copy.start()
            late.append(copy)
    for copy in sends:
        copy.wait_send()
    for copy in stores + late:
        copy.wait()


def place(out_from, q_from, out_to, q_to, sems):
    n_rows = out_from.shape[1]
    step = n_rows // PLACE_PARTS
    copies = [pltpu.make_async_copy(q_from, q_to, sems.at[PLACE_PARTS])]
    for i in range(PLACE_PARTS):
        rows = pl.ds(i * step, step)
        copies.append(pltpu.make_async_copy(out_from.at[0, rows], out_to.at[0, rows], sems.at[i]))
    for copy in copies:
        copy.start()
    for copy in copies:
        copy.wait()


def per_device(n_dp, n_sh, grads, errors, q_prev):
    _, n_rows, full = grads.shape
    share, rank = q_prev.shape
    width = share // 2
    nz = n_dp // 2
    split_z = rank % (8 * nz) == 0
    zrows = rank // nz if split_z else rank
    aligned = width % 128 == 0
    pieces = 2 * n_sh
    dims = (n_dp, n_sh, nz, zrows, split_z, aligned, width)
    chunks = ((0, width),)
    if aligned and width >= N_CHUNKS * 128:
        tiles = width // 128
        edges = [-(-tiles * i // N_CHUNKS) * 128 for i in range(N_CHUNKS + 1)]
        chunks = tuple(zip(edges[:-1], edges[1:]))
    vm = pltpu.VMEM
    dma = pltpu.SemaphoreType.DMA
    small = (8, 128)
    scratch = [
        vm((n_rows, full), BF16),
        vm((n_rows, full), F32),
        vm(small if aligned else (rank, share), F32),
        vm((pieces, 2 * n_rows, width), BF16),
        vm((pieces, n_rows, width), F32),
        vm((pieces, rank, width), F32),
        vm((n_dp, rank // 2, 2 * n_rows), F32),
        vm((n_sh, rank, 128), F32),
        vm((n_sh, rank, width), F32),
        vm((n_sh, rank, width), F32),
        vm((n_sh, rank, width), F32),
        vm((n_sh, rank, width), F32),
        vm((nz, zrows, width) if split_z else small, F32),
        vm((nz, zrows, width), F32),
        vm((nz, zrows, width) if split_z else (1, rank, width), F32),
        vm((pieces, rank, width), F32),
        vm(small if aligned else (n_rows, full), F32),
        vm(small if aligned else (rank, share), F32),
        dma((4,)),
    ]
    n_ch = len(chunks)
    per_chunk = [(n_ch, n_sh)] * 2 + [(n_dp,), (n_sh,)] + [(n_ch, n_sh)] * 2 + [(n_ch, nz)] * 2 + [(n_ch, n_sh)] * 2
    for shape in per_chunk:
        scratch += [dma(shape), dma(shape)]
    scratch += [dma((n_ch * pieces,)), dma((2,))]
    shapes = (
        jax.ShapeDtypeStruct((1, n_rows, full), F32),
        jax.ShapeDtypeStruct((rank, share), F32),
    )
    hbm = pl.BlockSpec(memory_space=pl.ANY)
    out, q_new = pl.pallas_call(
        functools.partial(kernel, dims, chunks),
        out_shape=shapes,
        in_specs=[hbm, hbm, hbm],
        out_specs=(hbm, hbm),
        scratch_shapes=scratch,
        compiler_params=pltpu.CompilerParams(
            collective_id=0, has_side_effects=True, vmem_limit_bytes=62 * 1024 * 1024
        ),
        cost_estimate=pl.CostEstimate(
            flops=18 * n_rows * full * rank, bytes_accessed=10 * n_rows * full, transcendentals=0
        ),
    )(grads, errors, q_prev.T)
    out, q_new = pl.pallas_call(
        place,
        out_shape=shapes,
        in_specs=[hbm, hbm],
        out_specs=(hbm, hbm),
        scratch_shapes=[dma((PLACE_PARTS + 1,))],
        compiler_params=pltpu.CompilerParams(vmem_limit_bytes=62 * 1024 * 1024),
    )(out, q_new)
    return out, q_new.T


def solution(mesh):
    in_specs = (P("dp", "shard", None), P("dp", "shard", None), P("shard", None))
    out_specs = (P("dp", "shard", None), P("shard", None))
    return jax.shard_map(
        functools.partial(per_device, mesh.shape["dp"], mesh.shape["shard"]),
        mesh=mesh, in_specs=in_specs, out_specs=out_specs, check_vma=False,
    )
```

```python
import functools
import math

import jax
import jax.numpy as jnp
from jax import lax
from jax.experimental import pallas as pl
from jax.experimental.pallas import tpu as pltpu
from jax.sharding import PartitionSpec as P

MESH = pl.DeviceIdType.MESH
HIGH = lax.Precision.HIGHEST
F32 = jnp.float32
BF16 = jnp.bfloat16
NT = (((1,), (1,)), ((), ()))
NN = (((1,), (0,)), ((), ()))
N_CHUNKS = 2
PLACE_PARTS = 4


def dot(a, b, dims=NN, precision=None):
    return lax.dot_general(a, b, dims, precision=precision, preferred_element_type=F32)


def halves(x):
    hi = x.astype(BF16)
    return hi, (x - hi.astype(F32)).astype(BF16)


def inverse_factor(gram):
    n = gram.shape[0]
    rows = lax.broadcasted_iota(jnp.int32, (n, 128), 0)
    lanes = lax.broadcasted_iota(jnp.int32, (n, 128), 1)
    work = jnp.where(lanes == rows + n, 1.0, gram)
    block = 8
    for first in range(0, n, block):
        columns = [jnp.broadcast_to(work[:, first + t : first + t + 1], (n, 128)) for t in range(block)]
        for t in range(block):
            j = first + t
            scale = jnp.where(rows > j, columns[t] * (1.0 / columns[t][j : j + 1]), 0.0)
            for u in range(t + 1, block):
                columns[u] = columns[u] - scale * columns[u][j : j + 1]
            work = work - scale * work[j : j + 1]
    diag = jnp.sum(jnp.where(lanes == rows, work, 0.0), axis=1, keepdims=True)
    work = work * lax.rsqrt(diag)
    return work[:, n : 2 * n]


def kernel(
    dims, chunks, g_hbm, e_hbm, q_hbm, out_hbm, qnew_hbm,
    g_v, e_v, q_v, m2, mf, q_all, pbuf, gbuf, w_a, w_b, w_c, w_r, r_buf, z_r, z_full, y_all, out_v, qn_v,
    in_sem, q_s, q_r, qf_s, qf_r, p_s, p_r, g_s, g_r, c_s, c_r, w_s, w_rs, zr_s, zr_r, za_s, za_r,
    y_s, y_r, yc_s, yc_r, out_sem, qn_sem,
):
    n_dp, n_sh, side, nz, zrows, split_z, aligned, width = dims
    spans = [pl.ds(lo, hi - lo) for lo, hi in chunks]
    n_ch = len(chunks)
    rank = q_hbm.shape[0]
    pieces = 2 * n_sh
    d = lax.axis_index("dp")
    s = lax.axis_index("shard")
    z = d // 2
    c = d % 2
    oc = 1 - c
    sib = d + 1 - 2 * c

    load_g = pltpu.make_async_copy(g_hbm.at[0], g_v, in_sem.at[0])
    load_e = pltpu.make_async_copy(e_hbm.at[0], e_v, in_sem.at[1])
    q_loads = []
    if aligned:
        for h in range(2):
            half_copy = pltpu.make_async_copy(
                q_hbm.at[:, h * width : (h + 1) * width], q_all.at[2 * s + h], in_sem.at[2 + h]
            )
            half_copy.start()
            q_loads.append(half_copy)
    else:
        whole_copy = pltpu.make_async_copy(q_hbm, q_v, in_sem.at[2])
        whole_copy.start()
        q_loads.append(whole_copy)
    load_g.start()
    load_e.start()

    def at_dp(i):
        return lax.rem(d + i, n_dp)

    def at_sh(i, core=c):
        first, second = i % side, i // side
        across = first + core * (second - first)
        down = second + core * (first - second)
        return lax.rem(s // side + down, side) * side + lax.rem(s % side + across, side)

    def at_z(i):
        return lax.rem(z + i, nz)

    barrier = pltpu.get_barrier_semaphore()
    for i in range(1, n_dp):
        pl.semaphore_signal(barrier, inc=1, device_id=(at_dp(i), s), device_id_type=MESH)
    for i in range(1, n_sh):
        pl.semaphore_signal(barrier, inc=1, device_id=(d, at_sh(i)), device_id_type=MESH)
    for q_load in q_loads:
        q_load.wait()
    if not aligned:
        for h in range(2):
            q_all[2 * s + h] = q_v[:, h * width : (h + 1) * width]
    pl.semaphore_wait(barrier, n_dp - 1 + n_sh - 1)

    def remote(src, dst, send, recv, target):
        return pltpu.make_async_remote_copy(
            src_ref=src, dst_ref=dst, send_sem=send, recv_sem=recv, device_id=target, device_id_type=MESH
        )

    sends = []

    def send(src, dst, send_sem, recv_sem, target):
        copy = remote(src, dst, send_sem, recv_sem, target)
        copy.start()
        sends.append(copy)

    def arrived(dst, send_sem, recv_sem):
        remote(dst, dst, send_sem, recv_sem, (sib, s)).wait_recv()

    mine = 2 * s + c
    other = 2 * s + oc
    for ch, span in enumerate(spans):
        part = q_all.at[mine, :, span]
        for i in range(1, n_sh):
            send(part, part, q_s.at[ch, i], q_r.at[ch, s], (d, at_sh(i)))

    load_g.wait()
    load_e.wait()
    for k in range(pieces):
        cols = slice(k * width, (k + 1) * width)
        m = g_v[:, cols].astype(F32) + e_v[:, cols]
        hi, lo = halves(m)
        mf[k] = m
        m2[k, : m.shape[0]] = hi
        m2[k, m.shape[0] :] = lo

    def left_term(k, span):
        hi, lo = halves(q_all[k, :, span])
        return dot(jnp.concatenate([hi, lo], axis=0), m2[k, :, span], NT)

    acc = left_term(2 * s, pl.ds(0, width)) + left_term(2 * s + 1, pl.ds(0, width))
    for ch, span in enumerate(spans):
        for i in range(1, n_sh):
            o = at_sh(i)
            part = q_all.at[2 * o + c, :, span]
            arrived(part, q_s.at[ch, i], q_r.at[ch, o])
            send(part, part, qf_s.at[ch, i], qf_r.at[ch, o], (sib, s))
        for i in range(1, n_sh):
            acc = acc + left_term(2 * at_sh(i) + c, span)
        for i in range(1, n_sh):
            o = at_sh(i, oc)
            arrived(q_all.at[2 * o + oc, :, span], qf_s.at[ch, i], qf_r.at[ch, o])
            acc = acc + left_term(2 * o + oc, span)
    acc = acc[:rank] + acc[rank:]
    n_rows = mf.shape[1]
    part = acc[:, :n_rows] + acc[:, n_rows:]
    half = rank // 2

    pbuf[d] = jnp.concatenate([part[:half], part[half:]], axis=1)
    for i in range(1, n_dp):
        send(pbuf.at[d], pbuf.at[d], p_s.at[i], p_r.at[d], (at_dp(i), s))
    for i in range(1, n_dp):
        o = at_dp(i)
        arrived(pbuf.at[o], p_s.at[i], p_r.at[o])
    total = pbuf[0]
    for k in range(1, n_dp):
        total = total + pbuf[k]
    total = total * (1.0 / n_dp)
    pt = jnp.concatenate([total[:, :n_rows], total[:, n_rows:]], axis=0)

    twice = jnp.concatenate([pt, pt], axis=1) * (1.0 / n_dp)
    p_hi, p_lo = halves(twice)
    p2 = jnp.concatenate([p_hi, p_lo], axis=0)

    def w_term(k, span):
        t = dot(p2, m2[k, :, span])
        return t[:rank] + t[rank:]

    order = list(range(1, n_sh)) + [0]
    for ch, span in enumerate(spans):
        for i in order:
            o = at_sh(i, oc)
            w_a[o, :, span] = w_term(2 * o + oc, span)
            send(w_a.at[o, :, span], w_b.at[o, :, span], c_s.at[ch, i], c_r.at[ch, o], (sib, s))
        if ch == 0:
            padded = jnp.concatenate([pt, jnp.zeros((128 - rank, n_rows), F32)], axis=0)
            gbuf[s] = dot(pt, padded, NT, HIGH)
            for i in range(1, n_sh):
                send(gbuf.at[s], gbuf.at[s], g_s.at[i], g_r.at[s], (d, at_sh(i)))
        for i in order:
            o = at_sh(i)
            own = w_term(2 * o + c, span)
            arrived(w_b.at[o, :, span], c_s.at[ch, i], c_r.at[ch, o])
            if i == 0:
                w_r[s, :, span] = own + w_b[s, :, span]
            else:
                w_c[o, :, span] = own + w_b[o, :, span]
                send(
                    w_c.at[o, :, span], w_r.at[s, :, span], w_s.at[ch, i], w_rs.at[ch, s], (d, at_sh(i))
                )

    for i in range(1, n_sh):
        o = at_sh(i)
        arrived(gbuf.at[o], g_s.at[i], g_r.at[o])
    gram = gbuf[0]
    for k in range(1, n_sh):
        gram = gram + gbuf[k]
    linv = inverse_factor(gram)
    p_hat_t = dot(linv, pt, NN, HIGH)
    three = jnp.concatenate([p_hat_t, p_hat_t, p_hat_t], axis=0)
    rounded = three.astype(BF16).astype(F32)
    row = lax.broadcasted_iota(jnp.int32, three.shape, 0)
    ph3 = jnp.where(row < 2 * rank, rounded, three - rounded).T.astype(BF16)

    def over_shards(ch, span):
        for i in range(1, n_sh):
            o = at_sh(i)
            arrived(w_r.at[o, :, span], w_s.at[ch, i], w_rs.at[ch, o])
        r = w_r[0, :, span]
        for k in range(1, n_sh):
            r = r + w_r[k, :, span]
        if split_z:
            for k in range(nz):
                r_buf[k, :, span] = r[k * zrows : (k + 1) * zrows]
            z_r[z, :, span] = r_buf[z, :, span]
        else:
            z_r[z, :, span] = r
        for i in range(1, nz):
            o = at_z(i)
            src = r_buf.at[o, :, span] if split_z else z_r.at[z, :, span]
            send(src, z_r.at[z, :, span], zr_s.at[ch, i], zr_r.at[ch, z], (2 * o + c, s))

    def over_z(ch, span):
        for i in range(1, nz):
            o = at_z(i)
            arrived(z_r.at[o, :, span], zr_s.at[ch, i], zr_r.at[ch, o])
        r = z_r[0, :, span]
        for k in range(1, nz):
            r = r + z_r[k, :, span]
        if split_z:
            z_full[z, :, span] = r
            part = z_full.at[z, :, span]
            for i in range(1, nz):
                send(part, part, za_s.at[ch, i], za_r.at[ch, z], (2 * at_z(i) + c, s))
        else:
            z_full[0, :, span] = r

    def share_out(ch, span):
        r = z_full[0, :, span]
        if split_z:
            for i in range(1, nz):
                o = at_z(i)
                arrived(z_full.at[o, :, span], za_s.at[ch, i], za_r.at[ch, o])
            r = jnp.concatenate([z_full[k, :, span] for k in range(nz)], axis=0)
        y_all[mine, :, span] = dot(linv, r, NN, HIGH)
        part = y_all.at[mine, :, span]
        for i in range(1, n_sh):
            send(part, part, y_s.at[ch, i], y_r.at[ch, s], (d, at_sh(i)))
        send(part, part, yc_s.at[ch, 0], yc_r.at[ch, s], (sib, s))

    for step in range(n_ch + 2):
        if step < n_ch:
            over_shards(step, spans[step])
        if 0 <= step - 1 < n_ch:
            over_z(step - 1, spans[step - 1])
        if 0 <= step - 2 < n_ch:
            share_out(step - 2, spans[step - 2])

    stores = []

    def finish(k, ch):
        lo_lane, hi_lane = chunks[ch]
        hi, lo = halves(y_all[k, :, spans[ch]])
        mf[k, :, spans[ch]] = mf[k, :, spans[ch]] - dot(ph3, jnp.concatenate([hi, lo, hi], axis=0))
        if aligned:
            columns = pl.ds(pl.multiple_of(k * width + lo_lane, 128), hi_lane - lo_lane)
            copy = pltpu.make_async_copy(
                mf.at[k, :, spans[ch]], out_hbm.at[0, :, columns], out_sem.at[len(stores)]
            )
            copy.start()
            stores.append(copy)

    for ch, span in enumerate(spans):
        finish(mine, ch)
        arrived(y_all.at[other, :, span], yc_s.at[ch, 0], yc_r.at[ch, s])
        finish(other, ch)
    late = []
    for h in range(2):
        if aligned:
            target = qnew_hbm.at[:, h * width : (h + 1) * width]
            copy = pltpu.make_async_copy(y_all.at[2 * s + h], target, qn_sem.at[h])
            copy.start()
            late.append(copy)
        else:
            qn_v[:, h * width : (h + 1) * width] = y_all[2 * s + h]
    for ch, span in enumerate(spans):
        for i in range(1, n_sh):
            o = at_sh(i)
            part = y_all.at[2 * o + c, :, span]
            arrived(part, y_s.at[ch, i], y_r.at[ch, o])
            send(part, part, yc_s.at[ch, i], yc_r.at[ch, o], (sib, s))
        for i in range(1, n_sh):
            finish(2 * at_sh(i) + c, ch)
        for i in range(1, n_sh):
            o = at_sh(i, oc)
            arrived(y_all.at[2 * o + oc, :, span], yc_s.at[ch, i], yc_r.at[ch, o])
            finish(2 * o + oc, ch)
    if not aligned:
        for k in range(pieces):
            out_v[:, k * width : (k + 1) * width] = mf[k]
        for src, dst, sem in ((out_v, out_hbm.at[0], out_sem.at[0]), (qn_v, qnew_hbm, qn_sem.at[0])):
            copy = pltpu.make_async_copy(src, dst, sem)
            copy.start()
            late.append(copy)
    for copy in sends:
        copy.wait_send()
    for copy in stores + late:
        copy.wait()


def place(out_from, q_from, out_to, q_to, out_v, q_v, in_sems, out_sems):
    n_rows = out_from.shape[1]
    step = n_rows // PLACE_PARTS
    pairs = [(q_from, q_v, q_to)]
    for i in range(PLACE_PARTS):
        rows = pl.ds(i * step, step)
        pairs.append((out_from.at[0, rows], out_v.at[rows], out_to.at[0, rows]))
    loads = [pltpu.make_async_copy(src, mid, in_sems.at[i]) for i, (src, mid, _) in enumerate(pairs)]
    stores = [pltpu.make_async_copy(mid, dst, out_sems.at[i]) for i, (_, mid, dst) in enumerate(pairs)]
    for load in loads:
        load.start()
    for load, store in zip(loads, stores):
        load.wait()
        store.start()
    for store in stores:
        store.wait()


def per_device(n_dp, n_sh, grads, errors, q_prev):
    _, n_rows, full = grads.shape
    share, rank = q_prev.shape
    width = share // 2
    nz = n_dp // 2
    split_z = rank % (8 * nz) == 0
    zrows = rank // nz if split_z else rank
    aligned = width % 128 == 0
    pieces = 2 * n_sh
    dims = (n_dp, n_sh, math.isqrt(n_sh), nz, zrows, split_z, aligned, width)
    chunks = ((0, width),)
    if aligned and width >= N_CHUNKS * 128:
        tiles = width // 128
        edges = [-(-tiles * i // N_CHUNKS) * 128 for i in range(N_CHUNKS + 1)]
        chunks = tuple(zip(edges[:-1], edges[1:]))
    vm = pltpu.VMEM
    dma = pltpu.SemaphoreType.DMA
    small = (8, 128)
    scratch = [
        vm((n_rows, full), BF16),
        vm((n_rows, full), F32),
        vm(small if aligned else (rank, share), F32),
        vm((pieces, 2 * n_rows, width), BF16),
        vm((pieces, n_rows, width), F32),
        vm((pieces, rank, width), F32),
        vm((n_dp, rank // 2, 2 * n_rows), F32),
        vm((n_sh, rank, 128), F32),
        vm((n_sh, rank, width), F32),
        vm((n_sh, rank, width), F32),
        vm((n_sh, rank, width), F32),
        vm((n_sh, rank, width), F32),
        vm((nz, zrows, width) if split_z else small, F32),
        vm((nz, zrows, width), F32),
        vm((nz, zrows, width) if split_z else (1, rank, width), F32),
        vm((pieces, rank, width), F32),
        vm(small if aligned else (n_rows, full), F32),
        vm(small if aligned else (rank, share), F32),
        dma((4,)),
    ]
    n_ch = len(chunks)
    per_chunk = [(n_ch, n_sh)] * 2 + [(n_dp,), (n_sh,)] + [(n_ch, n_sh)] * 2 + [(n_ch, nz)] * 2 + [(n_ch, n_sh)] * 2
    for shape in per_chunk:
        scratch += [dma(shape), dma(shape)]
    scratch += [dma((n_ch * pieces,)), dma((2,))]
    shapes = (
        jax.ShapeDtypeStruct((1, n_rows, full), F32),
        jax.ShapeDtypeStruct((rank, share), F32),
    )
    hbm = pl.BlockSpec(memory_space=pl.ANY)
    out, q_new = pl.pallas_call(
        functools.partial(kernel, dims, chunks),
        out_shape=shapes,
        in_specs=[hbm, hbm, hbm],
        out_specs=(hbm, hbm),
        scratch_shapes=scratch,
        compiler_params=pltpu.CompilerParams(
            collective_id=0, has_side_effects=True, vmem_limit_bytes=62 * 1024 * 1024
        ),
        cost_estimate=pl.CostEstimate(
            flops=18 * n_rows * full * rank, bytes_accessed=10 * n_rows * full, transcendentals=0
        ),
    )(grads, errors, q_prev.T)
    out, q_new = pl.pallas_call(
        place,
        out_shape=shapes,
        in_specs=[hbm, hbm],
        out_specs=(hbm, hbm),
        scratch_shapes=[
            vm((n_rows, full), F32), vm((rank, share), F32), dma((PLACE_PARTS + 1,)), dma((PLACE_PARTS + 1,)),
        ],
        compiler_params=pltpu.CompilerParams(vmem_limit_bytes=62 * 1024 * 1024),
    )(out, q_new)
    return out, q_new.T


def solution(mesh):
    in_specs = (P("dp", "shard", None), P("dp", "shard", None), P("shard", None))
    out_specs = (P("dp", "shard", None), P("shard", None))
    return jax.shard_map(
        functools.partial(per_device, mesh.shape["dp"], mesh.shape["shard"]),
        mesh=mesh, in_specs=in_specs, out_specs=out_specs, check_vma=False,
    )
```

```python
import functools
import math

import jax
import jax.numpy as jnp
from jax import lax
from jax.experimental import pallas as pl
from jax.experimental.pallas import tpu as pltpu
from jax.sharding import PartitionSpec as P

MESH = pl.DeviceIdType.MESH
HIGH = lax.Precision.HIGHEST
F32 = jnp.float32
BF16 = jnp.bfloat16
NT = (((1,), (1,)), ((), ()))
NN = (((1,), (0,)), ((), ()))
N_CHUNKS = 2
PLACE_PARTS = 4


def dot(a, b, dims=NN, precision=None):
    return lax.dot_general(a, b, dims, precision=precision, preferred_element_type=F32)


def halves(x):
    hi = x.astype(BF16)
    return hi, (x - hi.astype(F32)).astype(BF16)


def inverse_factor(gram):
    n = gram.shape[0]
    rows = lax.broadcasted_iota(jnp.int32, (n, 128), 0)
    lanes = lax.broadcasted_iota(jnp.int32, (n, 128), 1)
    work = jnp.where(lanes == rows + n, 1.0, gram)
    block = 8
    for first in range(0, n, block):
        columns = [jnp.broadcast_to(work[:, first + t : first + t + 1], (n, 128)) for t in range(block)]
        for t in range(block):
            j = first + t
            scale = jnp.where(rows > j, columns[t] * (1.0 / columns[t][j : j + 1]), 0.0)
            for u in range(t + 1, block):
                columns[u] = columns[u] - scale * columns[u][j : j + 1]
            work = work - scale * work[j : j + 1]
    diag = jnp.sum(jnp.where(lanes == rows, work, 0.0), axis=1, keepdims=True)
    work = work * lax.rsqrt(diag)
    return work[:, n : 2 * n]


def kernel(
    dims, chunks, g_hbm, e_hbm, q_hbm, out_hbm, qnew_hbm,
    g_v, e_v, q_v, m2, mf, mx, q_all, pbuf, gbuf, w_c, w_r, r_buf, z_r, z_full, y_all, out_v, qn_v,
    in_sem, q_s, q_r, p_s, p_r, g_s, g_r, m_s, m_r, w_s, w_rs, zr_s, zr_r, za_s, za_r,
    y_s, y_r, yc_s, yc_r, out_sem, qn_sem,
):
    n_dp, n_sh, side, nz, zrows, split_z, aligned, width = dims
    spans = [pl.ds(lo, hi - lo) for lo, hi in chunks]
    n_ch = len(chunks)
    rank = q_hbm.shape[0]
    pieces = 2 * n_sh
    d = lax.axis_index("dp")
    s = lax.axis_index("shard")
    z = d // 2
    c = d % 2
    oc = 1 - c
    sib = d + 1 - 2 * c

    load_g = pltpu.make_async_copy(g_hbm.at[0], g_v, in_sem.at[0])
    load_e = pltpu.make_async_copy(e_hbm.at[0], e_v, in_sem.at[1])
    q_loads = []
    if aligned:
        for h in range(2):
            half_copy = pltpu.make_async_copy(
                q_hbm.at[:, h * width : (h + 1) * width], q_all.at[2 * s + h], in_sem.at[2 + h]
            )
            half_copy.start()
            q_loads.append(half_copy)
    else:
        whole_copy = pltpu.make_async_copy(q_hbm, q_v, in_sem.at[2])
        whole_copy.start()
        q_loads.append(whole_copy)
    load_g.start()
    load_e.start()

    def at_dp(i):
        return lax.rem(d + i, n_dp)

    def at_sh(i, core=c):
        first, second = i % side, i // side
        across = first + core * (second - first)
        down = second + core * (first - second)
        return lax.rem(s // side + down, side) * side + lax.rem(s % side + across, side)

    def at_z(i):
        return lax.rem(z + i, nz)

    barrier = pltpu.get_barrier_semaphore()
    for i in range(1, n_dp):
        pl.semaphore_signal(barrier, inc=1, device_id=(at_dp(i), s), device_id_type=MESH)
    for i in range(1, n_sh):
        pl.semaphore_signal(barrier, inc=1, device_id=(d, at_sh(i)), device_id_type=MESH)
    for q_load in q_loads:
        q_load.wait()
    if not aligned:
        for h in range(2):
            q_all[2 * s + h] = q_v[:, h * width : (h + 1) * width]
    pl.semaphore_wait(barrier, n_dp - 1 + n_sh - 1)

    def remote(src, dst, send, recv, target):
        return pltpu.make_async_remote_copy(
            src_ref=src, dst_ref=dst, send_sem=send, recv_sem=recv, device_id=target, device_id_type=MESH
        )

    sends = []

    def send(src, dst, send_sem, recv_sem, target):
        copy = remote(src, dst, send_sem, recv_sem, target)
        copy.start()
        sends.append(copy)

    def arrived(dst, send_sem, recv_sem):
        remote(dst, dst, send_sem, recv_sem, (sib, s)).wait_recv()

    mine = 2 * s + c
    other = 2 * s + oc
    for ch, span in enumerate(spans):
        part = q_all.at[mine, :, span]
        for i in range(1, n_sh):
            send(part, part, q_s.at[ch, i], q_r.at[ch, s], (d, at_sh(i)))

    load_g.wait()
    load_e.wait()
    for k in range(pieces):
        cols = slice(k * width, (k + 1) * width)
        mf[k] = g_v[:, cols].astype(F32) + e_v[:, cols]

    swaps = []
    for i in range(n_sh):
        o = at_sh(i)
        swap = remote(mf.at[2 * o + oc], mx.at[o], m_s.at[i], m_r.at[o], (sib, s))
        swap.start()
        swaps.append(swap)
    n_rows = mf.shape[1]
    for i in range(n_sh):
        o = at_sh(i)
        arrived(mx.at[o], m_s.at[i], m_r.at[o])
        hi, lo = halves(mf[2 * o + c] + mx[o])
        m2[o, :n_rows] = hi
        m2[o, n_rows:] = lo

    def left_term(o, span):
        hi, lo = halves(q_all[2 * o + c, :, span])
        return dot(jnp.concatenate([hi, lo], axis=0), m2[o, :, span], NT)

    acc = left_term(s, pl.ds(0, width))
    for ch, span in enumerate(spans):
        for i in range(1, n_sh):
            o = at_sh(i)
            arrived(q_all.at[2 * o + c, :, span], q_s.at[ch, i], q_r.at[ch, o])
            acc = acc + left_term(o, span)
    acc = acc[:rank] + acc[rank:]
    part = acc[:, :n_rows] + acc[:, n_rows:]
    half = rank // 2

    pbuf[d] = jnp.concatenate([part[:half], part[half:]], axis=1)
    for i in range(1, n_dp):
        send(pbuf.at[d], pbuf.at[d], p_s.at[i], p_r.at[d], (at_dp(i), s))
    for i in range(1, n_dp):
        o = at_dp(i)
        arrived(pbuf.at[o], p_s.at[i], p_r.at[o])
    total = pbuf[0]
    for k in range(1, n_dp):
        total = total + pbuf[k]
    total = total * (1.0 / n_dp)
    pt = jnp.concatenate([total[:, :n_rows], total[:, n_rows:]], axis=0)

    twice = jnp.concatenate([pt, pt], axis=1) * (1.0 / n_dp)
    p_hi, p_lo = halves(twice)
    p2 = jnp.concatenate([p_hi, p_lo], axis=0)

    def w_term(o, span):
        t = dot(p2, m2[o, :, span])
        return t[:rank] + t[rank:]

    for ch, span in enumerate(spans):
        for i in range(1, n_sh):
            o = at_sh(i)
            w_c[o, :, span] = w_term(o, span)
            send(w_c.at[o, :, span], w_r.at[s, :, span], w_s.at[ch, i], w_rs.at[ch, s], (d, at_sh(i)))
        if ch == 0:
            padded = jnp.concatenate([pt, jnp.zeros((128 - rank, n_rows), F32)], axis=0)
            gbuf[s] = dot(pt, padded, NT, HIGH)
            for i in range(1, n_sh):
                send(gbuf.at[s], gbuf.at[s], g_s.at[i], g_r.at[s], (d, at_sh(i)))
    for span in spans:
        w_r[s, :, span] = w_term(s, span)
    for swap in swaps:
        swap.wait_send()

    for i in range(1, n_sh):
        o = at_sh(i)
        arrived(gbuf.at[o], g_s.at[i], g_r.at[o])
    gram = gbuf[0]
    for k in range(1, n_sh):
        gram = gram + gbuf[k]
    linv = inverse_factor(gram)
    p_hat_t = dot(linv, pt, NN, HIGH)
    three = jnp.concatenate([p_hat_t, p_hat_t, p_hat_t], axis=0)
    rounded = three.astype(BF16).astype(F32)
    row = lax.broadcasted_iota(jnp.int32, three.shape, 0)
    ph3 = jnp.where(row < 2 * rank, rounded, three - rounded).T.astype(BF16)

    l3 = jnp.concatenate([linv, linv, linv], axis=1)
    l_rounded = l3.astype(BF16).astype(F32)
    lane = lax.broadcasted_iota(jnp.int32, l3.shape, 1)
    l3 = jnp.where(lane < 2 * rank, l_rounded, l3 - l_rounded).astype(BF16)

    def over_shards(ch, span):
        for i in range(1, n_sh):
            o = at_sh(i)
            arrived(w_r.at[o, :, span], w_s.at[ch, i], w_rs.at[ch, o])
        r = w_r[0, :, span]
        for k in range(1, n_sh):
            r = r + w_r[k, :, span]
        if split_z:
            for k in range(nz):
                r_buf[k, :, span] = r[k * zrows : (k + 1) * zrows]
            z_r[z, :, span] = r_buf[z, :, span]
        else:
            z_r[z, :, span] = r
        for i in range(1, nz):
            o = at_z(i)
            src = r_buf.at[o, :, span] if split_z else z_r.at[z, :, span]
            send(src, z_r.at[z, :, span], zr_s.at[ch, i], zr_r.at[ch, z], (2 * o + c, s))

    def over_z(ch, span):
        for i in range(1, nz):
            o = at_z(i)
            arrived(z_r.at[o, :, span], zr_s.at[ch, i], zr_r.at[ch, o])
        r = z_r[0, :, span]
        for k in range(1, nz):
            r = r + z_r[k, :, span]
        if split_z:
            z_full[z, :, span] = r
            part = z_full.at[z, :, span]
            for i in range(1, nz):
                send(part, part, za_s.at[ch, i], za_r.at[ch, z], (2 * at_z(i) + c, s))
        else:
            z_full[0, :, span] = r

    def share_out(ch, span):
        r = z_full[0, :, span]
        if split_z:
            for i in range(1, nz):
                o = at_z(i)
                arrived(z_full.at[o, :, span], za_s.at[ch, i], za_r.at[ch, o])
            r = jnp.concatenate([z_full[k, :, span] for k in range(nz)], axis=0)
        hi, lo = halves(r)
        y_all[mine, :, span] = dot(l3, jnp.concatenate([hi, lo, hi], axis=0))
        part = y_all.at[mine, :, span]
        for i in range(1, n_sh):
            send(part, part, y_s.at[ch, i], y_r.at[ch, s], (d, at_sh(i)))
        send(part, part, yc_s.at[ch, 0], yc_r.at[ch, s], (sib, s))

    for step in range(n_ch + 2):
        if step < n_ch:
            over_shards(step, spans[step])
        if 0 <= step - 1 < n_ch:
            over_z(step - 1, spans[step - 1])
        if 0 <= step - 2 < n_ch:
            share_out(step - 2, spans[step - 2])

    stores = []

    def finish(k, ch):
        lo_lane, hi_lane = chunks[ch]
        hi, lo = halves(y_all[k, :, spans[ch]])
        mf[k, :, spans[ch]] = mf[k, :, spans[ch]] - dot(ph3, jnp.concatenate([hi, lo, hi], axis=0))
        if aligned:
            columns = pl.ds(pl.multiple_of(k * width + lo_lane, 128), hi_lane - lo_lane)
            copy = pltpu.make_async_copy(
                mf.at[k, :, spans[ch]], out_hbm.at[0, :, columns], out_sem.at[len(stores)]
            )
            copy.start()
            stores.append(copy)

    for ch, span in enumerate(spans):
        finish(mine, ch)
        arrived(y_all.at[other, :, span], yc_s.at[ch, 0], yc_r.at[ch, s])
        finish(other, ch)
    late = []
    for h in range(2):
        if aligned:
            target = qnew_hbm.at[:, h * width : (h + 1) * width]
            copy = pltpu.make_async_copy(y_all.at[2 * s + h], target, qn_sem.at[h])
            copy.start()
            late.append(copy)
        else:
            qn_v[:, h * width : (h + 1) * width] = y_all[2 * s + h]
    for ch, span in enumerate(spans):
        for i in range(1, n_sh):
            o = at_sh(i)
            part = y_all.at[2 * o + c, :, span]
            arrived(part, y_s.at[ch, i], y_r.at[ch, o])
            send(part, part, yc_s.at[ch, i], yc_r.at[ch, o], (sib, s))
        for i in range(1, n_sh):
            finish(2 * at_sh(i) + c, ch)
        for i in range(1, n_sh):
            o = at_sh(i, oc)
            arrived(y_all.at[2 * o + oc, :, span], yc_s.at[ch, i], yc_r.at[ch, o])
            finish(2 * o + oc, ch)
    if not aligned:
        for k in range(pieces):
            out_v[:, k * width : (k + 1) * width] = mf[k]
        for src, dst, sem in ((out_v, out_hbm.at[0], out_sem.at[0]), (qn_v, qnew_hbm, qn_sem.at[0])):
            copy = pltpu.make_async_copy(src, dst, sem)
            copy.start()
            late.append(copy)
    for copy in sends:
        copy.wait_send()
    for copy in stores + late:
        copy.wait()


def place(out_from, q_from, out_to, q_to, out_v, q_v, in_sems, out_sems):
    n_rows = out_from.shape[1]
    step = n_rows // PLACE_PARTS
    pairs = [(q_from, q_v, q_to)]
    for i in range(PLACE_PARTS):
        rows = pl.ds(i * step, step)
        pairs.append((out_from.at[0, rows], out_v.at[rows], out_to.at[0, rows]))
    loads = [pltpu.make_async_copy(src, mid, in_sems.at[i]) for i, (src, mid, _) in enumerate(pairs)]
    stores = [pltpu.make_async_copy(mid, dst, out_sems.at[i]) for i, (_, mid, dst) in enumerate(pairs)]
    for load in loads:
        load.start()
    for load, store in zip(loads, stores):
        load.wait()
        store.start()
    for store in stores:
        store.wait()


def per_device(n_dp, n_sh, grads, errors, q_prev):
    _, n_rows, full = grads.shape
    share, rank = q_prev.shape
    width = share // 2
    nz = n_dp // 2
    split_z = rank % (8 * nz) == 0
    zrows = rank // nz if split_z else rank
    aligned = width % 128 == 0
    pieces = 2 * n_sh
    dims = (n_dp, n_sh, math.isqrt(n_sh), nz, zrows, split_z, aligned, width)
    chunks = ((0, width),)
    if aligned and width >= N_CHUNKS * 128:
        tiles = width // 128
        edges = [-(-tiles * i // N_CHUNKS) * 128 for i in range(N_CHUNKS + 1)]
        chunks = tuple(zip(edges[:-1], edges[1:]))
    vm = pltpu.VMEM
    dma = pltpu.SemaphoreType.DMA
    small = (8, 128)
    scratch = [
        vm((n_rows, full), BF16),
        vm((n_rows, full), F32),
        vm(small if aligned else (rank, share), F32),
        vm((n_sh, 2 * n_rows, width), BF16),
        vm((pieces, n_rows, width), F32),
        vm((n_sh, n_rows, width), F32),
        vm((pieces, rank, width), F32),
        vm((n_dp, rank // 2, 2 * n_rows), F32),
        vm((n_sh, rank, 128), F32),
        vm((n_sh, rank, width), F32),
        vm((n_sh, rank, width), F32),
        vm((nz, zrows, width) if split_z else small, F32),
        vm((nz, zrows, width), F32),
        vm((nz, zrows, width) if split_z else (1, rank, width), F32),
        vm((pieces, rank, width), F32),
        vm(small if aligned else (n_rows, full), F32),
        vm(small if aligned else (rank, share), F32),
        dma((4,)),
    ]
    n_ch = len(chunks)
    per_chunk = [(n_ch, n_sh), (n_dp,), (n_sh,), (n_sh,), (n_ch, n_sh)] + [(n_ch, nz)] * 2 + [(n_ch, n_sh)] * 2
    for shape in per_chunk:
        scratch += [dma(shape), dma(shape)]
    scratch += [dma((n_ch * pieces,)), dma((2,))]
    shapes = (
        jax.ShapeDtypeStruct((1, n_rows, full), F32),
        jax.ShapeDtypeStruct((rank, share), F32),
    )
    hbm = pl.BlockSpec(memory_space=pl.ANY)
    out, q_new = pl.pallas_call(
        functools.partial(kernel, dims, chunks),
        out_shape=shapes,
        in_specs=[hbm, hbm, hbm],
        out_specs=(hbm, hbm),
        scratch_shapes=scratch,
        compiler_params=pltpu.CompilerParams(
            collective_id=0, has_side_effects=True, vmem_limit_bytes=62 * 1024 * 1024
        ),
        cost_estimate=pl.CostEstimate(
            flops=18 * n_rows * full * rank, bytes_accessed=10 * n_rows * full, transcendentals=0
        ),
    )(grads, errors, q_prev.T)
    out, q_new = pl.pallas_call(
        place,
        out_shape=shapes,
        in_specs=[hbm, hbm],
        out_specs=(hbm, hbm),
        scratch_shapes=[
            vm((n_rows, full), F32), vm((rank, share), F32), dma((PLACE_PARTS + 1,)), dma((PLACE_PARTS + 1,)),
        ],
        compiler_params=pltpu.CompilerParams(vmem_limit_bytes=62 * 1024 * 1024),
    )(out, q_new)
    return out, q_new.T


def solution(mesh):
    in_specs = (P("dp", "shard", None), P("dp", "shard", None), P("shard", None))
    out_specs = (P("dp", "shard", None), P("shard", None))
    return jax.shard_map(
        functools.partial(per_device, mesh.shape["dp"], mesh.shape["shard"]),
        mesh=mesh, in_specs=in_specs, out_specs=out_specs, check_vma=False,
    )
```

```python
import functools
import math

import jax
import jax.numpy as jnp
from jax import lax
from jax.experimental import pallas as pl
from jax.experimental.pallas import tpu as pltpu
from jax.sharding import PartitionSpec as P

MESH = pl.DeviceIdType.MESH
HIGH = lax.Precision.HIGHEST
F32 = jnp.float32
BF16 = jnp.bfloat16
NT = (((1,), (1,)), ((), ()))
NN = (((1,), (0,)), ((), ()))
N_CHUNKS = 2
PLACE_PARTS = 4


def dot(a, b, dims=NN, precision=None):
    return lax.dot_general(a, b, dims, precision=precision, preferred_element_type=F32)


def halves(x):
    hi = x.astype(BF16)
    return hi, (x - hi.astype(F32)).astype(BF16)


def inverse_factor(gram):
    n = gram.shape[0]
    rows = lax.broadcasted_iota(jnp.int32, (n, 128), 0)
    lanes = lax.broadcasted_iota(jnp.int32, (n, 128), 1)
    work = jnp.where(lanes == rows + n, 1.0, gram)
    block = 8
    for first in range(0, n, block):
        columns = [jnp.broadcast_to(work[:, first + t : first + t + 1], (n, 128)) for t in range(block)]
        for t in range(block):
            j = first + t
            scale = jnp.where(rows > j, columns[t] * (1.0 / columns[t][j : j + 1]), 0.0)
            for u in range(t + 1, block):
                columns[u] = columns[u] - scale * columns[u][j : j + 1]
            work = work - scale * work[j : j + 1]
    diag = jnp.sum(jnp.where(lanes == rows, work, 0.0), axis=1, keepdims=True)
    work = work * lax.rsqrt(diag)
    return work[:, n : 2 * n]


def kernel(
    dims, chunks, g_hbm, e_hbm, q_hbm, out_hbm, qnew_hbm,
    g_v, e_v, q_v, m2, mf, mx, q_all, pbuf, gbuf, w_c, w_r, w_t, r_buf, z_r, z_full, y_all, out_v, qn_v,
    in_sem, q_s, q_r, p_s, p_r, g_s, g_r, m_s, m_r, w_s, w_rs, zr_s, zr_r, za_s, za_r,
    y_s, y_r, yc_s, yc_r, out_sem, qn_sem,
):
    n_dp, n_sh, side, nz, zrows, split_z, aligned, width = dims
    spans = [pl.ds(lo, hi - lo) for lo, hi in chunks]
    n_ch = len(chunks)
    rank = q_hbm.shape[0]
    pieces = 2 * n_sh
    d = lax.axis_index("dp")
    s = lax.axis_index("shard")
    z = d // 2
    c = d % 2
    oc = 1 - c
    sib = d + 1 - 2 * c

    load_g = pltpu.make_async_copy(g_hbm.at[0], g_v, in_sem.at[0])
    load_e = pltpu.make_async_copy(e_hbm.at[0], e_v, in_sem.at[1])
    q_loads = []
    if aligned:
        for h in range(2):
            half_copy = pltpu.make_async_copy(
                q_hbm.at[:, h * width : (h + 1) * width], q_all.at[2 * s + h], in_sem.at[2 + h]
            )
            half_copy.start()
            q_loads.append(half_copy)
    else:
        whole_copy = pltpu.make_async_copy(q_hbm, q_v, in_sem.at[2])
        whole_copy.start()
        q_loads.append(whole_copy)
    load_g.start()
    load_e.start()

    def at_dp(i):
        return lax.rem(d + i, n_dp)

    def at_sh(i, core=c):
        first, second = i % side, i // side
        across = first + core * (second - first)
        down = second + core * (first - second)
        return lax.rem(s // side + down, side) * side + lax.rem(s % side + across, side)

    relay = side == 2 and n_ch == 2
    near, far, diag = at_sh(1), at_sh(2), at_sh(3)

    def at_z(i):
        return lax.rem(z + i, nz)

    barrier = pltpu.get_barrier_semaphore()
    for i in range(1, n_dp):
        pl.semaphore_signal(barrier, inc=1, device_id=(at_dp(i), s), device_id_type=MESH)
    for i in range(1, n_sh):
        pl.semaphore_signal(barrier, inc=1, device_id=(d, at_sh(i)), device_id_type=MESH)
    for q_load in q_loads:
        q_load.wait()
    if not aligned:
        for h in range(2):
            q_all[2 * s + h] = q_v[:, h * width : (h + 1) * width]
    pl.semaphore_wait(barrier, n_dp - 1 + n_sh - 1)

    def remote(src, dst, send, recv, target):
        return pltpu.make_async_remote_copy(
            src_ref=src, dst_ref=dst, send_sem=send, recv_sem=recv, device_id=target, device_id_type=MESH
        )

    sends = []

    def send(src, dst, send_sem, recv_sem, target):
        copy = remote(src, dst, send_sem, recv_sem, target)
        copy.start()
        sends.append(copy)

    def arrived(dst, send_sem, recv_sem):
        remote(dst, dst, send_sem, recv_sem, (sib, s)).wait_recv()

    mine = 2 * s + c
    other = 2 * s + oc
    def spread(buf, ch, sem_s, sem_r, peer, i):
        part = buf.at[mine, :, spans[ch]]
        send(part, part, sem_s.at[ch, i], sem_r.at[ch, s], (d, peer))

    def pass_on(buf, ch, sem_s, sem_r, owner, peer):
        part = buf.at[2 * owner + c, :, spans[ch]]
        send(part, part, sem_s.at[ch, 3], sem_r.at[ch, owner], (d, peer))

    def landed(buf, ch, sem_s, sem_r, owner):
        arrived(buf.at[2 * owner + c, :, spans[ch]], sem_s.at[ch, 1], sem_r.at[ch, owner])

    if relay:
        spread(q_all, 0, q_s, q_r, near, 1)
        spread(q_all, 1, q_s, q_r, far, 2)
        spread(q_all, 1, q_s, q_r, near, 1)
        spread(q_all, 0, q_s, q_r, far, 2)
    else:
        for ch in range(n_ch):
            for i in range(1, n_sh):
                spread(q_all, ch, q_s, q_r, at_sh(i), i)

    load_g.wait()
    load_e.wait()
    for k in range(pieces):
        cols = slice(k * width, (k + 1) * width)
        mf[k] = g_v[:, cols].astype(F32) + e_v[:, cols]

    swaps = []
    for i in range(n_sh):
        o = at_sh(i)
        swap = remote(mf.at[2 * o + oc], mx.at[o], m_s.at[i], m_r.at[o], (sib, s))
        swap.start()
        swaps.append(swap)
    n_rows = mf.shape[1]
    for i in range(n_sh):
        o = at_sh(i)
        arrived(mx.at[o], m_s.at[i], m_r.at[o])
        hi, lo = halves(mf[2 * o + c] + mx[o])
        m2[o, :n_rows] = hi
        m2[o, n_rows:] = lo

    def left_term(o, span):
        hi, lo = halves(q_all[2 * o + c, :, span])
        return dot(jnp.concatenate([hi, lo], axis=0), m2[o, :, span], NT)

    acc = left_term(s, pl.ds(0, width))
    if relay:
        landed(q_all, 0, q_s, q_r, near)
        pass_on(q_all, 0, q_s, q_r, near, far)
        landed(q_all, 1, q_s, q_r, far)
        pass_on(q_all, 1, q_s, q_r, far, near)
        acc = acc + left_term(near, spans[0]) + left_term(far, spans[1])
        for ch, owner in ((1, near), (0, far), (0, diag), (1, diag)):
            landed(q_all, ch, q_s, q_r, owner)
            acc = acc + left_term(owner, spans[ch])
    else:
        for ch, span in enumerate(spans):
            for i in range(1, n_sh):
                landed(q_all, ch, q_s, q_r, at_sh(i))
                acc = acc + left_term(at_sh(i), span)
    acc = acc[:rank] + acc[rank:]
    part = acc[:, :n_rows] + acc[:, n_rows:]
    half = rank // 2

    pbuf[d] = jnp.concatenate([part[:half], part[half:]], axis=1)
    for i in range(1, n_dp):
        send(pbuf.at[d], pbuf.at[d], p_s.at[i], p_r.at[d], (at_dp(i), s))
    for i in range(1, n_dp):
        o = at_dp(i)
        arrived(pbuf.at[o], p_s.at[i], p_r.at[o])
    total = pbuf[0]
    for k in range(1, n_dp):
        total = total + pbuf[k]
    total = total * (1.0 / n_dp)
    pt = jnp.concatenate([total[:, :n_rows], total[:, n_rows:]], axis=0)

    twice = jnp.concatenate([pt, pt], axis=1) * (1.0 / n_dp)
    p_hi, p_lo = halves(twice)
    p2 = jnp.concatenate([p_hi, p_lo], axis=0)

    def w_term(o, span):
        t = dot(p2, m2[o, :, span])
        return t[:rank] + t[rank:]

    def gram_terms():
        padded = jnp.concatenate([pt, jnp.zeros((128 - rank, n_rows), F32)], axis=0)
        gbuf[s] = dot(pt, padded, NT, HIGH)
        for i in range(1, n_sh):
            send(gbuf.at[s], gbuf.at[s], g_s.at[i], g_r.at[s], (d, at_sh(i)))

    def give(ch, peer, i):
        span = spans[ch]
        send(w_c.at[peer, :, span], w_r.at[s, :, span], w_s.at[ch, i], w_rs.at[ch, s], (d, peer))

    if relay:
        for ch, peer, slot in ((0, near, far), (1, far, near)):
            span = spans[ch]
            w_c[diag, :, span] = w_term(diag, span)
            send(w_c.at[diag, :, span], w_t.at[:, span], w_s.at[ch, 3], w_rs.at[ch, slot + n_sh], (d, peer))
        w_c[near, :, spans[0]] = w_term(near, spans[0])
        give(0, near, 1)
        w_c[far, :, spans[1]] = w_term(far, spans[1])
        give(1, far, 2)
        gram_terms()
        for ch, peer, i in ((0, far, 2), (1, near, 1)):
            span = spans[ch]
            own = w_term(peer, span)
            arrived(w_t.at[:, span], w_s.at[ch, 3], w_rs.at[ch, diag + n_sh])
            w_c[peer, :, span] = own + w_t[:, span]
            give(ch, peer, i)
    else:
        for ch, span in enumerate(spans):
            for i in range(1, n_sh):
                o = at_sh(i)
                w_c[o, :, span] = w_term(o, span)
                give(ch, o, i)
            if ch == 0:
                gram_terms()
    for span in spans:
        w_r[s, :, span] = w_term(s, span)
    for swap in swaps:
        swap.wait_send()

    for i in range(1, n_sh):
        o = at_sh(i)
        arrived(gbuf.at[o], g_s.at[i], g_r.at[o])
    gram = gbuf[0]
    for k in range(1, n_sh):
        gram = gram + gbuf[k]
    linv = inverse_factor(gram)
    p_hat_t = dot(linv, pt, NN, HIGH)
    three = jnp.concatenate([p_hat_t, p_hat_t, p_hat_t], axis=0)
    rounded = three.astype(BF16).astype(F32)
    row = lax.broadcasted_iota(jnp.int32, three.shape, 0)
    ph3 = jnp.where(row < 2 * rank, rounded, three - rounded).T.astype(BF16)

    l3 = jnp.concatenate([linv, linv, linv], axis=1)
    l_rounded = l3.astype(BF16).astype(F32)
    lane = lax.broadcasted_iota(jnp.int32, l3.shape, 1)
    l3 = jnp.where(lane < 2 * rank, l_rounded, l3 - l_rounded).astype(BF16)

    def over_shards(ch, span):
        sources = [near, far] if relay else [at_sh(i) for i in range(1, n_sh)]
        r = w_r[s, :, span]
        for o in sources:
            arrived(w_r.at[o, :, span], w_s.at[ch, 1], w_rs.at[ch, o])
            r = r + w_r[o, :, span]
        if split_z:
            for k in range(nz):
                r_buf[k, :, span] = r[k * zrows : (k + 1) * zrows]
            z_r[z, :, span] = r_buf[z, :, span]
        else:
            z_r[z, :, span] = r
        for i in range(1, nz):
            o = at_z(i)
            src = r_buf.at[o, :, span] if split_z else z_r.at[z, :, span]
            send(src, z_r.at[z, :, span], zr_s.at[ch, i], zr_r.at[ch, z], (2 * o + c, s))

    def over_z(ch, span):
        for i in range(1, nz):
            o = at_z(i)
            arrived(z_r.at[o, :, span], zr_s.at[ch, i], zr_r.at[ch, o])
        r = z_r[0, :, span]
        for k in range(1, nz):
            r = r + z_r[k, :, span]
        if split_z:
            z_full[z, :, span] = r
            part = z_full.at[z, :, span]
            for i in range(1, nz):
                send(part, part, za_s.at[ch, i], za_r.at[ch, z], (2 * at_z(i) + c, s))
        else:
            z_full[0, :, span] = r

    def share_out(ch, span):
        r = z_full[0, :, span]
        if split_z:
            for i in range(1, nz):
                o = at_z(i)
                arrived(z_full.at[o, :, span], za_s.at[ch, i], za_r.at[ch, o])
            r = jnp.concatenate([z_full[k, :, span] for k in range(nz)], axis=0)
        hi, lo = halves(r)
        y_all[mine, :, span] = dot(l3, jnp.concatenate([hi, lo, hi], axis=0))
        part = y_all.at[mine, :, span]
        for i in (1 + ch, 2 - ch) if relay else range(1, n_sh):
            spread(y_all, ch, y_s, y_r, at_sh(i), i)
        send(part, part, yc_s.at[ch, 0], yc_r.at[ch, s], (sib, s))

    for step in range(n_ch + 2):
        if step < n_ch:
            over_shards(step, spans[step])
        if 0 <= step - 1 < n_ch:
            over_z(step - 1, spans[step - 1])
        if 0 <= step - 2 < n_ch:
            share_out(step - 2, spans[step - 2])

    stores = []

    def finish(k, ch):
        lo_lane, hi_lane = chunks[ch]
        hi, lo = halves(y_all[k, :, spans[ch]])
        mf[k, :, spans[ch]] = mf[k, :, spans[ch]] - dot(ph3, jnp.concatenate([hi, lo, hi], axis=0))
        if aligned:
            columns = pl.ds(pl.multiple_of(k * width + lo_lane, 128), hi_lane - lo_lane)
            copy = pltpu.make_async_copy(
                mf.at[k, :, spans[ch]], out_hbm.at[0, :, columns], out_sem.at[len(stores)]
            )
            copy.start()
            stores.append(copy)

    for ch, span in enumerate(spans):
        finish(mine, ch)
        arrived(y_all.at[other, :, span], yc_s.at[ch, 0], yc_r.at[ch, s])
        finish(other, ch)
    late = []
    for h in range(2):
        if aligned:
            target = qnew_hbm.at[:, h * width : (h + 1) * width]
            copy = pltpu.make_async_copy(y_all.at[2 * s + h], target, qn_sem.at[h])
            copy.start()
            late.append(copy)
        else:
            qn_v[:, h * width : (h + 1) * width] = y_all[2 * s + h]
    def hand_over(ch, owner, i):
        part = y_all.at[2 * owner + c, :, spans[ch]]
        send(part, part, yc_s.at[ch, i], yc_r.at[ch, owner], (sib, s))

    def take(ch, owner):
        arrived(y_all.at[2 * owner + oc, :, spans[ch]], yc_s.at[ch, 0], yc_r.at[ch, owner])
        finish(2 * owner + oc, ch)

    if relay:
        first = ((0, near, far, 1), (1, far, near, 2))
        rest = ((0, far, 2), (1, near, 1), (0, diag, 3), (1, diag, 3))
        for ch, owner, peer, i in first:
            landed(y_all, ch, y_s, y_r, owner)
            pass_on(y_all, ch, y_s, y_r, owner, peer)
            hand_over(ch, owner, i)
            finish(2 * owner + c, ch)
        for ch, owner, i in rest:
            landed(y_all, ch, y_s, y_r, owner)
            hand_over(ch, owner, i)
            finish(2 * owner + c, ch)
        for ch, owner in ((0, far), (1, near), (0, near), (1, far), (0, diag), (1, diag)):
            take(ch, owner)
    else:
        for ch in range(n_ch):
            for i in range(1, n_sh):
                landed(y_all, ch, y_s, y_r, at_sh(i))
                hand_over(ch, at_sh(i), i)
            for i in range(1, n_sh):
                finish(2 * at_sh(i) + c, ch)
            for i in range(1, n_sh):
                take(ch, at_sh(i, oc))
    if not aligned:
        for k in range(pieces):
            out_v[:, k * width : (k + 1) * width] = mf[k]
        for src, dst, sem in ((out_v, out_hbm.at[0], out_sem.at[0]), (qn_v, qnew_hbm, qn_sem.at[0])):
            copy = pltpu.make_async_copy(src, dst, sem)
            copy.start()
            late.append(copy)
    for copy in sends:
        copy.wait_send()
    for copy in stores + late:
        copy.wait()


def place(out_from, q_from, out_to, q_to, out_v, q_v, in_sems, out_sems):
    n_rows = out_from.shape[1]
    step = n_rows // PLACE_PARTS
    pairs = [(q_from, q_v, q_to)]
    for i in range(PLACE_PARTS):
        rows = pl.ds(i * step, step)
        pairs.append((out_from.at[0, rows], out_v.at[rows], out_to.at[0, rows]))
    loads = [pltpu.make_async_copy(src, mid, in_sems.at[i]) for i, (src, mid, _) in enumerate(pairs)]
    stores = [pltpu.make_async_copy(mid, dst, out_sems.at[i]) for i, (_, mid, dst) in enumerate(pairs)]
    for load in loads:
        load.start()
    for load, store in zip(loads, stores):
        load.wait()
        store.start()
    for store in stores:
        store.wait()


def per_device(n_dp, n_sh, grads, errors, q_prev):
    _, n_rows, full = grads.shape
    share, rank = q_prev.shape
    width = share // 2
    nz = n_dp // 2
    split_z = rank % (8 * nz) == 0
    zrows = rank // nz if split_z else rank
    aligned = width % 128 == 0
    pieces = 2 * n_sh
    dims = (n_dp, n_sh, math.isqrt(n_sh), nz, zrows, split_z, aligned, width)
    chunks = ((0, width),)
    if aligned and width >= N_CHUNKS * 128:
        tiles = width // 128
        edges = [-(-tiles * i // N_CHUNKS) * 128 for i in range(N_CHUNKS + 1)]
        chunks = tuple(zip(edges[:-1], edges[1:]))
    vm = pltpu.VMEM
    dma = pltpu.SemaphoreType.DMA
    small = (8, 128)
    scratch = [
        vm((n_rows, full), BF16),
        vm((n_rows, full), F32),
        vm(small if aligned else (rank, share), F32),
        vm((n_sh, 2 * n_rows, width), BF16),
        vm((pieces, n_rows, width), F32),
        vm((n_sh, n_rows, width), F32),
        vm((pieces, rank, width), F32),
        vm((n_dp, rank // 2, 2 * n_rows), F32),
        vm((n_sh, rank, 128), F32),
        vm((n_sh, rank, width), F32),
        vm((n_sh, rank, width), F32),
        vm((rank, width), F32),
        vm((nz, zrows, width) if split_z else small, F32),
        vm((nz, zrows, width), F32),
        vm((nz, zrows, width) if split_z else (1, rank, width), F32),
        vm((pieces, rank, width), F32),
        vm(small if aligned else (n_rows, full), F32),
        vm(small if aligned else (rank, share), F32),
        dma((4,)),
    ]
    n_ch = len(chunks)
    per_chunk = [(n_ch, n_sh), (n_dp,), (n_sh,), (n_sh,), (n_ch, n_sh)] + [(n_ch, nz)] * 2 + [(n_ch, n_sh)] * 2
    per_chunk[4] = (n_ch, 2 * n_sh)
    for shape in per_chunk:
        scratch += [dma(shape), dma(shape)]
    scratch += [dma((n_ch * pieces,)), dma((2,))]
    shapes = (
        jax.ShapeDtypeStruct((1, n_rows, full), F32),
        jax.ShapeDtypeStruct((rank, share), F32),
    )
    hbm = pl.BlockSpec(memory_space=pl.ANY)
    out, q_new = pl.pallas_call(
        functools.partial(kernel, dims, chunks),
        out_shape=shapes,
        in_specs=[hbm, hbm, hbm],
        out_specs=(hbm, hbm),
        scratch_shapes=scratch,
        compiler_params=pltpu.CompilerParams(
            collective_id=0, has_side_effects=True, vmem_limit_bytes=62 * 1024 * 1024
        ),
        cost_estimate=pl.CostEstimate(
            flops=18 * n_rows * full * rank, bytes_accessed=10 * n_rows * full, transcendentals=0
        ),
    )(grads, errors, q_prev.T)
    out, q_new = pl.pallas_call(
        place,
        out_shape=shapes,
        in_specs=[hbm, hbm],
        out_specs=(hbm, hbm),
        scratch_shapes=[
            vm((n_rows, full), F32), vm((rank, share), F32), dma((PLACE_PARTS + 1,)), dma((PLACE_PARTS + 1,)),
        ],
        compiler_params=pltpu.CompilerParams(vmem_limit_bytes=62 * 1024 * 1024),
    )(out, q_new)
    return out, q_new.T


def solution(mesh):
    in_specs = (P("dp", "shard", None), P("dp", "shard", None), P("shard", None))
    out_specs = (P("dp", "shard", None), P("shard", None))
    return jax.shard_map(
        functools.partial(per_device, mesh.shape["dp"], mesh.shape["shard"]),
        mesh=mesh, in_specs=in_specs, out_specs=out_specs, check_vma=False,
    )
```

```python
import functools
import math

import jax
import jax.numpy as jnp
from jax import lax
from jax.experimental import pallas as pl
from jax.experimental.pallas import tpu as pltpu
from jax.sharding import PartitionSpec as P

MESH = pl.DeviceIdType.MESH
HIGH = lax.Precision.HIGHEST
F32 = jnp.float32
BF16 = jnp.bfloat16
NT = (((1,), (1,)), ((), ()))
NN = (((1,), (0,)), ((), ()))
N_CHUNKS = 3
PLACE_PARTS = 4


def dot(a, b, dims=NN, precision=None):
    return lax.dot_general(a, b, dims, precision=precision, preferred_element_type=F32)


def halves(x):
    hi = x.astype(BF16)
    return hi, (x - hi.astype(F32)).astype(BF16)


def inverse_factor(gram):
    n = gram.shape[0]
    rows = lax.broadcasted_iota(jnp.int32, (n, 128), 0)
    lanes = lax.broadcasted_iota(jnp.int32, (n, 128), 1)
    work = jnp.where(lanes == rows + n, 1.0, gram)
    block = 8
    for first in range(0, n, block):
        columns = [jnp.broadcast_to(work[:, first + t : first + t + 1], (n, 128)) for t in range(block)]
        for t in range(block):
            j = first + t
            scale = jnp.where(rows > j, columns[t] * (1.0 / columns[t][j : j + 1]), 0.0)
            for u in range(t + 1, block):
                columns[u] = columns[u] - scale * columns[u][j : j + 1]
            work = work - scale * work[j : j + 1]
    diag = jnp.sum(jnp.where(lanes == rows, work, 0.0), axis=1, keepdims=True)
    work = work * lax.rsqrt(diag)
    return work[:, n : 2 * n]


def kernel(
    dims, chunks, g_hbm, e_hbm, q_hbm, out_hbm, qnew_hbm,
    g_v, e_v, q_v, m2, mf, mx, q_all, pbuf, gbuf, w_c, w_r, r_buf, z_r, z_full, y_all, out_v, qn_v,
    in_sem, q_s, q_r, p_s, p_r, g_s, g_r, m_s, m_r, w_s, w_rs, zr_s, zr_r, za_s, za_r,
    y_s, y_r, yc_s, yc_r, out_sem, qn_sem,
):
    n_dp, n_sh, side, nz, zrows, split_z, aligned, width = dims
    spans = [pl.ds(lo, hi - lo) for lo, hi in chunks]
    n_ch = len(chunks)
    rank = q_hbm.shape[0]
    pieces = 2 * n_sh
    d = lax.axis_index("dp")
    s = lax.axis_index("shard")
    z = d // 2
    c = d % 2
    oc = 1 - c
    sib = d + 1 - 2 * c

    def at_dp(i):
        return lax.rem(d + i, n_dp)

    def at_sh(i, core=c):
        first, second = i % side, i // side
        across = first + core * (second - first)
        down = second + core * (first - second)
        return lax.rem(s // side + down, side) * side + lax.rem(s % side + across, side)

    def at_z(i):
        return lax.rem(z + i, nz)

    barrier = pltpu.get_barrier_semaphore()
    for i in range(1, n_dp):
        pl.semaphore_signal(barrier, inc=1, device_id=(at_dp(i), s), device_id_type=MESH)
    for i in range(1, n_sh):
        pl.semaphore_signal(barrier, inc=1, device_id=(d, at_sh(i)), device_id_type=MESH)

    q_loads = []
    if aligned:
        for h in range(2):
            half_copy = pltpu.make_async_copy(
                q_hbm.at[:, h * width : (h + 1) * width], q_all.at[2 * s + h], in_sem.at[2 + h]
            )
            half_copy.start()
            q_loads.append(half_copy)
    else:
        whole_copy = pltpu.make_async_copy(q_hbm, q_v, in_sem.at[2])
        whole_copy.start()
        q_loads.append(whole_copy)

    def merged_loads(k, slot):
        if not aligned:
            return []
        columns = pl.ds(pl.multiple_of(k * width, 128), width)
        return [
            pltpu.make_async_copy(src.at[0, :, columns], dst.at[k], in_sem.at[4 + 2 * slot + n])
            for n, (src, dst) in enumerate(((g_hbm, g_v), (e_hbm, e_v)))
        ]

    order = [(i, oc) for i in range(n_sh)] + [(i, c) for i in range(n_sh)]
    loads = [merged_loads(2 * at_sh(i, core) + core, slot) for slot, (i, core) in enumerate(order)]
    if not aligned:
        loads[0] = [
            pltpu.make_async_copy(g_hbm.at[0], g_v, in_sem.at[4]),
            pltpu.make_async_copy(e_hbm.at[0], e_v, in_sem.at[5]),
        ]
    for pair in loads:
        for copy in pair:
            copy.start()

    for q_load in q_loads:
        q_load.wait()
    if not aligned:
        for h in range(2):
            q_all[2 * s + h] = q_v[:, h * width : (h + 1) * width]
    pl.semaphore_wait(barrier, n_dp - 1 + n_sh - 1)

    def remote(src, dst, send, recv, target):
        return pltpu.make_async_remote_copy(
            src_ref=src, dst_ref=dst, send_sem=send, recv_sem=recv, device_id=target, device_id_type=MESH
        )

    sends = []

    def send(src, dst, send_sem, recv_sem, target):
        copy = remote(src, dst, send_sem, recv_sem, target)
        copy.start()
        sends.append(copy)

    def arrived(dst, send_sem, recv_sem):
        remote(dst, dst, send_sem, recv_sem, (sib, s)).wait_recv()

    mine = 2 * s + c
    other = 2 * s + oc
    for ch, span in enumerate(spans):
        part = q_all.at[mine, :, span]
        for i in range(1, n_sh):
            send(part, part, q_s.at[ch, i], q_r.at[ch, s], (d, at_sh(i)))

    n_rows = mf.shape[1]
    if not aligned:
        for copy in loads[0]:
            copy.wait()
        for k in range(pieces):
            cols = slice(k * width, (k + 1) * width)
            mf[k] = g_v[:, cols].astype(F32) + e_v[:, cols]

    def merge(slot):
        i, core = order[slot]
        k = 2 * at_sh(i, core) + core
        if aligned:
            for copy in loads[slot]:
                copy.wait()
            mf[k] = g_v[k].astype(F32) + e_v[k]
        return k

    swaps = []
    for i in range(n_sh):
        o = at_sh(i, oc)
        swap = remote(mf.at[merge(i)], mx.at[o], m_s.at[i], m_r.at[o], (sib, s))
        swap.start()
        swaps.append(swap)
    for i in range(n_sh):
        merge(n_sh + i)

    def chip_sum(o, i):
        arrived(mx.at[o], m_s.at[i], m_r.at[o])
        hi, lo = halves(mf[2 * o + c] + mx[o])
        m2[o, :n_rows] = hi
        m2[o, n_rows:] = lo

    def left_term(o, span):
        hi, lo = halves(q_all[2 * o + c, :, span])
        return dot(jnp.concatenate([hi, lo], axis=0), m2[o, :, span], NT)

    chip_sum(s, 0)
    acc = left_term(s, pl.ds(0, width))
    for ch, span in enumerate(spans):
        for i in range(1, n_sh):
            o = at_sh(i)
            if ch == 0:
                chip_sum(o, i)
            arrived(q_all.at[2 * o + c, :, span], q_s.at[ch, i], q_r.at[ch, o])
            acc = acc + left_term(o, span)
    acc = acc[:rank] + acc[rank:]
    part = acc[:, :n_rows] + acc[:, n_rows:]
    half = rank // 2

    pbuf[d] = jnp.concatenate([part[:half], part[half:]], axis=1)
    for i in range(1, n_dp):
        send(pbuf.at[d], pbuf.at[d], p_s.at[i], p_r.at[d], (at_dp(i), s))
    for i in range(1, n_dp):
        o = at_dp(i)
        arrived(pbuf.at[o], p_s.at[i], p_r.at[o])
    total = pbuf[0]
    for k in range(1, n_dp):
        total = total + pbuf[k]
    total = total * (1.0 / n_dp)
    pt = jnp.concatenate([total[:, :n_rows], total[:, n_rows:]], axis=0)

    twice = jnp.concatenate([pt, pt], axis=1) * (1.0 / n_dp)
    p_hi, p_lo = halves(twice)
    p2 = jnp.concatenate([p_hi, p_lo], axis=0)

    def w_term(o, span):
        t = dot(p2, m2[o, :, span])
        return t[:rank] + t[rank:]

    for ch, span in enumerate(spans):
        for i in range(1, n_sh):
            o = at_sh(i)
            w_c[o, :, span] = w_term(o, span)
            send(w_c.at[o, :, span], w_r.at[s, :, span], w_s.at[ch, i], w_rs.at[ch, s], (d, o))
            if ch == 0 and i == 1:
                padded = jnp.concatenate([pt, jnp.zeros((128 - rank, n_rows), F32)], axis=0)
                gbuf[s] = dot(pt, padded, NT, HIGH)
                for j in range(1, n_sh):
                    send(gbuf.at[s], gbuf.at[s], g_s.at[j], g_r.at[s], (d, at_sh(j)))
    for span in spans:
        w_r[s, :, span] = w_term(s, span)
    for swap in swaps:
        swap.wait_send()

    for i in range(1, n_sh):
        o = at_sh(i)
        arrived(gbuf.at[o], g_s.at[i], g_r.at[o])
    gram = gbuf[0]
    for k in range(1, n_sh):
        gram = gram + gbuf[k]
    linv = inverse_factor(gram)
    p_hat_t = dot(linv, pt, NN, HIGH)
    three = jnp.concatenate([p_hat_t, p_hat_t, p_hat_t], axis=0)
    rounded = three.astype(BF16).astype(F32)
    row = lax.broadcasted_iota(jnp.int32, three.shape, 0)
    ph3 = jnp.where(row < 2 * rank, rounded, three - rounded).T.astype(BF16)

    l3 = jnp.concatenate([linv, linv, linv], axis=1)
    l_rounded = l3.astype(BF16).astype(F32)
    lane = lax.broadcasted_iota(jnp.int32, l3.shape, 1)
    l3 = jnp.where(lane < 2 * rank, l_rounded, l3 - l_rounded).astype(BF16)

    def over_shards(ch, span):
        for i in range(1, n_sh):
            o = at_sh(i)
            arrived(w_r.at[o, :, span], w_s.at[ch, i], w_rs.at[ch, o])
        r = w_r[0, :, span]
        for k in range(1, n_sh):
            r = r + w_r[k, :, span]
        if split_z:
            for k in range(nz):
                r_buf[k, :, span] = r[k * zrows : (k + 1) * zrows]
            z_r[z, :, span] = r_buf[z, :, span]
        else:
            z_r[z, :, span] = r
        for i in range(1, nz):
            o = at_z(i)
            src = r_buf.at[o, :, span] if split_z else z_r.at[z, :, span]
            send(src, z_r.at[z, :, span], zr_s.at[ch, i], zr_r.at[ch, z], (2 * o + c, s))

    def over_z(ch, span):
        for i in range(1, nz):
            o = at_z(i)
            arrived(z_r.at[o, :, span], zr_s.at[ch, i], zr_r.at[ch, o])
        r = z_r[0, :, span]
        for k in range(1, nz):
            r = r + z_r[k, :, span]
        if split_z:
            z_full[z, :, span] = r
            part = z_full.at[z, :, span]
            for i in range(1, nz):
                send(part, part, za_s.at[ch, i], za_r.at[ch, z], (2 * at_z(i) + c, s))
        else:
            z_full[0, :, span] = r

    def share_out(ch, span):
        r = z_full[0, :, span]
        if split_z:
            for i in range(1, nz):
                o = at_z(i)
                arrived(z_full.at[o, :, span], za_s.at[ch, i], za_r.at[ch, o])
            r = jnp.concatenate([z_full[k, :, span] for k in range(nz)], axis=0)
        hi, lo = halves(r)
        y_all[mine, :, span] = dot(l3, jnp.concatenate([hi, lo, hi], axis=0))
        part = y_all.at[mine, :, span]
        for i in range(1, n_sh):
            send(part, part, y_s.at[ch, i], y_r.at[ch, s], (d, at_sh(i)))
        send(part, part, yc_s.at[ch, 0], yc_r.at[ch, s], (sib, s))

    for step in range(n_ch + 2):
        if step < n_ch:
            over_shards(step, spans[step])
        if 0 <= step - 1 < n_ch:
            over_z(step - 1, spans[step - 1])
        if 0 <= step - 2 < n_ch:
            share_out(step - 2, spans[step - 2])

    stores = []

    def finish(k, ch):
        lo_lane, hi_lane = chunks[ch]
        hi, lo = halves(y_all[k, :, spans[ch]])
        mf[k, :, spans[ch]] = mf[k, :, spans[ch]] - dot(ph3, jnp.concatenate([hi, lo, hi], axis=0))
        if aligned:
            columns = pl.ds(pl.multiple_of(k * width + lo_lane, 128), hi_lane - lo_lane)
            copy = pltpu.make_async_copy(
                mf.at[k, :, spans[ch]], out_hbm.at[0, :, columns], out_sem.at[len(stores)]
            )
            copy.start()
            stores.append(copy)

    for ch, span in enumerate(spans):
        finish(mine, ch)
        arrived(y_all.at[other, :, span], yc_s.at[ch, 0], yc_r.at[ch, s])
        finish(other, ch)
    late = []
    for h in range(2):
        if aligned:
            target = qnew_hbm.at[:, h * width : (h + 1) * width]
            copy = pltpu.make_async_copy(y_all.at[2 * s + h], target, qn_sem.at[h])
            copy.start()
            late.append(copy)
        else:
            qn_v[:, h * width : (h + 1) * width] = y_all[2 * s + h]
    for ch, span in enumerate(spans):
        for i in range(1, n_sh):
            o = at_sh(i)
            part = y_all.at[2 * o + c, :, span]
            arrived(part, y_s.at[ch, i], y_r.at[ch, o])
            send(part, part, yc_s.at[ch, i], yc_r.at[ch, o], (sib, s))
        for i in range(1, n_sh):
            finish(2 * at_sh(i) + c, ch)
        for i in range(1, n_sh):
            o = at_sh(i, oc)
            arrived(y_all.at[2 * o + oc, :, span], yc_s.at[ch, i], yc_r.at[ch, o])
            finish(2 * o + oc, ch)
    if not aligned:
        for k in range(pieces):
            out_v[:, k * width : (k + 1) * width] = mf[k]
        for src, dst, sem in ((out_v, out_hbm.at[0], out_sem.at[0]), (qn_v, qnew_hbm, qn_sem.at[0])):
            copy = pltpu.make_async_copy(src, dst, sem)
            copy.start()
            late.append(copy)
    for copy in sends:
        copy.wait_send()
    for copy in stores + late:
        copy.wait()


def place(out_from, q_from, out_to, q_to, out_v, q_v, in_sems, out_sems):
    n_rows = out_from.shape[1]
    step = n_rows // PLACE_PARTS
    pairs = [(q_from, q_v, q_to)]
    for i in range(PLACE_PARTS):
        rows = pl.ds(i * step, step)
        pairs.append((out_from.at[0, rows], out_v.at[rows], out_to.at[0, rows]))
    loads = [pltpu.make_async_copy(src, mid, in_sems.at[i]) for i, (src, mid, _) in enumerate(pairs)]
    stores = [pltpu.make_async_copy(mid, dst, out_sems.at[i]) for i, (_, mid, dst) in enumerate(pairs)]
    for load in loads:
        load.start()
    for load, store in zip(loads, stores):
        load.wait()
        store.start()
    for store in stores:
        store.wait()


def per_device(n_dp, n_sh, grads, errors, q_prev):
    _, n_rows, full = grads.shape
    share, rank = q_prev.shape
    width = share // 2
    nz = n_dp // 2
    split_z = rank % (8 * nz) == 0
    zrows = rank // nz if split_z else rank
    aligned = width % 128 == 0
    pieces = 2 * n_sh
    dims = (n_dp, n_sh, math.isqrt(n_sh), nz, zrows, split_z, aligned, width)
    chunks = ((0, width),)
    if aligned and width >= N_CHUNKS * 128:
        tiles = width // 128
        edges = [-(-tiles * i // N_CHUNKS) * 128 for i in range(N_CHUNKS + 1)]
        chunks = tuple(zip(edges[:-1], edges[1:]))
    vm = pltpu.VMEM
    dma = pltpu.SemaphoreType.DMA
    small = (8, 128)
    scratch = [
        vm((pieces, n_rows, width) if aligned else (n_rows, full), BF16),
        vm((pieces, n_rows, width) if aligned else (n_rows, full), F32),
        vm(small if aligned else (rank, share), F32),
        vm((n_sh, 2 * n_rows, width), BF16),
        vm((pieces, n_rows, width), F32),
        vm((n_sh, n_rows, width), F32),
        vm((pieces, rank, width), F32),
        vm((n_dp, rank // 2, 2 * n_rows), F32),
        vm((n_sh, rank, 128), F32),
        vm((n_sh, rank, width), F32),
        vm((n_sh, rank, width), F32),
        vm((nz, zrows, width) if split_z else small, F32),
        vm((nz, zrows, width), F32),
        vm((nz, zrows, width) if split_z else (1, rank, width), F32),
        vm((pieces, rank, width), F32),
        vm(small if aligned else (n_rows, full), F32),
        vm(small if aligned else (rank, share), F32),
        dma((4 + 2 * pieces,)),
    ]
    n_ch = len(chunks)
    per_chunk = [(n_ch, n_sh), (n_dp,), (n_sh,), (n_sh,), (n_ch, n_sh)] + [(n_ch, nz)] * 2 + [(n_ch, n_sh)] * 2
    for shape in per_chunk:
        scratch += [dma(shape), dma(shape)]
    scratch += [dma((n_ch * pieces,)), dma((2,))]
    shapes = (
        jax.ShapeDtypeStruct((1, n_rows, full), F32),
        jax.ShapeDtypeStruct((rank, share), F32),
    )
    hbm = pl.BlockSpec(memory_space=pl.ANY)
    out, q_new = pl.pallas_call(
        functools.partial(kernel, dims, chunks),
        out_shape=shapes,
        in_specs=[hbm, hbm, hbm],
        out_specs=(hbm, hbm),
        scratch_shapes=scratch,
        compiler_params=pltpu.CompilerParams(
            collective_id=0, has_side_effects=True, vmem_limit_bytes=62 * 1024 * 1024
        ),
        cost_estimate=pl.CostEstimate(
            flops=18 * n_rows * full * rank, bytes_accessed=10 * n_rows * full, transcendentals=0
        ),
    )(grads, errors, q_prev.T)
    out, q_new = pl.pallas_call(
        place,
        out_shape=shapes,
        in_specs=[hbm, hbm],
        out_specs=(hbm, hbm),
        scratch_shapes=[
            vm((n_rows, full), F32), vm((rank, share), F32), dma((PLACE_PARTS + 1,)), dma((PLACE_PARTS + 1,)),
        ],
        compiler_params=pltpu.CompilerParams(vmem_limit_bytes=62 * 1024 * 1024),
    )(out, q_new)
    return out, q_new.T


def solution(mesh):
    in_specs = (P("dp", "shard", None), P("dp", "shard", None), P("shard", None))
    out_specs = (P("dp", "shard", None), P("shard", None))
    return jax.shard_map(
        functools.partial(per_device, mesh.shape["dp"], mesh.shape["shard"]),
        mesh=mesh, in_specs=in_specs, out_specs=out_specs, check_vma=False,
    )
```

```python
import functools
import math

import jax
import jax.numpy as jnp
from jax import lax
from jax.experimental import pallas as pl
from jax.experimental.pallas import tpu as pltpu
from jax.sharding import PartitionSpec as P

MESH = pl.DeviceIdType.MESH
HIGH = lax.Precision.HIGHEST
F32 = jnp.float32
BF16 = jnp.bfloat16
NT = (((1,), (1,)), ((), ()))
NN = (((1,), (0,)), ((), ()))
N_CHUNKS = 2
PLACE_PARTS = 4


def dot(a, b, dims=NN, precision=None):
    return lax.dot_general(a, b, dims, precision=precision, preferred_element_type=F32)


def halves(x):
    hi = x.astype(BF16)
    return hi, (x - hi.astype(F32)).astype(BF16)


def inverse_factor(gram):
    n = gram.shape[0]
    rows = lax.broadcasted_iota(jnp.int32, (n, 128), 0)
    lanes = lax.broadcasted_iota(jnp.int32, (n, 128), 1)
    work = jnp.where(lanes == rows + n, 1.0, gram)
    block = 8
    for first in range(0, n, block):
        columns = [jnp.broadcast_to(work[:, first + t : first + t + 1], (n, 128)) for t in range(block)]
        for t in range(block):
            j = first + t
            scale = jnp.where(rows > j, columns[t] * (1.0 / columns[t][j : j + 1]), 0.0)
            for u in range(t + 1, block):
                columns[u] = columns[u] - scale * columns[u][j : j + 1]
            work = work - scale * work[j : j + 1]
    diag = jnp.sum(jnp.where(lanes == rows, work, 0.0), axis=1, keepdims=True)
    work = work * lax.rsqrt(diag)
    return work[:, n : 2 * n]


def kernel(
    dims, chunks, g_hbm, e_hbm, q_hbm, out_hbm, qnew_hbm,
    g_v, e_v, q_v, m2, mf, mx, q_all, pbuf, gbuf, w_c, w_r, r_buf, z_r, z_full, y_all, out_v, qn_v,
    in_sem, q_s, q_r, p_s, p_r, g_s, g_r, m_s, m_r, w_s, w_rs, zr_s, zr_r, za_s, za_r,
    y_s, y_r, yc_s, yc_r, out_sem, qn_sem,
):
    n_dp, n_sh, side, nz, zrows, split_z, aligned, width = dims
    spans = [pl.ds(lo, hi - lo) for lo, hi in chunks]
    n_ch = len(chunks)
    rank = q_hbm.shape[0]
    pieces = 2 * n_sh
    d = lax.axis_index("dp")
    s = lax.axis_index("shard")
    z = lax.div(d, 2)
    c = lax.rem(d, 2)
    oc = 1 - c
    sib = d + 1 - 2 * c

    def ring(at, count):
        places = [at]
        for _ in range(count - 1):
            step = places[-1] + 1
            places.append(jnp.where(step == count, 0, step))
        return places

    dp_at = ring(d, n_dp)
    z_at = ring(z, nz)
    rows_at = ring(lax.div(s, side), side)
    cols_at = ring(lax.rem(s, side), side)
    in_rows = [rows_at[i // side] * side + cols_at[i % side] for i in range(n_sh)]
    in_cols = [rows_at[i % side] * side + cols_at[i // side] for i in range(n_sh)]
    mine_at = [jnp.where(c == 0, a, b) for a, b in zip(in_rows, in_cols)]
    theirs_at = [jnp.where(c == 0, b, a) for a, b in zip(in_rows, in_cols)]

    def at_dp(i):
        return dp_at[i]

    def at_sh(i, core=None):
        return mine_at[i] if core is None else theirs_at[i]

    def at_z(i):
        return z_at[i]

    barrier = pltpu.get_barrier_semaphore()
    for i in range(1, n_dp):
        pl.semaphore_signal(barrier, inc=1, device_id=(at_dp(i), s), device_id_type=MESH)
    for i in range(1, n_sh):
        pl.semaphore_signal(barrier, inc=1, device_id=(d, at_sh(i)), device_id_type=MESH)

    load_g = pltpu.make_async_copy(g_hbm.at[0], g_v, in_sem.at[0])
    load_e = pltpu.make_async_copy(e_hbm.at[0], e_v, in_sem.at[1])
    q_loads = []
    if aligned:
        for h in range(2):
            half_copy = pltpu.make_async_copy(
                q_hbm.at[:, h * width : (h + 1) * width], q_all.at[2 * s + h], in_sem.at[2 + h]
            )
            half_copy.start()
            q_loads.append(half_copy)
    else:
        whole_copy = pltpu.make_async_copy(q_hbm, q_v, in_sem.at[2])
        whole_copy.start()
        q_loads.append(whole_copy)
    load_g.start()
    load_e.start()

    for q_load in q_loads:
        q_load.wait()
    if not aligned:
        for h in range(2):
            q_all[2 * s + h] = q_v[:, h * width : (h + 1) * width]
    pl.semaphore_wait(barrier, n_dp - 1 + n_sh - 1)

    def remote(src, dst, send, recv, target):
        return pltpu.make_async_remote_copy(
            src_ref=src, dst_ref=dst, send_sem=send, recv_sem=recv, device_id=target, device_id_type=MESH
        )

    sends = []

    def send(src, dst, send_sem, recv_sem, target):
        copy = remote(src, dst, send_sem, recv_sem, target)
        copy.start()
        sends.append(copy)

    def arrived(dst, send_sem, recv_sem):
        remote(dst, dst, send_sem, recv_sem, (sib, s)).wait_recv()

    mine = 2 * s + c
    other = 2 * s + oc
    for i in range(1, n_sh):
        send(q_all.at[mine], q_all.at[mine], q_s.at[i], q_r.at[s], (d, at_sh(i)))

    load_g.wait()
    load_e.wait()
    for k in range(pieces):
        cols = slice(k * width, (k + 1) * width)
        mf[k] = g_v[:, cols].astype(F32) + e_v[:, cols]

    swaps = []
    for i in range(n_sh):
        o = at_sh(i, oc)
        swap = remote(mf.at[2 * o + oc], mx.at[o], m_s.at[i], m_r.at[o], (sib, s))
        swap.start()
        swaps.append(swap)
    n_rows = mf.shape[1]
    acc = None
    for i in range(n_sh):
        o = at_sh(i)
        arrived(mx.at[o], m_s.at[i], m_r.at[o])
        hi, lo = halves(mf[2 * o + c] + mx[o])
        m2[o, :n_rows] = hi
        m2[o, n_rows:] = lo
        if i > 0:
            arrived(q_all.at[2 * o + c], q_s.at[i], q_r.at[o])
        hi, lo = halves(q_all[2 * o + c])
        term = dot(jnp.concatenate([hi, lo], axis=0), m2[o], NT)
        acc = term if acc is None else acc + term
    acc = acc[:rank] + acc[rank:]
    part = acc[:, :n_rows] + acc[:, n_rows:]
    half = rank // 2

    pbuf[d] = jnp.concatenate([part[:half], part[half:]], axis=1)
    for i in range(1, n_dp):
        send(pbuf.at[d], pbuf.at[d], p_s.at[i], p_r.at[d], (at_dp(i), s))
    for i in range(1, n_dp):
        o = at_dp(i)
        arrived(pbuf.at[o], p_s.at[i], p_r.at[o])
    total = pbuf[0]
    for k in range(1, n_dp):
        total = total + pbuf[k]
    total = total * (1.0 / n_dp)
    pt = jnp.concatenate([total[:, :n_rows], total[:, n_rows:]], axis=0)

    twice = jnp.concatenate([pt, pt], axis=1) * (1.0 / n_dp)
    p_hi, p_lo = halves(twice)
    p2 = jnp.concatenate([p_hi, p_lo], axis=0)

    def w_term(o, span):
        t = dot(p2, m2[o, :, span])
        return t[:rank] + t[rank:]

    for ch, span in enumerate(spans):
        for i in range(1, n_sh):
            o = at_sh(i)
            w_c[o, :, span] = w_term(o, span)
            send(w_c.at[o, :, span], w_r.at[s, :, span], w_s.at[ch, i], w_rs.at[ch, s], (d, o))
            if ch == 0 and i == 1:
                padded = jnp.concatenate([pt, jnp.zeros((128 - rank, n_rows), F32)], axis=0)
                gbuf[s] = dot(pt, padded, NT, HIGH)
                for j in range(1, n_sh):
                    send(gbuf.at[s], gbuf.at[s], g_s.at[j], g_r.at[s], (d, at_sh(j)))
    for span in spans:
        w_r[s, :, span] = w_term(s, span)
    for swap in swaps:
        swap.wait_send()

    for i in range(1, n_sh):
        o = at_sh(i)
        arrived(gbuf.at[o], g_s.at[i], g_r.at[o])
    gram = gbuf[0]
    for k in range(1, n_sh):
        gram = gram + gbuf[k]
    linv = inverse_factor(gram)
    p_hat_t = dot(linv, pt, NN, HIGH)
    three = jnp.concatenate([p_hat_t, p_hat_t, p_hat_t], axis=0)
    rounded = three.astype(BF16).astype(F32)
    row = lax.broadcasted_iota(jnp.int32, three.shape, 0)
    ph3 = jnp.where(row < 2 * rank, rounded, three - rounded).T.astype(BF16)

    l3 = jnp.concatenate([linv, linv, linv], axis=1)
    l_rounded = l3.astype(BF16).astype(F32)
    lane = lax.broadcasted_iota(jnp.int32, l3.shape, 1)
    l3 = jnp.where(lane < 2 * rank, l_rounded, l3 - l_rounded).astype(BF16)

    def over_shards(ch, span):
        for i in range(1, n_sh):
            o = at_sh(i)
            arrived(w_r.at[o, :, span], w_s.at[ch, i], w_rs.at[ch, o])
        r = w_r[0, :, span]
        for k in range(1, n_sh):
            r = r + w_r[k, :, span]
        if split_z:
            for k in range(nz):
                r_buf[k, :, span] = r[k * zrows : (k + 1) * zrows]
            z_r[z, :, span] = r_buf[z, :, span]
        else:
            z_r[z, :, span] = r
        for i in range(1, nz):
            o = at_z(i)
            src = r_buf.at[o, :, span] if split_z else z_r.at[z, :, span]
            send(src, z_r.at[z, :, span], zr_s.at[ch, i], zr_r.at[ch, z], (2 * o + c, s))

    def over_z(ch, span):
        for i in range(1, nz):
            o = at_z(i)
            arrived(z_r.at[o, :, span], zr_s.at[ch, i], zr_r.at[ch, o])
        r = z_r[0, :, span]
        for k in range(1, nz):
            r = r + z_r[k, :, span]
        if split_z:
            z_full[z, :, span] = r
            part = z_full.at[z, :, span]
            for i in range(1, nz):
                send(part, part, za_s.at[ch, i], za_r.at[ch, z], (2 * at_z(i) + c, s))
        else:
            z_full[0, :, span] = r

    def share_out(ch, span):
        r = z_full[0, :, span]
        if split_z:
            for i in range(1, nz):
                o = at_z(i)
                arrived(z_full.at[o, :, span], za_s.at[ch, i], za_r.at[ch, o])
            r = jnp.concatenate([z_full[k, :, span] for k in range(nz)], axis=0)
        hi, lo = halves(r)
        y_all[mine, :, span] = dot(l3, jnp.concatenate([hi, lo, hi], axis=0))
        part = y_all.at[mine, :, span]
        for i in range(1, n_sh):
            send(part, part, y_s.at[ch, i], y_r.at[ch, s], (d, at_sh(i)))
        send(part, part, yc_s.at[ch, 0], yc_r.at[ch, s], (sib, s))

    for step in range(n_ch + 2):
        if step < n_ch:
            over_shards(step, spans[step])
        if 0 <= step - 1 < n_ch:
            over_z(step - 1, spans[step - 1])
        if 0 <= step - 2 < n_ch:
            share_out(step - 2, spans[step - 2])

    stores = []

    def finish(k, ch):
        lo_lane, hi_lane = chunks[ch]
        hi, lo = halves(y_all[k, :, spans[ch]])
        mf[k, :, spans[ch]] = mf[k, :, spans[ch]] - dot(ph3, jnp.concatenate([hi, lo, hi], axis=0))
        if aligned:
            columns = pl.ds(pl.multiple_of(k * width + lo_lane, 128), hi_lane - lo_lane)
            copy = pltpu.make_async_copy(
                mf.at[k, :, spans[ch]], out_hbm.at[0, :, columns], out_sem.at[len(stores)]
            )
            copy.start()
            stores.append(copy)

    for ch, span in enumerate(spans):
        finish(mine, ch)
        arrived(y_all.at[other, :, span], yc_s.at[ch, 0], yc_r.at[ch, s])
        finish(other, ch)
    late = []
    for h in range(2):
        if aligned:
            target = qnew_hbm.at[:, h * width : (h + 1) * width]
            copy = pltpu.make_async_copy(y_all.at[2 * s + h], target, qn_sem.at[h])
            copy.start()
            late.append(copy)
        else:
            qn_v[:, h * width : (h + 1) * width] = y_all[2 * s + h]
    for ch, span in enumerate(spans):
        for i in range(1, n_sh):
            o = at_sh(i)
            part = y_all.at[2 * o + c, :, span]
            arrived(part, y_s.at[ch, i], y_r.at[ch, o])
            send(part, part, yc_s.at[ch, i], yc_r.at[ch, o], (sib, s))
        for i in range(1, n_sh):
            finish(2 * at_sh(i) + c, ch)
        for i in range(1, n_sh):
            o = at_sh(i, oc)
            arrived(y_all.at[2 * o + oc, :, span], yc_s.at[ch, i], yc_r.at[ch, o])
            finish(2 * o + oc, ch)
    if not aligned:
        for k in range(pieces):
            out_v[:, k * width : (k + 1) * width] = mf[k]
        for src, dst, sem in ((out_v, out_hbm.at[0], out_sem.at[0]), (qn_v, qnew_hbm, qn_sem.at[0])):
            copy = pltpu.make_async_copy(src, dst, sem)
            copy.start()
            late.append(copy)
    for copy in sends:
        copy.wait_send()
    for copy in stores + late:
        copy.wait()


def place(out_from, q_from, out_to, q_to, out_v, q_v, in_sems, out_sems):
    n_rows = out_from.shape[1]
    step = n_rows // PLACE_PARTS
    pairs = [(q_from, q_v, q_to)]
    for i in range(PLACE_PARTS):
        rows = pl.ds(i * step, step)
        pairs.append((out_from.at[0, rows], out_v.at[rows], out_to.at[0, rows]))
    loads = [pltpu.make_async_copy(src, mid, in_sems.at[i]) for i, (src, mid, _) in enumerate(pairs)]
    stores = [pltpu.make_async_copy(mid, dst, out_sems.at[i]) for i, (_, mid, dst) in enumerate(pairs)]
    for load in loads:
        load.start()
    for load, store in zip(loads, stores):
        load.wait()
        store.start()
    for store in stores:
        store.wait()


def per_device(n_dp, n_sh, grads, errors, q_prev):
    _, n_rows, full = grads.shape
    share, rank = q_prev.shape
    width = share // 2
    nz = n_dp // 2
    split_z = rank % (8 * nz) == 0
    zrows = rank // nz if split_z else rank
    aligned = width % 128 == 0
    pieces = 2 * n_sh
    dims = (n_dp, n_sh, math.isqrt(n_sh), nz, zrows, split_z, aligned, width)
    chunks = ((0, width),)
    if aligned and width >= N_CHUNKS * 128:
        tiles = width // 128
        edges = [-(-tiles * i // N_CHUNKS) * 128 for i in range(N_CHUNKS + 1)]
        chunks = tuple(zip(edges[:-1], edges[1:]))
    vm = pltpu.VMEM
    dma = pltpu.SemaphoreType.DMA
    small = (8, 128)
    scratch = [
        vm((n_rows, full), BF16),
        vm((n_rows, full), F32),
        vm(small if aligned else (rank, share), F32),
        vm((n_sh, 2 * n_rows, width), BF16),
        vm((pieces, n_rows, width), F32),
        vm((n_sh, n_rows, width), F32),
        vm((pieces, rank, width), F32),
        vm((n_dp, rank // 2, 2 * n_rows), F32),
        vm((n_sh, rank, 128), F32),
        vm((n_sh, rank, width), F32),
        vm((n_sh, rank, width), F32),
        vm((nz, zrows, width) if split_z else small, F32),
        vm((nz, zrows, width), F32),
        vm((nz, zrows, width) if split_z else (1, rank, width), F32),
        vm((pieces, rank, width), F32),
        vm(small if aligned else (n_rows, full), F32),
        vm(small if aligned else (rank, share), F32),
        dma((4,)),
    ]
    n_ch = len(chunks)
    per_chunk = [(n_sh,), (n_dp,), (n_sh,), (n_sh,), (n_ch, n_sh)] + [(n_ch, nz)] * 2 + [(n_ch, n_sh)] * 2
    for shape in per_chunk:
        scratch += [dma(shape), dma(shape)]
    scratch += [dma((n_ch * pieces,)), dma((2,))]
    shapes = (
        jax.ShapeDtypeStruct((1, n_rows, full), F32),
        jax.ShapeDtypeStruct((rank, share), F32),
    )
    hbm = pl.BlockSpec(memory_space=pl.ANY)
    out, q_new = pl.pallas_call(
        functools.partial(kernel, dims, chunks),
        out_shape=shapes,
        in_specs=[hbm, hbm, hbm],
        out_specs=(hbm, hbm),
        scratch_shapes=scratch,
        compiler_params=pltpu.CompilerParams(
            collective_id=0, has_side_effects=True, vmem_limit_bytes=62 * 1024 * 1024
        ),
        cost_estimate=pl.CostEstimate(
            flops=18 * n_rows * full * rank, bytes_accessed=10 * n_rows * full, transcendentals=0
        ),
    )(grads, errors, q_prev.T)
    out, q_new = pl.pallas_call(
        place,
        out_shape=shapes,
        in_specs=[hbm, hbm],
        out_specs=(hbm, hbm),
        scratch_shapes=[
            vm((n_rows, full), F32), vm((rank, share), F32), dma((PLACE_PARTS + 1,)), dma((PLACE_PARTS + 1,)),
        ],
        compiler_params=pltpu.CompilerParams(vmem_limit_bytes=62 * 1024 * 1024),
    )(out, q_new)
    return out, q_new.T


def solution(mesh):
    in_specs = (P("dp", "shard", None), P("dp", "shard", None), P("shard", None))
    out_specs = (P("dp", "shard", None), P("shard", None))
    return jax.shard_map(
        functools.partial(per_device, mesh.shape["dp"], mesh.shape["shard"]),
        mesh=mesh, in_specs=in_specs, out_specs=out_specs, check_vma=False,
    )
```

```python
import functools
import math

import jax
import jax.numpy as jnp
from jax import lax
from jax.experimental import pallas as pl
from jax.experimental.pallas import tpu as pltpu
from jax.sharding import PartitionSpec as P

MESH = pl.DeviceIdType.MESH
HIGH = lax.Precision.HIGHEST
F32 = jnp.float32
BF16 = jnp.bfloat16
NT = (((1,), (1,)), ((), ()))
NN = (((1,), (0,)), ((), ()))
N_CHUNKS = 2
PLACE_PARTS = 4


def dot(a, b, dims=NN, precision=None):
    return lax.dot_general(a, b, dims, precision=precision, preferred_element_type=F32)


def halves(x):
    hi = x.astype(BF16)
    return hi, (x - hi.astype(F32)).astype(BF16)


def inverse_factor(gram):
    n = gram.shape[0]
    rows = lax.broadcasted_iota(jnp.int32, (n, 128), 0)
    lanes = lax.broadcasted_iota(jnp.int32, (n, 128), 1)
    work = jnp.where(lanes == rows + n, 1.0, gram)
    block = 8
    for first in range(0, n, block):
        columns = [jnp.broadcast_to(work[:, first + t : first + t + 1], (n, 128)) for t in range(block)]
        for t in range(block):
            j = first + t
            scale = jnp.where(rows > j, columns[t] * (1.0 / columns[t][j : j + 1]), 0.0)
            for u in range(t + 1, block):
                columns[u] = columns[u] - scale * columns[u][j : j + 1]
            work = work - scale * work[j : j + 1]
    diag = jnp.sum(jnp.where(lanes == rows, work, 0.0), axis=1, keepdims=True)
    work = work * lax.rsqrt(diag)
    return work[:, n : 2 * n]


def kernel(
    dims, chunks, g_hbm, e_hbm, q_hbm, out_hbm, qnew_hbm,
    g_v, e_v, q_v, m2, mf, mx, q_all, pbuf, gbuf, w_c, w_r, r_buf, z_r, z_full, y_all, out_v, qn_v,
    in_sem, q_s, q_r, p_s, p_r, g_s, g_r, m_s, m_r, w_s, w_rs, zr_s, zr_r, za_s, za_r,
    y_s, y_r, yc_s, yc_r, out_sem, qn_sem,
):
    n_dp, n_sh, side, nz, zrows, split_z, aligned, width = dims
    spans = [pl.ds(lo, hi - lo) for lo, hi in chunks]
    n_ch = len(chunks)
    rank = q_hbm.shape[0]
    pieces = 2 * n_sh
    d = lax.axis_index("dp")
    s = lax.axis_index("shard")
    z = lax.div(d, 2)
    c = lax.rem(d, 2)
    oc = 1 - c
    sib = d + 1 - 2 * c

    def ring(at, count):
        places = [at]
        for _ in range(count - 1):
            step = places[-1] + 1
            places.append(jnp.where(step == count, 0, step))
        return places

    dp_at = ring(d, n_dp)
    z_at = ring(z, nz)
    rows_at = ring(lax.div(s, side), side)
    cols_at = ring(lax.rem(s, side), side)
    in_rows = [rows_at[i // side] * side + cols_at[i % side] for i in range(n_sh)]
    in_cols = [rows_at[i % side] * side + cols_at[i // side] for i in range(n_sh)]
    mine_at = [jnp.where(c == 0, a, b) for a, b in zip(in_rows, in_cols)]
    theirs_at = [jnp.where(c == 0, b, a) for a, b in zip(in_rows, in_cols)]

    def at_dp(i):
        return dp_at[i]

    def at_sh(i, core=None):
        return mine_at[i] if core is None else theirs_at[i]

    def at_z(i):
        return z_at[i]

    barrier = pltpu.get_barrier_semaphore()
    for i in range(1, n_dp):
        pl.semaphore_signal(barrier, inc=1, device_id=(at_dp(i), s), device_id_type=MESH)
    for i in range(1, n_sh):
        pl.semaphore_signal(barrier, inc=1, device_id=(d, at_sh(i)), device_id_type=MESH)

    load_g = pltpu.make_async_copy(g_hbm.at[0], g_v, in_sem.at[0])
    load_e = pltpu.make_async_copy(e_hbm.at[0], e_v, in_sem.at[1])
    q_loads = []
    if aligned:
        for h in range(2):
            half_copy = pltpu.make_async_copy(
                q_hbm.at[:, h * width : (h + 1) * width], q_all.at[2 * s + h], in_sem.at[2 + h]
            )
            half_copy.start()
            q_loads.append(half_copy)
    else:
        whole_copy = pltpu.make_async_copy(q_hbm, q_v, in_sem.at[2])
        whole_copy.start()
        q_loads.append(whole_copy)
    load_g.start()
    load_e.start()

    for q_load in q_loads:
        q_load.wait()
    if not aligned:
        for h in range(2):
            q_all[2 * s + h] = q_v[:, h * width : (h + 1) * width]
    pl.semaphore_wait(barrier, n_dp - 1 + n_sh - 1)

    def remote(src, dst, send, recv, target):
        return pltpu.make_async_remote_copy(
            src_ref=src, dst_ref=dst, send_sem=send, recv_sem=recv, device_id=target, device_id_type=MESH
        )

    sends = []
    stores = []

    def lanes(start, ch):
        first, last = chunks[ch]
        return pl.ds(pl.multiple_of(start + first, 128), last - first)

    def send(src, dst, send_sem, recv_sem, target):
        copy = remote(src, dst, send_sem, recv_sem, target)
        copy.start()
        sends.append(copy)

    def arrived(dst, send_sem, recv_sem):
        remote(dst, dst, send_sem, recv_sem, (sib, s)).wait_recv()

    mine = 2 * s + c
    other = 2 * s + oc
    for i in range(1, n_sh):
        send(q_all.at[mine], q_all.at[mine], q_s.at[i], q_r.at[s], (d, at_sh(i)))

    load_g.wait()
    load_e.wait()
    for k in range(pieces):
        cols = slice(k * width, (k + 1) * width)
        mf[k] = g_v[:, cols].astype(F32) + e_v[:, cols]

    swaps = []
    for i in range(n_sh):
        o = at_sh(i, oc)
        swap = remote(mf.at[2 * o + oc], mx.at[o], m_s.at[i], m_r.at[o], (sib, s))
        swap.start()
        swaps.append(swap)
    n_rows = mf.shape[1]
    acc = None
    for i in range(n_sh):
        o = at_sh(i)
        arrived(mx.at[o], m_s.at[i], m_r.at[o])
        hi, lo = halves(mf[2 * o + c] + mx[o])
        m2[o, :n_rows] = hi
        m2[o, n_rows:] = lo
        if i > 0:
            arrived(q_all.at[2 * o + c], q_s.at[i], q_r.at[o])
        hi, lo = halves(q_all[2 * o + c])
        term = dot(jnp.concatenate([hi, lo], axis=0), m2[o], NT)
        acc = term if acc is None else acc + term
    acc = acc[:rank] + acc[rank:]
    part = acc[:, :n_rows] + acc[:, n_rows:]
    half = rank // 2

    pbuf[d] = jnp.concatenate([part[:half], part[half:]], axis=1)
    for i in range(1, n_dp):
        send(pbuf.at[d], pbuf.at[d], p_s.at[i], p_r.at[d], (at_dp(i), s))
    for i in range(1, n_dp):
        o = at_dp(i)
        arrived(pbuf.at[o], p_s.at[i], p_r.at[o])
    total = pbuf[0]
    for k in range(1, n_dp):
        total = total + pbuf[k]
    total = total * (1.0 / n_dp)
    pt = jnp.concatenate([total[:, :n_rows], total[:, n_rows:]], axis=0)

    twice = jnp.concatenate([pt, pt], axis=1) * (1.0 / n_dp)
    p_hi, p_lo = halves(twice)
    p2 = jnp.concatenate([p_hi, p_lo], axis=0)

    def w_term(o, span):
        t = dot(p2, m2[o, :, span])
        return t[:rank] + t[rank:]

    for ch, span in enumerate(spans):
        for i in range(1, n_sh):
            o = at_sh(i)
            w_c[o, :, span] = w_term(o, span)
            send(w_c.at[o, :, span], w_r.at[s, :, span], w_s.at[ch, i], w_rs.at[ch, s], (d, o))
            if ch == 0 and i == 1:
                padded = jnp.concatenate([pt, jnp.zeros((128 - rank, n_rows), F32)], axis=0)
                gbuf[s] = dot(pt, padded, NT, HIGH)
                for j in range(1, n_sh):
                    send(gbuf.at[s], gbuf.at[s], g_s.at[j], g_r.at[s], (d, at_sh(j)))
    for span in spans:
        w_r[s, :, span] = w_term(s, span)
    for swap in swaps:
        swap.wait_send()

    for i in range(1, n_sh):
        o = at_sh(i)
        arrived(gbuf.at[o], g_s.at[i], g_r.at[o])
    gram = gbuf[0]
    for k in range(1, n_sh):
        gram = gram + gbuf[k]
    linv = inverse_factor(gram)
    p_hat_t = dot(linv, pt, NN, HIGH)
    three = jnp.concatenate([p_hat_t, p_hat_t, p_hat_t], axis=0)
    rounded = three.astype(BF16).astype(F32)
    row = lax.broadcasted_iota(jnp.int32, three.shape, 0)
    ph3 = jnp.where(row < 2 * rank, rounded, three - rounded).T.astype(BF16)

    l3 = jnp.concatenate([linv, linv, linv], axis=1)
    l_rounded = l3.astype(BF16).astype(F32)
    lane = lax.broadcasted_iota(jnp.int32, l3.shape, 1)
    l3 = jnp.where(lane < 2 * rank, l_rounded, l3 - l_rounded).astype(BF16)

    def over_shards(ch, span):
        for i in range(1, n_sh):
            o = at_sh(i)
            arrived(w_r.at[o, :, span], w_s.at[ch, i], w_rs.at[ch, o])
        r = w_r[0, :, span]
        for k in range(1, n_sh):
            r = r + w_r[k, :, span]
        if split_z:
            for k in range(nz):
                r_buf[k, :, span] = r[k * zrows : (k + 1) * zrows]
            z_r[z, :, span] = r_buf[z, :, span]
        else:
            z_r[z, :, span] = r
        for i in range(1, nz):
            o = at_z(i)
            src = r_buf.at[o, :, span] if split_z else z_r.at[z, :, span]
            send(src, z_r.at[z, :, span], zr_s.at[ch, i], zr_r.at[ch, z], (2 * o + c, s))

    def over_z(ch, span):
        for i in range(1, nz):
            o = at_z(i)
            arrived(z_r.at[o, :, span], zr_s.at[ch, i], zr_r.at[ch, o])
        r = z_r[0, :, span]
        for k in range(1, nz):
            r = r + z_r[k, :, span]
        if split_z:
            z_full[z, :, span] = r
            part = z_full.at[z, :, span]
            for i in range(1, nz):
                send(part, part, za_s.at[ch, i], za_r.at[ch, z], (2 * at_z(i) + c, s))
        else:
            z_full[0, :, span] = r

    def share_out(ch, span):
        r = z_full[0, :, span]
        if split_z:
            for i in range(1, nz):
                o = at_z(i)
                arrived(z_full.at[o, :, span], za_s.at[ch, i], za_r.at[ch, o])
            r = jnp.concatenate([z_full[k, :, span] for k in range(nz)], axis=0)
        hi, lo = halves(r)
        y_all[mine, :, span] = dot(l3, jnp.concatenate([hi, lo, hi], axis=0))
        part = y_all.at[mine, :, span]
        for i in range(1, n_sh):
            send(part, part, y_s.at[ch, i], y_r.at[ch, s], (d, at_sh(i)))
        if aligned:
            target = qnew_hbm.at[:, lanes(c * width, ch)]
            send(part, target, yc_s.at[ch, n_sh], yc_r.at[ch, n_sh], (sib, s))
            copy = pltpu.make_async_copy(part, target, qn_sem.at[ch])
            copy.start()
            stores.append(copy)
        else:
            send(part, part, yc_s.at[ch, n_sh], yc_r.at[ch, n_sh], (sib, s))

    for step in range(n_ch + 2):
        if step < n_ch:
            over_shards(step, spans[step])
        if 0 <= step - 1 < n_ch:
            over_z(step - 1, spans[step - 1])
        if 0 <= step - 2 < n_ch:
            share_out(step - 2, spans[step - 2])

    def finish(i, ch):
        o = at_sh(i)
        k = 2 * o + c
        span = spans[ch]
        hi, lo = halves(y_all[k, :, span])
        product = dot(ph3, jnp.concatenate([hi, lo, hi], axis=0))
        mx[o, :, span] = mx[o, :, span] - product
        theirs = out_hbm.at[0, :, lanes(k * width, ch)] if aligned else mf.at[k, :, span]
        send(mx.at[o, :, span], theirs, yc_s.at[ch, i], yc_r.at[ch, o], (sib, s))
        mf[k, :, span] = mf[k, :, span] - product
        if aligned:
            copy = pltpu.make_async_copy(mf.at[k, :, span], theirs, out_sem.at[ch, i])
            copy.start()
            stores.append(copy)

    for ch in range(n_ch):
        finish(0, ch)
    for ch, span in enumerate(spans):
        for i in range(1, n_sh):
            o = at_sh(i)
            arrived(y_all.at[2 * o + c, :, span], y_s.at[ch, i], y_r.at[ch, o])
            finish(i, ch)
    for ch, span in enumerate(spans):
        q_part = qnew_hbm.at[:, lanes(oc * width, ch)] if aligned else y_all.at[other, :, span]
        arrived(q_part, yc_s.at[ch, n_sh], yc_r.at[ch, n_sh])
        for i in range(n_sh):
            o = at_sh(i, oc)
            k = 2 * o + oc
            part = out_hbm.at[0, :, lanes(k * width, ch)] if aligned else mf.at[k, :, span]
            arrived(part, yc_s.at[ch, i], yc_r.at[ch, o])
    late = []
    if not aligned:
        for h in range(2):
            qn_v[:, h * width : (h + 1) * width] = y_all[2 * s + h]
    if not aligned:
        for k in range(pieces):
            out_v[:, k * width : (k + 1) * width] = mf[k]
        for src, dst, sem in ((out_v, out_hbm.at[0], out_sem.at[0, 0]), (qn_v, qnew_hbm, qn_sem.at[0])):
            copy = pltpu.make_async_copy(src, dst, sem)
            copy.start()
            late.append(copy)
    for copy in sends:
        copy.wait_send()
    for copy in stores + late:
        copy.wait()


def place(out_from, q_from, out_to, q_to, out_v, q_v, in_sems, out_sems):
    n_rows = out_from.shape[1]
    step = n_rows // PLACE_PARTS
    pairs = [(q_from, q_v, q_to)]
    for i in range(PLACE_PARTS):
        rows = pl.ds(i * step, step)
        pairs.append((out_from.at[0, rows], out_v.at[rows], out_to.at[0, rows]))
    loads = [pltpu.make_async_copy(src, mid, in_sems.at[i]) for i, (src, mid, _) in enumerate(pairs)]
    stores = [pltpu.make_async_copy(mid, dst, out_sems.at[i]) for i, (_, mid, dst) in enumerate(pairs)]
    for load in loads:
        load.start()
    for load, store in zip(loads, stores):
        load.wait()
        store.start()
    for store in stores:
        store.wait()


def per_device(n_dp, n_sh, grads, errors, q_prev):
    _, n_rows, full = grads.shape
    share, rank = q_prev.shape
    width = share // 2
    nz = n_dp // 2
    split_z = rank % (8 * nz) == 0
    zrows = rank // nz if split_z else rank
    aligned = width % 128 == 0
    pieces = 2 * n_sh
    dims = (n_dp, n_sh, math.isqrt(n_sh), nz, zrows, split_z, aligned, width)
    chunks = ((0, width),)
    if aligned and width >= N_CHUNKS * 128:
        tiles = width // 128
        edges = [-(-tiles * i // N_CHUNKS) * 128 for i in range(N_CHUNKS + 1)]
        chunks = tuple(zip(edges[:-1], edges[1:]))
    vm = pltpu.VMEM
    dma = pltpu.SemaphoreType.DMA
    small = (8, 128)
    scratch = [
        vm((n_rows, full), BF16),
        vm((n_rows, full), F32),
        vm(small if aligned else (rank, share), F32),
        vm((n_sh, 2 * n_rows, width), BF16),
        vm((pieces, n_rows, width), F32),
        vm((n_sh, n_rows, width), F32),
        vm((pieces, rank, width), F32),
        vm((n_dp, rank // 2, 2 * n_rows), F32),
        vm((n_sh, rank, 128), F32),
        vm((n_sh, rank, width), F32),
        vm((n_sh, rank, width), F32),
        vm((nz, zrows, width) if split_z else small, F32),
        vm((nz, zrows, width), F32),
        vm((nz, zrows, width) if split_z else (1, rank, width), F32),
        vm((pieces, rank, width), F32),
        vm(small if aligned else (n_rows, full), F32),
        vm(small if aligned else (rank, share), F32),
        dma((4,)),
    ]
    n_ch = len(chunks)
    per_chunk = [(n_sh,), (n_dp,), (n_sh,), (n_sh,), (n_ch, n_sh)] + [(n_ch, nz)] * 2 + [(n_ch, n_sh)] * 2
    per_chunk[-1] = (n_ch, n_sh + 1)
    for shape in per_chunk:
        scratch += [dma(shape), dma(shape)]
    scratch += [dma((n_ch, n_sh)), dma((max(n_ch, 2),))]
    shapes = (
        jax.ShapeDtypeStruct((1, n_rows, full), F32),
        jax.ShapeDtypeStruct((rank, share), F32),
    )
    hbm = pl.BlockSpec(memory_space=pl.ANY)
    out, q_new = pl.pallas_call(
        functools.partial(kernel, dims, chunks),
        out_shape=shapes,
        in_specs=[hbm, hbm, hbm],
        out_specs=(hbm, hbm),
        scratch_shapes=scratch,
        compiler_params=pltpu.CompilerParams(
            collective_id=0, has_side_effects=True, vmem_limit_bytes=62 * 1024 * 1024
        ),
        cost_estimate=pl.CostEstimate(
            flops=18 * n_rows * full * rank, bytes_accessed=10 * n_rows * full, transcendentals=0
        ),
    )(grads, errors, q_prev.T)
    out, q_new = pl.pallas_call(
        place,
        out_shape=shapes,
        in_specs=[hbm, hbm],
        out_specs=(hbm, hbm),
        scratch_shapes=[
            vm((n_rows, full), F32), vm((rank, share), F32), dma((PLACE_PARTS + 1,)), dma((PLACE_PARTS + 1,)),
        ],
        compiler_params=pltpu.CompilerParams(vmem_limit_bytes=62 * 1024 * 1024),
    )(out, q_new)
    return out, q_new.T


def solution(mesh):
    in_specs = (P("dp", "shard", None), P("dp", "shard", None), P("shard", None))
    out_specs = (P("dp", "shard", None), P("shard", None))
    return jax.shard_map(
        functools.partial(per_device, mesh.shape["dp"], mesh.shape["shard"]),
        mesh=mesh, in_specs=in_specs, out_specs=out_specs, check_vma=False,
    )
```

```python
import functools
import math

import jax
import jax.numpy as jnp
from jax import lax
from jax.experimental import pallas as pl
from jax.experimental.pallas import tpu as pltpu
from jax.sharding import PartitionSpec as P

MESH = pl.DeviceIdType.MESH
HIGH = lax.Precision.HIGHEST
F32 = jnp.float32
BF16 = jnp.bfloat16
NT = (((1,), (1,)), ((), ()))
NN = (((1,), (0,)), ((), ()))
N_CHUNKS = 2
PLACE_PARTS = 4


def dot(a, b, dims=NN, precision=None):
    return lax.dot_general(a, b, dims, precision=precision, preferred_element_type=F32)


def halves(x):
    hi = x.astype(BF16)
    return hi, (x - hi.astype(F32)).astype(BF16)


def inverse_factor(gram):
    n = gram.shape[0]
    rows = lax.broadcasted_iota(jnp.int32, (n, 128), 0)
    lanes = lax.broadcasted_iota(jnp.int32, (n, 128), 1)
    work = jnp.where(lanes == rows + n, 1.0, gram)
    block = 8
    for first in range(0, n, block):
        columns = [jnp.broadcast_to(work[:, first + t : first + t + 1], (n, 128)) for t in range(block)]
        for t in range(block):
            j = first + t
            scale = jnp.where(rows > j, columns[t] * (1.0 / columns[t][j : j + 1]), 0.0)
            for u in range(t + 1, block):
                columns[u] = columns[u] - scale * columns[u][j : j + 1]
            work = work - scale * work[j : j + 1]
    diag = jnp.sum(jnp.where(lanes == rows, work, 0.0), axis=1, keepdims=True)
    work = work * lax.rsqrt(diag)
    return work[:, n : 2 * n]


def kernel(
    dims, chunks, g_hbm, e_hbm, q_hbm, out_hbm, qnew_hbm,
    g_v, e_v, q_v, m2, mf, mx, q_all, pbuf, gbuf, w_c, w_r, r_buf, z_r, z_full, y_all, out_v, qn_v,
    in_sem, q_s, q_r, p_s, p_r, g_s, g_r, m_s, m_r, w_s, w_rs, zr_s, zr_r, za_s, za_r,
    y_s, y_r, yc_s, yc_r, out_sem, qn_sem,
):
    n_dp, n_sh, side, nz, zrows, split_z, aligned, width = dims
    spans = [pl.ds(lo, hi - lo) for lo, hi in chunks]
    n_ch = len(chunks)
    rank = q_hbm.shape[0]
    pieces = 2 * n_sh
    d = lax.axis_index("dp")
    s = lax.axis_index("shard")
    z = lax.div(d, 2)
    c = lax.rem(d, 2)
    oc = 1 - c
    sib = d + 1 - 2 * c

    def ring(at, count):
        places = [at]
        for _ in range(count - 1):
            step = places[-1] + 1
            places.append(jnp.where(step == count, 0, step))
        return places

    dp_at = ring(d, n_dp)
    z_at = ring(z, nz)
    rows_at = ring(lax.div(s, side), side)
    cols_at = ring(lax.rem(s, side), side)
    in_rows = [rows_at[i // side] * side + cols_at[i % side] for i in range(n_sh)]
    in_cols = [rows_at[i % side] * side + cols_at[i // side] for i in range(n_sh)]
    mine_at = [jnp.where(c == 0, a, b) for a, b in zip(in_rows, in_cols)]
    theirs_at = [jnp.where(c == 0, b, a) for a, b in zip(in_rows, in_cols)]

    def at_dp(i):
        return dp_at[i]

    def at_sh(i, core=None):
        return mine_at[i] if core is None else theirs_at[i]

    def at_z(i):
        return z_at[i]

    barrier = pltpu.get_barrier_semaphore()
    for i in range(1, n_dp):
        pl.semaphore_signal(barrier, inc=1, device_id=(at_dp(i), s), device_id_type=MESH)
    for i in range(1, n_sh):
        pl.semaphore_signal(barrier, inc=1, device_id=(d, at_sh(i)), device_id_type=MESH)

    load_g = pltpu.make_async_copy(g_hbm.at[0], g_v, in_sem.at[0])
    load_e = pltpu.make_async_copy(e_hbm.at[0], e_v, in_sem.at[1])
    q_loads = []
    if aligned:
        for h in range(2):
            half_copy = pltpu.make_async_copy(
                q_hbm.at[:, h * width : (h + 1) * width], q_all.at[2 * s + h], in_sem.at[2 + h]
            )
            half_copy.start()
            q_loads.append(half_copy)
    else:
        whole_copy = pltpu.make_async_copy(q_hbm, q_v, in_sem.at[2])
        whole_copy.start()
        q_loads.append(whole_copy)
    load_g.start()
    load_e.start()

    for q_load in q_loads:
        q_load.wait()
    if not aligned:
        for h in range(2):
            q_all[2 * s + h] = q_v[:, h * width : (h + 1) * width]
    pl.semaphore_wait(barrier, n_dp - 1 + n_sh - 1)

    def remote(src, dst, send, recv, target):
        return pltpu.make_async_remote_copy(
            src_ref=src, dst_ref=dst, send_sem=send, recv_sem=recv, device_id=target, device_id_type=MESH
        )

    sends = []
    stores = []

    def lanes(start, ch):
        first, last = chunks[ch]
        return pl.ds(pl.multiple_of(start + first, 128), last - first)

    def send(src, dst, send_sem, recv_sem, target):
        copy = remote(src, dst, send_sem, recv_sem, target)
        copy.start()
        sends.append(copy)

    def arrived(dst, send_sem, recv_sem):
        remote(dst, dst, send_sem, recv_sem, (sib, s)).wait_recv()

    mine = 2 * s + c
    other = 2 * s + oc
    for i in range(1, n_sh):
        send(q_all.at[mine], q_all.at[mine], q_s.at[i], q_r.at[s], (d, at_sh(i)))

    load_g.wait()
    load_e.wait()
    n_rows = mf.shape[1]

    def merge(k):
        cols = pl.ds(pl.multiple_of(k * width, 128), width) if aligned else pl.ds(k * width, width)
        mf[k] = g_v[:, cols].astype(F32) + e_v[:, cols]

    if not aligned:
        for k in range(pieces):
            merge(k)

    swaps = []
    for i in range(n_sh):
        o = at_sh(i, oc)
        if aligned:
            merge(2 * o + oc)
        swap = remote(mf.at[2 * o + oc], mx.at[o], m_s.at[i], m_r.at[o], (sib, s))
        swap.start()
        swaps.append(swap)
    if aligned:
        for i in range(n_sh):
            merge(2 * at_sh(i) + c)
    acc = None
    for i in range(n_sh):
        o = at_sh(i)
        arrived(mx.at[o], m_s.at[i], m_r.at[o])
        hi, lo = halves(mf[2 * o + c] + mx[o])
        m2[o, :n_rows] = hi
        m2[o, n_rows:] = lo
        if i > 0:
            arrived(q_all.at[2 * o + c], q_s.at[i], q_r.at[o])
        hi, lo = halves(q_all[2 * o + c])
        term = dot(jnp.concatenate([hi, lo], axis=0), m2[o], NT)
        acc = term if acc is None else acc + term
    acc = acc[:rank] + acc[rank:]
    part = acc[:, :n_rows] + acc[:, n_rows:]
    half = rank // 2

    pbuf[d] = jnp.concatenate([part[:half], part[half:]], axis=1)
    for i in range(1, n_dp):
        send(pbuf.at[d], pbuf.at[d], p_s.at[i], p_r.at[d], (at_dp(i), s))
    for i in range(1, n_dp):
        o = at_dp(i)
        arrived(pbuf.at[o], p_s.at[i], p_r.at[o])
    total = pbuf[0]
    for k in range(1, n_dp):
        total = total + pbuf[k]
    total = total * (1.0 / n_dp)
    pt = jnp.concatenate([total[:, :n_rows], total[:, n_rows:]], axis=0)

    twice = jnp.concatenate([pt, pt], axis=1) * (1.0 / n_dp)
    p_hi, p_lo = halves(twice)
    p2 = jnp.concatenate([p_hi, p_lo], axis=0)

    def w_term(o, span):
        t = dot(p2, m2[o, :, span])
        return t[:rank] + t[rank:]

    for ch, span in enumerate(spans):
        for i in range(1, n_sh):
            o = at_sh(i)
            w_c[o, :, span] = w_term(o, span)
            send(w_c.at[o, :, span], w_r.at[s, :, span], w_s.at[ch, i], w_rs.at[ch, s], (d, o))
            if ch == 0 and i == 1:
                padded = jnp.concatenate([pt, jnp.zeros((128 - rank, n_rows), F32)], axis=0)
                gbuf[s] = dot(pt, padded, NT, HIGH)
                for j in range(1, n_sh):
                    send(gbuf.at[s], gbuf.at[s], g_s.at[j], g_r.at[s], (d, at_sh(j)))
    for span in spans:
        w_r[s, :, span] = w_term(s, span)
    for swap in swaps:
        swap.wait_send()

    def over_shards(ch, span):
        for i in range(1, n_sh):
            o = at_sh(i)
            arrived(w_r.at[o, :, span], w_s.at[ch, i], w_rs.at[ch, o])
        r = w_r[0, :, span]
        for k in range(1, n_sh):
            r = r + w_r[k, :, span]
        if split_z:
            for k in range(nz):
                r_buf[k, :, span] = r[k * zrows : (k + 1) * zrows]
            z_r[z, :, span] = r_buf[z, :, span]
        else:
            z_r[z, :, span] = r
        for i in range(1, nz):
            o = at_z(i)
            src = r_buf.at[o, :, span] if split_z else z_r.at[z, :, span]
            send(src, z_r.at[z, :, span], zr_s.at[ch, i], zr_r.at[ch, z], (2 * o + c, s))

    def over_z(ch, span):
        for i in range(1, nz):
            o = at_z(i)
            arrived(z_r.at[o, :, span], zr_s.at[ch, i], zr_r.at[ch, o])
        r = z_r[0, :, span]
        for k in range(1, nz):
            r = r + z_r[k, :, span]
        if split_z:
            z_full[z, :, span] = r
            part = z_full.at[z, :, span]
            for i in range(1, nz):
                send(part, part, za_s.at[ch, i], za_r.at[ch, z], (2 * at_z(i) + c, s))
        else:
            z_full[0, :, span] = r

    over_shards(0, spans[0])

    for i in range(1, n_sh):
        o = at_sh(i)
        arrived(gbuf.at[o], g_s.at[i], g_r.at[o])
    gram = gbuf[0]
    for k in range(1, n_sh):
        gram = gram + gbuf[k]
    linv = inverse_factor(gram)
    l3 = jnp.concatenate([linv, linv, linv], axis=1)
    l_rounded = l3.astype(BF16).astype(F32)
    lane = lax.broadcasted_iota(jnp.int32, l3.shape, 1)
    l3 = jnp.where(lane < 2 * rank, l_rounded, l3 - l_rounded).astype(BF16)

    def share_out(ch, span):
        r = z_full[0, :, span]
        if split_z:
            for i in range(1, nz):
                o = at_z(i)
                arrived(z_full.at[o, :, span], za_s.at[ch, i], za_r.at[ch, o])
            r = jnp.concatenate([z_full[k, :, span] for k in range(nz)], axis=0)
        hi, lo = halves(r)
        y_all[mine, :, span] = dot(l3, jnp.concatenate([hi, lo, hi], axis=0))
        part = y_all.at[mine, :, span]
        for i in range(1, n_sh):
            send(part, part, y_s.at[ch, i], y_r.at[ch, s], (d, at_sh(i)))
        if aligned:
            target = qnew_hbm.at[:, lanes(c * width, ch)]
            send(part, target, yc_s.at[ch, n_sh], yc_r.at[ch, n_sh], (sib, s))
            copy = pltpu.make_async_copy(part, target, qn_sem.at[ch])
            copy.start()
            stores.append(copy)
        else:
            send(part, part, yc_s.at[ch, n_sh], yc_r.at[ch, n_sh], (sib, s))

    for step in range(n_ch + 2):
        if 0 < step < n_ch:
            over_shards(step, spans[step])
        if 0 <= step - 1 < n_ch:
            over_z(step - 1, spans[step - 1])
        if 0 <= step - 2 < n_ch:
            share_out(step - 2, spans[step - 2])

    p_hat_t = dot(linv, pt, NN, HIGH)
    three = jnp.concatenate([p_hat_t, p_hat_t, p_hat_t], axis=0)
    rounded = three.astype(BF16).astype(F32)
    row = lax.broadcasted_iota(jnp.int32, three.shape, 0)
    ph3 = jnp.where(row < 2 * rank, rounded, three - rounded).T.astype(BF16)

    def finish(i, ch):
        o = at_sh(i)
        k = 2 * o + c
        span = spans[ch]
        hi, lo = halves(y_all[k, :, span])
        product = dot(ph3, jnp.concatenate([hi, lo, hi], axis=0))
        mx[o, :, span] = mx[o, :, span] - product
        theirs = out_hbm.at[0, :, lanes(k * width, ch)] if aligned else mf.at[k, :, span]
        send(mx.at[o, :, span], theirs, yc_s.at[ch, i], yc_r.at[ch, o], (sib, s))
        mf[k, :, span] = mf[k, :, span] - product
        if aligned:
            copy = pltpu.make_async_copy(mf.at[k, :, span], theirs, out_sem.at[ch, i])
            copy.start()
            stores.append(copy)

    for ch in range(n_ch):
        finish(0, ch)
    for ch, span in enumerate(spans):
        for i in range(1, n_sh):
            o = at_sh(i)
            arrived(y_all.at[2 * o + c, :, span], y_s.at[ch, i], y_r.at[ch, o])
            finish(i, ch)
    for ch, span in enumerate(spans):
        q_part = qnew_hbm.at[:, lanes(oc * width, ch)] if aligned else y_all.at[other, :, span]
        arrived(q_part, yc_s.at[ch, n_sh], yc_r.at[ch, n_sh])
        for i in range(n_sh):
            o = at_sh(i, oc)
            k = 2 * o + oc
            part = out_hbm.at[0, :, lanes(k * width, ch)] if aligned else mf.at[k, :, span]
            arrived(part, yc_s.at[ch, i], yc_r.at[ch, o])
    late = []
    if not aligned:
        for h in range(2):
            qn_v[:, h * width : (h + 1) * width] = y_all[2 * s + h]
    if not aligned:
        for k in range(pieces):
            out_v[:, k * width : (k + 1) * width] = mf[k]
        for src, dst, sem in ((out_v, out_hbm.at[0], out_sem.at[0, 0]), (qn_v, qnew_hbm, qn_sem.at[0])):
            copy = pltpu.make_async_copy(src, dst, sem)
            copy.start()
            late.append(copy)
    for copy in sends:
        copy.wait_send()
    for copy in stores + late:
        copy.wait()


def place(out_from, q_from, out_to, q_to, out_v, q_v, in_sems, out_sems):
    n_rows = out_from.shape[1]
    step = n_rows // PLACE_PARTS
    pairs = [(q_from, q_v, q_to)]
    for i in range(PLACE_PARTS):
        rows = pl.ds(i * step, step)
        pairs.append((out_from.at[0, rows], out_v.at[rows], out_to.at[0, rows]))
    loads = [pltpu.make_async_copy(src, mid, in_sems.at[i]) for i, (src, mid, _) in enumerate(pairs)]
    stores = [pltpu.make_async_copy(mid, dst, out_sems.at[i]) for i, (_, mid, dst) in enumerate(pairs)]
    for load in loads:
        load.start()
    for load, store in zip(loads, stores):
        load.wait()
        store.start()
    for store in stores:
        store.wait()


def per_device(n_dp, n_sh, grads, errors, q_prev):
    _, n_rows, full = grads.shape
    share, rank = q_prev.shape
    width = share // 2
    nz = n_dp // 2
    split_z = rank % (8 * nz) == 0
    zrows = rank // nz if split_z else rank
    aligned = width % 128 == 0
    pieces = 2 * n_sh
    dims = (n_dp, n_sh, math.isqrt(n_sh), nz, zrows, split_z, aligned, width)
    chunks = ((0, width),)
    if aligned and width >= N_CHUNKS * 128:
        tiles = width // 128
        edges = [-(-tiles * i // N_CHUNKS) * 128 for i in range(N_CHUNKS + 1)]
        chunks = tuple(zip(edges[:-1], edges[1:]))
    vm = pltpu.VMEM
    dma = pltpu.SemaphoreType.DMA
    small = (8, 128)
    scratch = [
        vm((n_rows, full), BF16),
        vm((n_rows, full), F32),
        vm(small if aligned else (rank, share), F32),
        vm((n_sh, 2 * n_rows, width), BF16),
        vm((pieces, n_rows, width), F32),
        vm((n_sh, n_rows, width), F32),
        vm((pieces, rank, width), F32),
        vm((n_dp, rank // 2, 2 * n_rows), F32),
        vm((n_sh, rank, 128), F32),
        vm((n_sh, rank, width), F32),
        vm((n_sh, rank, width), F32),
        vm((nz, zrows, width) if split_z else small, F32),
        vm((nz, zrows, width), F32),
        vm((nz, zrows, width) if split_z else (1, rank, width), F32),
        vm((pieces, rank, width), F32),
        vm(small if aligned else (n_rows, full), F32),
        vm(small if aligned else (rank, share), F32),
        dma((4,)),
    ]
    n_ch = len(chunks)
    per_chunk = [(n_sh,), (n_dp,), (n_sh,), (n_sh,), (n_ch, n_sh)] + [(n_ch, nz)] * 2 + [(n_ch, n_sh)] * 2
    per_chunk[-1] = (n_ch, n_sh + 1)
    for shape in per_chunk:
        scratch += [dma(shape), dma(shape)]
    scratch += [dma((n_ch, n_sh)), dma((max(n_ch, 2),))]
    shapes = (
        jax.ShapeDtypeStruct((1, n_rows, full), F32),
        jax.ShapeDtypeStruct((rank, share), F32),
    )
    hbm = pl.BlockSpec(memory_space=pl.ANY)
    out, q_new = pl.pallas_call(
        functools.partial(kernel, dims, chunks),
        out_shape=shapes,
        in_specs=[hbm, hbm, hbm],
        out_specs=(hbm, hbm),
        scratch_shapes=scratch,
        compiler_params=pltpu.CompilerParams(
            collective_id=0, has_side_effects=True, vmem_limit_bytes=62 * 1024 * 1024
        ),
        cost_estimate=pl.CostEstimate(
            flops=18 * n_rows * full * rank, bytes_accessed=10 * n_rows * full, transcendentals=0
        ),
    )(grads, errors, q_prev.T)
    out, q_new = pl.pallas_call(
        place,
        out_shape=shapes,
        in_specs=[hbm, hbm],
        out_specs=(hbm, hbm),
        scratch_shapes=[
            vm((n_rows, full), F32), vm((rank, share), F32), dma((PLACE_PARTS + 1,)), dma((PLACE_PARTS + 1,)),
        ],
        compiler_params=pltpu.CompilerParams(vmem_limit_bytes=62 * 1024 * 1024),
    )(out, q_new)
    return out, q_new.T


def solution(mesh):
    in_specs = (P("dp", "shard", None), P("dp", "shard", None), P("shard", None))
    out_specs = (P("dp", "shard", None), P("shard", None))
    return jax.shard_map(
        functools.partial(per_device, mesh.shape["dp"], mesh.shape["shard"]),
        mesh=mesh, in_specs=in_specs, out_specs=out_specs, check_vma=False,
    )
```

```python
import functools
import math

import jax
import jax.numpy as jnp
from jax import lax
from jax.experimental import pallas as pl
from jax.experimental.pallas import tpu as pltpu
from jax.sharding import PartitionSpec as P

MESH = pl.DeviceIdType.MESH
HIGH = lax.Precision.HIGHEST
F32 = jnp.float32
BF16 = jnp.bfloat16
NT = (((1,), (1,)), ((), ()))
NN = (((1,), (0,)), ((), ()))
N_CHUNKS = 2
PLACE_PARTS = 8


def dot(a, b, dims=NN, precision=None):
    return lax.dot_general(a, b, dims, precision=precision, preferred_element_type=F32)


def halves(x):
    hi = x.astype(BF16)
    return hi, (x - hi.astype(F32)).astype(BF16)


def inverse_factor(gram):
    n = gram.shape[0]
    rows = lax.broadcasted_iota(jnp.int32, (n, 128), 0)
    lanes = lax.broadcasted_iota(jnp.int32, (n, 128), 1)
    work = jnp.where(lanes == rows + n, 1.0, gram)
    block = 8
    for first in range(0, n, block):
        columns = [jnp.broadcast_to(work[:, first + t : first + t + 1], (n, 128)) for t in range(block)]
        for t in range(block):
            j = first + t
            scale = jnp.where(rows > j, columns[t] * (1.0 / columns[t][j : j + 1]), 0.0)
            for u in range(t + 1, block):
                columns[u] = columns[u] - scale * columns[u][j : j + 1]
            work = work - scale * work[j : j + 1]
    diag = jnp.sum(jnp.where(lanes == rows, work, 0.0), axis=1, keepdims=True)
    work = work * lax.rsqrt(diag)
    return work[:, n : 2 * n]


def kernel(
    dims, chunks, g_hbm, e_hbm, q_hbm, out_hbm, qnew_hbm,
    g_v, e_v, q_v, m2, mf, mx, q_all, pbuf, gbuf, w_c, w_r, r_buf, z_r, z_full, y_all, out_v, qn_v,
    in_sem, q_s, q_r, p_s, p_r, g_s, g_r, m_s, m_r, w_s, w_rs, zr_s, zr_r, za_s, za_r,
    y_s, y_r, yc_s, yc_r, out_sem, qn_sem,
):
    n_dp, n_sh, side, nz, zrows, split_z, aligned, width = dims
    spans = [pl.ds(lo, hi - lo) for lo, hi in chunks]
    n_ch = len(chunks)
    rank = q_hbm.shape[0]
    pieces = 2 * n_sh
    d = lax.axis_index("dp")
    s = lax.axis_index("shard")
    z = lax.div(d, 2)
    c = lax.rem(d, 2)
    oc = 1 - c
    sib = d + 1 - 2 * c

    def ring(at, count):
        places = [at]
        for _ in range(count - 1):
            step = places[-1] + 1
            places.append(jnp.where(step == count, 0, step))
        return places

    dp_at = ring(d, n_dp)
    z_at = ring(z, nz)
    rows_at = ring(lax.div(s, side), side)
    cols_at = ring(lax.rem(s, side), side)
    in_rows = [rows_at[i // side] * side + cols_at[i % side] for i in range(n_sh)]
    in_cols = [rows_at[i % side] * side + cols_at[i // side] for i in range(n_sh)]
    mine_at = [jnp.where(c == 0, a, b) for a, b in zip(in_rows, in_cols)]
    theirs_at = [jnp.where(c == 0, b, a) for a, b in zip(in_rows, in_cols)]

    def at_dp(i):
        return dp_at[i]

    def at_sh(i, core=None):
        return mine_at[i] if core is None else theirs_at[i]

    def at_z(i):
        return z_at[i]

    barrier = pltpu.get_barrier_semaphore()
    for i in range(1, n_dp):
        pl.semaphore_signal(barrier, inc=1, device_id=(at_dp(i), s), device_id_type=MESH)
    for i in range(1, n_sh):
        pl.semaphore_signal(barrier, inc=1, device_id=(d, at_sh(i)), device_id_type=MESH)

    load_g = pltpu.make_async_copy(g_hbm.at[0], g_v, in_sem.at[0])
    load_e = pltpu.make_async_copy(e_hbm.at[0], e_v, in_sem.at[1])
    q_loads = []
    if aligned:
        for h in range(2):
            half_copy = pltpu.make_async_copy(
                q_hbm.at[:, h * width : (h + 1) * width], q_all.at[2 * s + h], in_sem.at[2 + h]
            )
            half_copy.start()
            q_loads.append(half_copy)
    else:
        whole_copy = pltpu.make_async_copy(q_hbm, q_v, in_sem.at[2])
        whole_copy.start()
        q_loads.append(whole_copy)
    load_g.start()
    load_e.start()

    for q_load in q_loads:
        q_load.wait()
    if not aligned:
        for h in range(2):
            q_all[2 * s + h] = q_v[:, h * width : (h + 1) * width]
    pl.semaphore_wait(barrier, n_dp - 1 + n_sh - 1)

    def remote(src, dst, send, recv, target):
        return pltpu.make_async_remote_copy(
            src_ref=src, dst_ref=dst, send_sem=send, recv_sem=recv, device_id=target, device_id_type=MESH
        )

    sends = []
    last_sends = []
    stores = []

    def lanes(start, ch):
        first, last = chunks[ch]
        return pl.ds(pl.multiple_of(start + first, 128), last - first)

    def send(src, dst, send_sem, recv_sem, target, kept=sends):
        copy = remote(src, dst, send_sem, recv_sem, target)
        copy.start()
        kept.append(copy)

    def arrived(dst, send_sem, recv_sem):
        remote(dst, dst, send_sem, recv_sem, (sib, s)).wait_recv()

    mine = 2 * s + c
    other = 2 * s + oc
    for i in range(1, n_sh):
        send(q_all.at[mine], q_all.at[mine], q_s.at[i], q_r.at[s], (d, at_sh(i)))

    load_g.wait()
    load_e.wait()
    n_rows = mf.shape[1]

    def merge(k):
        cols = pl.ds(pl.multiple_of(k * width, 128), width) if aligned else pl.ds(k * width, width)
        mf[k] = g_v[:, cols].astype(F32) + e_v[:, cols]

    if not aligned:
        for k in range(pieces):
            merge(k)

    swaps = []
    for i in range(n_sh):
        o = at_sh(i, oc)
        if aligned:
            merge(2 * o + oc)
        swap = remote(mf.at[2 * o + oc], mx.at[o], m_s.at[i], m_r.at[o], (sib, s))
        swap.start()
        swaps.append(swap)
    if aligned:
        for i in range(n_sh):
            merge(2 * at_sh(i) + c)
    acc = None
    for i in range(n_sh):
        o = at_sh(i)
        arrived(mx.at[o], m_s.at[i], m_r.at[o])
        hi, lo = halves(mf[2 * o + c] + mx[o])
        m2[o, :n_rows] = hi
        m2[o, n_rows:] = lo
        if i > 0:
            arrived(q_all.at[2 * o + c], q_s.at[i], q_r.at[o])
        hi, lo = halves(q_all[2 * o + c])
        term = dot(jnp.concatenate([hi, lo], axis=0), m2[o], NT)
        acc = term if acc is None else acc + term
    acc = acc[:rank] + acc[rank:]
    part = acc[:, :n_rows] + acc[:, n_rows:]
    half = rank // 2

    pbuf[d] = jnp.concatenate([part[:half], part[half:]], axis=1)
    for i in range(1, n_dp):
        send(pbuf.at[d], pbuf.at[d], p_s.at[i], p_r.at[d], (at_dp(i), s))
    for i in range(1, n_dp):
        o = at_dp(i)
        arrived(pbuf.at[o], p_s.at[i], p_r.at[o])
    total = pbuf[0]
    for k in range(1, n_dp):
        total = total + pbuf[k]
    total = total * (1.0 / n_dp)
    pt = jnp.concatenate([total[:, :n_rows], total[:, n_rows:]], axis=0)

    twice = jnp.concatenate([pt, pt], axis=1) * (1.0 / n_dp)
    p_hi, p_lo = halves(twice)
    p2 = jnp.concatenate([p_hi, p_lo], axis=0)

    def w_term(o, span):
        t = dot(p2, m2[o, :, span])
        return t[:rank] + t[rank:]

    for ch, span in enumerate(spans):
        for i in range(1, n_sh):
            o = at_sh(i)
            w_c[o, :, span] = w_term(o, span)
            send(w_c.at[o, :, span], w_r.at[s, :, span], w_s.at[ch, i], w_rs.at[ch, s], (d, o))
            if ch == 0 and i == 1:
                padded = jnp.concatenate([pt, jnp.zeros((128 - rank, n_rows), F32)], axis=0)
                gbuf[s] = dot(pt, padded, NT, HIGH)
                for j in range(1, n_sh):
                    send(gbuf.at[s], gbuf.at[s], g_s.at[j], g_r.at[s], (d, at_sh(j)))
    for span in spans:
        w_r[s, :, span] = w_term(s, span)
    for swap in swaps:
        swap.wait_send()

    def over_shards(ch, span):
        for i in range(1, n_sh):
            o = at_sh(i)
            arrived(w_r.at[o, :, span], w_s.at[ch, i], w_rs.at[ch, o])
        r = w_r[0, :, span]
        for k in range(1, n_sh):
            r = r + w_r[k, :, span]
        if split_z:
            for k in range(nz):
                r_buf[k, :, span] = r[k * zrows : (k + 1) * zrows]
            z_r[z, :, span] = r_buf[z, :, span]
        else:
            z_r[z, :, span] = r
        for i in range(1, nz):
            o = at_z(i)
            src = r_buf.at[o, :, span] if split_z else z_r.at[z, :, span]
            send(src, z_r.at[z, :, span], zr_s.at[ch, i], zr_r.at[ch, z], (2 * o + c, s))

    def over_z(ch, span):
        for i in range(1, nz):
            o = at_z(i)
            arrived(z_r.at[o, :, span], zr_s.at[ch, i], zr_r.at[ch, o])
        r = z_r[0, :, span]
        for k in range(1, nz):
            r = r + z_r[k, :, span]
        if split_z:
            z_full[z, :, span] = r
            part = z_full.at[z, :, span]
            for i in range(1, nz):
                send(part, part, za_s.at[ch, i], za_r.at[ch, z], (2 * at_z(i) + c, s))
        else:
            z_full[0, :, span] = r

    over_shards(0, spans[0])

    for i in range(1, n_sh):
        o = at_sh(i)
        arrived(gbuf.at[o], g_s.at[i], g_r.at[o])
    gram = gbuf[0]
    for k in range(1, n_sh):
        gram = gram + gbuf[k]
    linv = inverse_factor(gram)
    l3 = jnp.concatenate([linv, linv, linv], axis=1)
    l_rounded = l3.astype(BF16).astype(F32)
    lane = lax.broadcasted_iota(jnp.int32, l3.shape, 1)
    l3 = jnp.where(lane < 2 * rank, l_rounded, l3 - l_rounded).astype(BF16)

    def share_out(ch, span):
        r = z_full[0, :, span]
        if split_z:
            for i in range(1, nz):
                o = at_z(i)
                arrived(z_full.at[o, :, span], za_s.at[ch, i], za_r.at[ch, o])
            r = jnp.concatenate([z_full[k, :, span] for k in range(nz)], axis=0)
        hi, lo = halves(r)
        y_all[mine, :, span] = dot(l3, jnp.concatenate([hi, lo, hi], axis=0))
        part = y_all.at[mine, :, span]
        for i in range(1, n_sh):
            send(part, part, y_s.at[ch, i], y_r.at[ch, s], (d, at_sh(i)), last_sends)
        if aligned:
            target = qnew_hbm.at[:, lanes(c * width, ch)]
            send(part, target, yc_s.at[ch, n_sh], yc_r.at[ch, n_sh], (sib, s), last_sends)
            copy = pltpu.make_async_copy(part, target, qn_sem.at[ch])
            copy.start()
            stores.append(copy)
        else:
            send(part, part, yc_s.at[ch, n_sh], yc_r.at[ch, n_sh], (sib, s), last_sends)

    for step in range(n_ch + 2):
        if 0 < step < n_ch:
            over_shards(step, spans[step])
        if 0 <= step - 1 < n_ch:
            over_z(step - 1, spans[step - 1])
        if 0 <= step - 2 < n_ch:
            share_out(step - 2, spans[step - 2])

    p_hat_t = dot(linv, pt, NN, HIGH)
    three = jnp.concatenate([p_hat_t, p_hat_t, p_hat_t], axis=0)
    rounded = three.astype(BF16).astype(F32)
    row = lax.broadcasted_iota(jnp.int32, three.shape, 0)
    ph3 = jnp.where(row < 2 * rank, rounded, three - rounded).T.astype(BF16)

    def finish(i, ch):
        o = at_sh(i)
        k = 2 * o + c
        span = spans[ch]
        hi, lo = halves(y_all[k, :, span])
        product = dot(ph3, jnp.concatenate([hi, lo, hi], axis=0))
        mx[o, :, span] = mx[o, :, span] - product
        theirs = out_hbm.at[0, :, lanes(k * width, ch)] if aligned else mf.at[k, :, span]
        send(mx.at[o, :, span], theirs, yc_s.at[ch, i], yc_r.at[ch, o], (sib, s), last_sends)
        mf[k, :, span] = mf[k, :, span] - product
        if aligned:
            copy = pltpu.make_async_copy(mf.at[k, :, span], theirs, out_sem.at[ch, i])
            copy.start()
            stores.append(copy)

    for ch in range(n_ch):
        finish(0, ch)
    for copy in sends:
        copy.wait_send()
    for ch, span in enumerate(spans):
        for i in range(1, n_sh):
            o = at_sh(i)
            arrived(y_all.at[2 * o + c, :, span], y_s.at[ch, i], y_r.at[ch, o])
            finish(i, ch)
    for ch, span in enumerate(spans):
        q_part = qnew_hbm.at[:, lanes(oc * width, ch)] if aligned else y_all.at[other, :, span]
        arrived(q_part, yc_s.at[ch, n_sh], yc_r.at[ch, n_sh])
        for i in range(n_sh):
            o = at_sh(i, oc)
            k = 2 * o + oc
            part = out_hbm.at[0, :, lanes(k * width, ch)] if aligned else mf.at[k, :, span]
            arrived(part, yc_s.at[ch, i], yc_r.at[ch, o])
    late = []
    if not aligned:
        for h in range(2):
            qn_v[:, h * width : (h + 1) * width] = y_all[2 * s + h]
    if not aligned:
        for k in range(pieces):
            out_v[:, k * width : (k + 1) * width] = mf[k]
        for src, dst, sem in ((out_v, out_hbm.at[0], out_sem.at[0, 0]), (qn_v, qnew_hbm, qn_sem.at[0])):
            copy = pltpu.make_async_copy(src, dst, sem)
            copy.start()
            late.append(copy)
    for copy in last_sends:
        copy.wait_send()
    for copy in stores + late:
        copy.wait()


def place(out_from, q_from, out_to, q_to, out_v, q_v, in_sems, out_sems):
    n_rows = out_from.shape[1]
    step = n_rows // PLACE_PARTS
    pairs = [(q_from, q_v, q_to)]
    for i in range(PLACE_PARTS):
        rows = pl.ds(i * step, step)
        pairs.append((out_from.at[0, rows], out_v.at[rows], out_to.at[0, rows]))
    loads = [pltpu.make_async_copy(src, mid, in_sems.at[i]) for i, (src, mid, _) in enumerate(pairs)]
    stores = [pltpu.make_async_copy(mid, dst, out_sems.at[i]) for i, (_, mid, dst) in enumerate(pairs)]
    for load in loads:
        load.start()
    for load, store in zip(loads, stores):
        load.wait()
        store.start()
    for store in stores:
        store.wait()


def per_device(n_dp, n_sh, grads, errors, q_prev):
    _, n_rows, full = grads.shape
    share, rank = q_prev.shape
    width = share // 2
    nz = n_dp // 2
    split_z = rank % (8 * nz) == 0
    zrows = rank // nz if split_z else rank
    aligned = width % 128 == 0
    pieces = 2 * n_sh
    dims = (n_dp, n_sh, math.isqrt(n_sh), nz, zrows, split_z, aligned, width)
    chunks = ((0, width),)
    if aligned and width >= N_CHUNKS * 128:
        tiles = width // 128
        edges = [-(-tiles * i // N_CHUNKS) * 128 for i in range(N_CHUNKS + 1)]
        chunks = tuple(zip(edges[:-1], edges[1:]))
    vm = pltpu.VMEM
    dma = pltpu.SemaphoreType.DMA
    small = (8, 128)
    scratch = [
        vm((n_rows, full), BF16),
        vm((n_rows, full), F32),
        vm(small if aligned else (rank, share), F32),
        vm((n_sh, 2 * n_rows, width), BF16),
        vm((pieces, n_rows, width), F32),
        vm((n_sh, n_rows, width), F32),
        vm((pieces, rank, width), F32),
        vm((n_dp, rank // 2, 2 * n_rows), F32),
        vm((n_sh, rank, 128), F32),
        vm((n_sh, rank, width), F32),
        vm((n_sh, rank, width), F32),
        vm((nz, zrows, width) if split_z else small, F32),
        vm((nz, zrows, width), F32),
        vm((nz, zrows, width) if split_z else (1, rank, width), F32),
        vm((pieces, rank, width), F32),
        vm(small if aligned else (n_rows, full), F32),
        vm(small if aligned else (rank, share), F32),
        dma((4,)),
    ]
    n_ch = len(chunks)
    per_chunk = [(n_sh,), (n_dp,), (n_sh,), (n_sh,), (n_ch, n_sh)] + [(n_ch, nz)] * 2 + [(n_ch, n_sh)] * 2
    per_chunk[-1] = (n_ch, n_sh + 1)
    for shape in per_chunk:
        scratch += [dma(shape), dma(shape)]
    scratch += [dma((n_ch, n_sh)), dma((max(n_ch, 2),))]
    shapes = (
        jax.ShapeDtypeStruct((1, n_rows, full), F32),
        jax.ShapeDtypeStruct((rank, share), F32),
    )
    hbm = pl.BlockSpec(memory_space=pl.ANY)
    out, q_new = pl.pallas_call(
        functools.partial(kernel, dims, chunks),
        out_shape=shapes,
        in_specs=[hbm, hbm, hbm],
        out_specs=(hbm, hbm),
        scratch_shapes=scratch,
        compiler_params=pltpu.CompilerParams(
            collective_id=0, has_side_effects=True, vmem_limit_bytes=62 * 1024 * 1024
        ),
        cost_estimate=pl.CostEstimate(
            flops=18 * n_rows * full * rank, bytes_accessed=10 * n_rows * full, transcendentals=0
        ),
    )(grads, errors, q_prev.T)
    out, q_new = pl.pallas_call(
        place,
        out_shape=shapes,
        in_specs=[hbm, hbm],
        out_specs=(hbm, hbm),
        scratch_shapes=[
            vm((n_rows, full), F32), vm((rank, share), F32), dma((PLACE_PARTS + 1,)), dma((PLACE_PARTS + 1,)),
        ],
        compiler_params=pltpu.CompilerParams(vmem_limit_bytes=62 * 1024 * 1024),
    )(out, q_new)
    return out, q_new.T


def solution(mesh):
    in_specs = (P("dp", "shard", None), P("dp", "shard", None), P("shard", None))
    out_specs = (P("dp", "shard", None), P("shard", None))
    return jax.shard_map(
        functools.partial(per_device, mesh.shape["dp"], mesh.shape["shard"]),
        mesh=mesh, in_specs=in_specs, out_specs=out_specs, check_vma=False,
    )
```

```python
import functools
import math

import jax
import jax.numpy as jnp
from jax import lax
from jax.experimental import pallas as pl
from jax.experimental.pallas import tpu as pltpu
from jax.sharding import PartitionSpec as P

MESH = pl.DeviceIdType.MESH
HIGH = lax.Precision.HIGHEST
F32 = jnp.float32
BF16 = jnp.bfloat16
NT = (((1,), (1,)), ((), ()))
NN = (((1,), (0,)), ((), ()))
N_CHUNKS = 1
PLACE_PARTS = 8


def dot(a, b, dims=NN, precision=None):
    return lax.dot_general(a, b, dims, precision=precision, preferred_element_type=F32)


def halves(x):
    hi = x.astype(BF16)
    return hi, (x - hi.astype(F32)).astype(BF16)


def inverse_factor(gram):
    n = gram.shape[0]
    rows = lax.broadcasted_iota(jnp.int32, (n, 128), 0)
    lanes = lax.broadcasted_iota(jnp.int32, (n, 128), 1)
    work = jnp.where(lanes == rows + n, 1.0, gram)
    block = 8
    for first in range(0, n, block):
        columns = [jnp.broadcast_to(work[:, first + t : first + t + 1], (n, 128)) for t in range(block)]
        for t in range(block):
            j = first + t
            scale = jnp.where(rows > j, columns[t] * (1.0 / columns[t][j : j + 1]), 0.0)
            for u in range(t + 1, block):
                columns[u] = columns[u] - scale * columns[u][j : j + 1]
            work = work - scale * work[j : j + 1]
    diag = jnp.sum(jnp.where(lanes == rows, work, 0.0), axis=1, keepdims=True)
    work = work * lax.rsqrt(diag)
    return work[:, n : 2 * n]


def kernel(
    dims, chunks, g_hbm, e_hbm, q_hbm, out_hbm, qnew_hbm,
    g_v, e_v, q_v, m2, mf, mx, q_all, pbuf, gbuf, w_c, w_r, r_buf, z_r, z_full, y_all, out_v, qn_v,
    in_sem, q_s, q_r, p_s, p_r, g_s, g_r, m_s, m_r, w_s, w_rs, zr_s, zr_r, za_s, za_r,
    y_s, y_r, yc_s, yc_r, out_sem, qn_sem,
):
    n_dp, n_sh, side, nz, zrows, split_z, aligned, width = dims
    spans = [pl.ds(lo, hi - lo) for lo, hi in chunks]
    n_ch = len(chunks)
    rank = q_hbm.shape[0]
    pieces = 2 * n_sh
    d = lax.axis_index("dp")
    s = lax.axis_index("shard")
    z = lax.div(d, 2)
    c = lax.rem(d, 2)
    oc = 1 - c
    sib = d + 1 - 2 * c

    def ring(at, count):
        places = [at]
        for _ in range(count - 1):
            step = places[-1] + 1
            places.append(jnp.where(step == count, 0, step))
        return places

    dp_at = ring(d, n_dp)
    z_at = ring(z, nz)
    rows_at = ring(lax.div(s, side), side)
    cols_at = ring(lax.rem(s, side), side)
    in_rows = [rows_at[i // side] * side + cols_at[i % side] for i in range(n_sh)]
    in_cols = [rows_at[i % side] * side + cols_at[i // side] for i in range(n_sh)]
    mine_at = [jnp.where(c == 0, a, b) for a, b in zip(in_rows, in_cols)]
    theirs_at = [jnp.where(c == 0, b, a) for a, b in zip(in_rows, in_cols)]

    def at_dp(i):
        return dp_at[i]

    def at_sh(i, core=None):
        return mine_at[i] if core is None else theirs_at[i]

    def at_z(i):
        return z_at[i]

    barrier = pltpu.get_barrier_semaphore()
    for i in range(1, n_dp):
        pl.semaphore_signal(barrier, inc=1, device_id=(at_dp(i), s), device_id_type=MESH)
    for i in range(1, n_sh):
        pl.semaphore_signal(barrier, inc=1, device_id=(d, at_sh(i)), device_id_type=MESH)

    load_g = pltpu.make_async_copy(g_hbm.at[0], g_v, in_sem.at[0])
    load_e = pltpu.make_async_copy(e_hbm.at[0], e_v, in_sem.at[1])
    q_loads = []
    if aligned:
        for h in range(2):
            half_copy = pltpu.make_async_copy(
                q_hbm.at[:, h * width : (h + 1) * width], q_all.at[2 * s + h], in_sem.at[2 + h]
            )
            half_copy.start()
            q_loads.append(half_copy)
    else:
        whole_copy = pltpu.make_async_copy(q_hbm, q_v, in_sem.at[2])
        whole_copy.start()
        q_loads.append(whole_copy)
    load_g.start()
    load_e.start()

    for q_load in q_loads:
        q_load.wait()
    if not aligned:
        for h in range(2):
            q_all[2 * s + h] = q_v[:, h * width : (h + 1) * width]
    pl.semaphore_wait(barrier, n_dp - 1 + n_sh - 1)

    def remote(src, dst, send, recv, target):
        return pltpu.make_async_remote_copy(
            src_ref=src, dst_ref=dst, send_sem=send, recv_sem=recv, device_id=target, device_id_type=MESH
        )

    sends = []
    last_sends = []
    stores = []

    def lanes(start, ch):
        first, last = chunks[ch]
        return pl.ds(pl.multiple_of(start + first, 128), last - first)

    def send(src, dst, send_sem, recv_sem, target, kept=sends):
        copy = remote(src, dst, send_sem, recv_sem, target)
        copy.start()
        kept.append(copy)

    def arrived(dst, send_sem, recv_sem):
        remote(dst, dst, send_sem, recv_sem, (sib, s)).wait_recv()

    mine = 2 * s + c
    other = 2 * s + oc
    for i in range(1, n_sh):
        send(q_all.at[mine], q_all.at[mine], q_s.at[i], q_r.at[s], (d, at_sh(i)))

    load_g.wait()
    load_e.wait()
    n_rows = mf.shape[1]

    def merge(k):
        cols = pl.ds(pl.multiple_of(k * width, 128), width) if aligned else pl.ds(k * width, width)
        mf[k] = g_v[:, cols].astype(F32) + e_v[:, cols]

    if not aligned:
        for k in range(pieces):
            merge(k)

    swaps = []
    for i in range(n_sh):
        o = at_sh(i, oc)
        if aligned:
            merge(2 * o + oc)
        swap = remote(mf.at[2 * o + oc], mx.at[o], m_s.at[i], m_r.at[o], (sib, s))
        swap.start()
        swaps.append(swap)
    if aligned:
        for i in range(n_sh):
            merge(2 * at_sh(i) + c)
    acc = None
    for i in range(n_sh):
        o = at_sh(i)
        arrived(mx.at[o], m_s.at[i], m_r.at[o])
        hi, lo = halves(mf[2 * o + c] + mx[o])
        m2[o, :n_rows] = hi
        m2[o, n_rows:] = lo
        if i > 0:
            arrived(q_all.at[2 * o + c], q_s.at[i], q_r.at[o])
        hi, lo = halves(q_all[2 * o + c])
        term = dot(jnp.concatenate([hi, lo], axis=0), m2[o], NT)
        acc = term if acc is None else acc + term
    acc = acc[:rank] + acc[rank:]
    part = acc[:, :n_rows] + acc[:, n_rows:]
    half = rank // 2

    pbuf[d] = jnp.concatenate([part[:half], part[half:]], axis=1)
    for i in range(1, n_dp):
        send(pbuf.at[d], pbuf.at[d], p_s.at[i], p_r.at[d], (at_dp(i), s))
    for i in range(1, n_dp):
        o = at_dp(i)
        arrived(pbuf.at[o], p_s.at[i], p_r.at[o])
    total = pbuf[0]
    for k in range(1, n_dp):
        total = total + pbuf[k]
    total = total * (1.0 / n_dp)
    pt = jnp.concatenate([total[:, :n_rows], total[:, n_rows:]], axis=0)

    twice = jnp.concatenate([pt, pt], axis=1) * (1.0 / n_dp)
    p_hi, p_lo = halves(twice)
    p2 = jnp.concatenate([p_hi, p_lo], axis=0)

    def w_term(o, span):
        t = dot(p2, m2[o, :, span])
        return t[:rank] + t[rank:]

    for ch, span in enumerate(spans):
        for i in range(1, n_sh):
            o = at_sh(i)
            w_c[o, :, span] = w_term(o, span)
            send(w_c.at[o, :, span], w_r.at[s, :, span], w_s.at[ch, i], w_rs.at[ch, s], (d, o))
            if ch == 0 and i == 1:
                padded = jnp.concatenate([pt, jnp.zeros((128 - rank, n_rows), F32)], axis=0)
                gbuf[s] = dot(pt, padded, NT, HIGH)
                for j in range(1, n_sh):
                    send(gbuf.at[s], gbuf.at[s], g_s.at[j], g_r.at[s], (d, at_sh(j)))
    for span in spans:
        w_r[s, :, span] = w_term(s, span)
    for swap in swaps:
        swap.wait_send()

    def over_shards(ch, span):
        for i in range(1, n_sh):
            o = at_sh(i)
            arrived(w_r.at[o, :, span], w_s.at[ch, i], w_rs.at[ch, o])
        r = w_r[0, :, span]
        for k in range(1, n_sh):
            r = r + w_r[k, :, span]
        if split_z:
            for k in range(nz):
                r_buf[k, :, span] = r[k * zrows : (k + 1) * zrows]
            z_r[z, :, span] = r_buf[z, :, span]
        else:
            z_r[z, :, span] = r
        for i in range(1, nz):
            o = at_z(i)
            src = r_buf.at[o, :, span] if split_z else z_r.at[z, :, span]
            send(src, z_r.at[z, :, span], zr_s.at[ch, i], zr_r.at[ch, z], (2 * o + c, s))

    def over_z(ch, span):
        for i in range(1, nz):
            o = at_z(i)
            arrived(z_r.at[o, :, span], zr_s.at[ch, i], zr_r.at[ch, o])
        r = z_r[0, :, span]
        for k in range(1, nz):
            r = r + z_r[k, :, span]
        if split_z:
            z_full[z, :, span] = r
            part = z_full.at[z, :, span]
            for i in range(1, nz):
                send(part, part, za_s.at[ch, i], za_r.at[ch, z], (2 * at_z(i) + c, s))
        else:
            z_full[0, :, span] = r

    over_shards(0, spans[0])

    for i in range(1, n_sh):
        o = at_sh(i)
        arrived(gbuf.at[o], g_s.at[i], g_r.at[o])
    gram = gbuf[0]
    for k in range(1, n_sh):
        gram = gram + gbuf[k]
    linv = inverse_factor(gram)
    l3 = jnp.concatenate([linv, linv, linv], axis=1)
    l_rounded = l3.astype(BF16).astype(F32)
    lane = lax.broadcasted_iota(jnp.int32, l3.shape, 1)
    l3 = jnp.where(lane < 2 * rank, l_rounded, l3 - l_rounded).astype(BF16)

    def share_out(ch, span):
        r = z_full[0, :, span]
        if split_z:
            for i in range(1, nz):
                o = at_z(i)
                arrived(z_full.at[o, :, span], za_s.at[ch, i], za_r.at[ch, o])
            r = jnp.concatenate([z_full[k, :, span] for k in range(nz)], axis=0)
        hi, lo = halves(r)
        y_all[mine, :, span] = dot(l3, jnp.concatenate([hi, lo, hi], axis=0))
        part = y_all.at[mine, :, span]
        for i in range(1, n_sh):
            send(part, part, y_s.at[ch, i], y_r.at[ch, s], (d, at_sh(i)), last_sends)
        if aligned:
            target = qnew_hbm.at[:, lanes(c * width, ch)]
            send(part, target, yc_s.at[ch, n_sh], yc_r.at[ch, n_sh], (sib, s), last_sends)
            copy = pltpu.make_async_copy(part, target, qn_sem.at[ch])
            copy.start()
            stores.append(copy)
        else:
            send(part, part, yc_s.at[ch, n_sh], yc_r.at[ch, n_sh], (sib, s), last_sends)

    for step in range(n_ch + 2):
        if 0 < step < n_ch:
            over_shards(step, spans[step])
        if 0 <= step - 1 < n_ch:
            over_z(step - 1, spans[step - 1])
        if 0 <= step - 2 < n_ch:
            share_out(step - 2, spans[step - 2])

    p_hat_t = dot(linv, pt, NN, HIGH)
    three = jnp.concatenate([p_hat_t, p_hat_t, p_hat_t], axis=0)
    rounded = three.astype(BF16).astype(F32)
    row = lax.broadcasted_iota(jnp.int32, three.shape, 0)
    ph3 = jnp.where(row < 2 * rank, rounded, three - rounded).T.astype(BF16)

    def finish(i, ch):
        o = at_sh(i)
        k = 2 * o + c
        span = spans[ch]
        hi, lo = halves(y_all[k, :, span])
        product = dot(ph3, jnp.concatenate([hi, lo, hi], axis=0))
        mx[o, :, span] = mx[o, :, span] - product
        theirs = out_hbm.at[0, :, lanes(k * width, ch)] if aligned else mf.at[k, :, span]
        send(mx.at[o, :, span], theirs, yc_s.at[ch, i], yc_r.at[ch, o], (sib, s), last_sends)
        mf[k, :, span] = mf[k, :, span] - product
        if aligned:
            copy = pltpu.make_async_copy(mf.at[k, :, span], theirs, out_sem.at[ch, i])
            copy.start()
            stores.append(copy)

    for ch in range(n_ch):
        finish(0, ch)
    for copy in sends:
        copy.wait_send()
    for ch, span in enumerate(spans):
        for i in range(1, n_sh):
            o = at_sh(i)
            arrived(y_all.at[2 * o + c, :, span], y_s.at[ch, i], y_r.at[ch, o])
            finish(i, ch)
    for ch, span in enumerate(spans):
        q_part = qnew_hbm.at[:, lanes(oc * width, ch)] if aligned else y_all.at[other, :, span]
        arrived(q_part, yc_s.at[ch, n_sh], yc_r.at[ch, n_sh])
        for i in range(n_sh):
            o = at_sh(i, oc)
            k = 2 * o + oc
            part = out_hbm.at[0, :, lanes(k * width, ch)] if aligned else mf.at[k, :, span]
            arrived(part, yc_s.at[ch, i], yc_r.at[ch, o])
    late = []
    if not aligned:
        for h in range(2):
            qn_v[:, h * width : (h + 1) * width] = y_all[2 * s + h]
    if not aligned:
        for k in range(pieces):
            out_v[:, k * width : (k + 1) * width] = mf[k]
        for src, dst, sem in ((out_v, out_hbm.at[0], out_sem.at[0, 0]), (qn_v, qnew_hbm, qn_sem.at[0])):
            copy = pltpu.make_async_copy(src, dst, sem)
            copy.start()
            late.append(copy)
    for copy in last_sends:
        copy.wait_send()
    for copy in stores + late:
        copy.wait()


def place(out_from, q_from, out_to, q_to, out_v, q_v, in_sems, out_sems):
    n_rows = out_from.shape[1]
    step = n_rows // PLACE_PARTS
    pairs = [(q_from, q_v, q_to)]
    for i in range(PLACE_PARTS):
        rows = pl.ds(i * step, step)
        pairs.append((out_from.at[0, rows], out_v.at[rows], out_to.at[0, rows]))
    loads = [pltpu.make_async_copy(src, mid, in_sems.at[i]) for i, (src, mid, _) in enumerate(pairs)]
    stores = [pltpu.make_async_copy(mid, dst, out_sems.at[i]) for i, (_, mid, dst) in enumerate(pairs)]
    for load in loads:
        load.start()
    for load, store in zip(loads, stores):
        load.wait()
        store.start()
    for store in stores:
        store.wait()


def per_device(n_dp, n_sh, grads, errors, q_prev):
    _, n_rows, full = grads.shape
    share, rank = q_prev.shape
    width = share // 2
    nz = n_dp // 2
    split_z = rank % (8 * nz) == 0
    zrows = rank // nz if split_z else rank
    aligned = width % 128 == 0
    pieces = 2 * n_sh
    dims = (n_dp, n_sh, math.isqrt(n_sh), nz, zrows, split_z, aligned, width)
    chunks = ((0, width),)
    if aligned and width >= N_CHUNKS * 128:
        tiles = width // 128
        edges = [-(-tiles * i // N_CHUNKS) * 128 for i in range(N_CHUNKS + 1)]
        chunks = tuple(zip(edges[:-1], edges[1:]))
    vm = pltpu.VMEM
    dma = pltpu.SemaphoreType.DMA
    small = (8, 128)
    scratch = [
        vm((n_rows, full), BF16),
        vm((n_rows, full), F32),
        vm(small if aligned else (rank, share), F32),
        vm((n_sh, 2 * n_rows, width), BF16),
        vm((pieces, n_rows, width), F32),
        vm((n_sh, n_rows, width), F32),
        vm((pieces, rank, width), F32),
        vm((n_dp, rank // 2, 2 * n_rows), F32),
        vm((n_sh, rank, 128), F32),
        vm((n_sh, rank, width), F32),
        vm((n_sh, rank, width), F32),
        vm((nz, zrows, width) if split_z else small, F32),
        vm((nz, zrows, width), F32),
        vm((nz, zrows, width) if split_z else (1, rank, width), F32),
        vm((pieces, rank, width), F32),
        vm(small if aligned else (n_rows, full), F32),
        vm(small if aligned else (rank, share), F32),
        dma((4,)),
    ]
    n_ch = len(chunks)
    per_chunk = [(n_sh,), (n_dp,), (n_sh,), (n_sh,), (n_ch, n_sh)] + [(n_ch, nz)] * 2 + [(n_ch, n_sh)] * 2
    per_chunk[-1] = (n_ch, n_sh + 1)
    for shape in per_chunk:
        scratch += [dma(shape), dma(shape)]
    scratch += [dma((n_ch, n_sh)), dma((max(n_ch, 2),))]
    shapes = (
        jax.ShapeDtypeStruct((1, n_rows, full), F32),
        jax.ShapeDtypeStruct((rank, share), F32),
    )
    hbm = pl.BlockSpec(memory_space=pl.ANY)
    out, q_new = pl.pallas_call(
        functools.partial(kernel, dims, chunks),
        out_shape=shapes,
        in_specs=[hbm, hbm, hbm],
        out_specs=(hbm, hbm),
        scratch_shapes=scratch,
        compiler_params=pltpu.CompilerParams(
            collective_id=0, has_side_effects=True, vmem_limit_bytes=62 * 1024 * 1024
        ),
        cost_estimate=pl.CostEstimate(
            flops=18 * n_rows * full * rank, bytes_accessed=10 * n_rows * full, transcendentals=0
        ),
    )(grads, errors, q_prev.T)
    out, q_new = pl.pallas_call(
        place,
        out_shape=shapes,
        in_specs=[hbm, hbm],
        out_specs=(hbm, hbm),
        scratch_shapes=[
            vm((n_rows, full), F32), vm((rank, share), F32), dma((PLACE_PARTS + 1,)), dma((PLACE_PARTS + 1,)),
        ],
        compiler_params=pltpu.CompilerParams(vmem_limit_bytes=62 * 1024 * 1024),
    )(out, q_new)
    return out, q_new.T


def solution(mesh):
    in_specs = (P("dp", "shard", None), P("dp", "shard", None), P("shard", None))
    out_specs = (P("dp", "shard", None), P("shard", None))
    return jax.shard_map(
        functools.partial(per_device, mesh.shape["dp"], mesh.shape["shard"]),
        mesh=mesh, in_specs=in_specs, out_specs=out_specs, check_vma=False,
    )
```
